32 devices in a mesh: row: 4 (over y, x), col: 8 (over z, core).
Axes of the slice: x: 2, y: 2, z: 4, core: 2. Of those that a mesh axis runs over, the one named last changes fastest.
Arguments:
- node_features: bfloat16 [3072, 1024], P('row'), may hold values from -28 to 28
- edge_weight: bfloat16 [3072, 3072], P('row', 'col'), may hold values from -0.109375 to 0.109375
- pattern: int32 [24, 24], P('row', 'col'), may hold values from 0 to 1, as said below
- w_qkv: bfloat16 [1024, 3072], replicated, may hold values from -0.1875 to 0.1875
- w_out: bfloat16 [1024, 1024], P(None, 'col'), may hold values from -0.1875 to 0.1875
- bias_gain: float32 [16], replicated, may hold values from -2 to 2
- bias_rate: float32 [16], replicated, may hold values from 2 to 12
Outputs:
- mixed: bfloat16 [3072, 1024], P('row', 'col')
The draws below stay inside these ranges and needn't reach their ends.
Inputs may be any that keep to these rules, and one draw needn't show every extreme that they name: pattern[i][i] is 1 for every i; the share of ones differs from block-row to block-row.
All inputs are finite; a program needn't handle non-finite values.
Results may differ from the reference program's by a relative error of at most 0.02.
Values may be sent and summed in bfloat16 or wider, within the bound.
No kernel may reach another device: no remote copies, remote signals or barrier semaphores. Data moves between devices by JAX's collectives and lax.ppermute only.
A program may use at most 128 MiB of HBM per device.

```python
import math
import jax
import jax.numpy as jnp
from jax import lax

D = 1024
HEADS = 16
BLK = 128
SWEEPS = 3
HDIM = 64
NODES = 3072
NBLK = 24


def draw_pattern(key, part):
    first, second = jax.random.split(jax.random.fold_in(key, 11))
    density = jax.random.randint(first, (NBLK, 1), 2, 10)
    coins = jax.random.randint(second, (NBLK, NBLK), 0, 10)
    diagonal = jnp.arange(NBLK)[:, None] == jnp.arange(NBLK)[None, :]
    return jnp.where(diagonal | (coins < density), 1, 0).astype(jnp.int32)


def draw_node_features(key, part):
    first = jax.random.fold_in(jax.random.fold_in(key, 23), 0)
    values = jax.random.truncated_normal(first, -4.0, 4.0, (NODES, D), jnp.float32)
    return values.astype(jnp.bfloat16)


def level_of(stream_key, dims, cuts, least, top_value):
    level = 1.0
    for axis_at, parts in cuts:
        draws = jax.random.uniform(jax.random.fold_in(jax.random.fold_in(stream_key, 6), axis_at), (parts,), jnp.float32, least / len(cuts), top_value / len(cuts))
        level = level * jnp.repeat(jnp.exp(draws), dims[axis_at] // parts).reshape((-1,) + (1,) * (len(dims) - 1 - axis_at))
    return level


def normal_values(key, shape, spread, reach, shards=(), kind=jnp.bfloat16):
    level = level_of(key, shape, shards, -0.22, 0.18) if shards else 1.0
    array = jax.random.normal(key, shape, jnp.float32) * spread * level
    return jnp.minimum(jnp.maximum(array, -reach), reach).astype(kind)


def setup_inputs(seed: int = 0) -> dict:
    streams_of = jax.random.split(jax.random.key(seed), 8)
    return {
        "node_features": draw_node_features(jax.random.fold_in(streams_of[7], 71), 0),
        "edge_weight": normal_values(streams_of[1], (NODES, NODES), NODES ** -0.5, 0.109375, ((0, 4), (1, 8))),
        "pattern": draw_pattern(jax.random.fold_in(streams_of[7], 71), 0),
        "w_qkv": normal_values(streams_of[3], (D, 3 * D), D ** -0.5, 0.1875),
        "w_out": normal_values(streams_of[4], (D, D), D ** -0.5, 0.1875, ((1, 8),)),
        "bias_gain": jnp.clip(jax.random.uniform(streams_of[5], (HEADS,), jnp.float32, -2.0, 2.0), -2.0, 2.0),
        "bias_rate": jnp.clip(jnp.exp(jax.random.uniform(streams_of[6], (HEADS,), jnp.float32, math.log(2.0), math.log(12.0))), 2.0, 12.0),
    }


def expand_blocks(pattern):
    block_rows, block_cols = pattern.shape
    grid = jnp.broadcast_to(pattern[:, None, :, None] > 0, (block_rows, BLK, block_cols, BLK))
    return grid.reshape(block_rows * BLK, block_cols * BLK)

def reference(node_features, edge_weight, pattern, w_qkv, w_out, bias_gain, bias_rate):
    keep_mask = expand_blocks(pattern)
    adjacency = jnp.where(keep_mask, edge_weight, jnp.zeros_like(edge_weight))
    indices = lax.iota(jnp.int32, NODES)
    identity = (indices[:, None] == indices[None, :]).astype(jnp.float32)
    zero = jnp.zeros((), jnp.float32)
    ranks = jnp.where(keep_mask, 0.15 * identity + 0.1275 * adjacency.astype(jnp.float32), zero)
    for sweep_index in range(SWEEPS - 1):
        product = jnp.dot(adjacency, ranks.astype(jnp.bfloat16), preferred_element_type=jnp.float32)
        ranks = jnp.where(keep_mask, 0.15 * identity + 0.85 * product, zero)
    projected = jnp.dot(node_features, w_qkv, preferred_element_type=jnp.float32).astype(jnp.bfloat16)
    heads_query = projected[:, :D].reshape(NODES, HEADS, HDIM).transpose(1, 0, 2)
    heads_key = projected[:, D:2 * D].reshape(NODES, HEADS, HDIM).transpose(1, 0, 2)
    heads_value = projected[:, 2 * D:].reshape(NODES, HEADS, HDIM).transpose(1, 0, 2)
    root_nodes = math.sqrt(NODES)
    score_scale = 1.0 / math.sqrt(HDIM)

    def one_head(items):
        query, keys, values, gain, rate = items
        scores = jnp.dot(query, keys.T, preferred_element_type=jnp.float32) * score_scale
        scores = scores + gain * jnp.tanh(rate * root_nodes * ranks)
        masked = jnp.where(keep_mask, scores, -1e+30)
        peak = lax.optimization_barrier(jnp.max(masked, axis=1, keepdims=True))
        expo = jnp.where(keep_mask, jnp.exp(masked - peak), zero)
        totals = lax.optimization_barrier(jnp.sum(expo, axis=1, keepdims=True))
        numer = jnp.dot(expo.astype(jnp.bfloat16), values, preferred_element_type=jnp.float32)
        return (numer / totals).astype(jnp.bfloat16)
    attended = lax.map(one_head, (heads_query, heads_key, heads_value, bias_gain, bias_rate))
    attended = attended.transpose(1, 0, 2).reshape(NODES, D)
    return jnp.dot(attended, w_out, preferred_element_type=jnp.float32).astype(jnp.bfloat16)
```

```python
import functools
import math

import jax
import jax.numpy as jnp
from jax import lax
from jax.experimental import pallas as pl
from jax.experimental.pallas import tpu as pltpu
from jax.sharding import PartitionSpec as P

D = 1024
HEADS = 16
BLK = 128
HDIM = 64
PAIRS = HEADS // 2
LANES = 128
VMEM_LIMIT = 56 * 2**20

VMEM = pl.BlockSpec(memory_space=pltpu.VMEM)
SMEM = pl.BlockSpec(memory_space=pltpu.SMEM)
BF16 = jnp.bfloat16
F32 = jnp.float32


def params():
    return pltpu.CompilerParams(vmem_limit_bytes=VMEM_LIMIT)


def cost(flops, nbytes, trans=0):
    return pl.CostEstimate(flops=int(flops), bytes_accessed=int(nbytes), transcendentals=int(trans))


def xor_pairs(n, j):
    return [(i, i ^ j) for i in range(n)]


def keep_rows(pattern_ref, block_row, block_cols):
    parts = [
        jnp.full((1, BLK), jnp.where(pattern_ref[block_row, b] > 0, 1.0, 0.0), F32)
        for b in range(block_cols)
    ]
    return jnp.concatenate(parts, axis=1)


def sweep_kernel(first, ratio, place_ref, pattern_ref, own_ref, panel_ref, *rest):
    blocks, out_ref = rest[:-1], rest[-1]
    rows, cols = own_ref.shape
    row_pos, col_pos = place_ref[0], place_ref[1]
    block_cols = cols // BLK
    tile = 256

    def step(t, carry):
        start = pl.multiple_of(t * tile, tile)
        acc = jnp.zeros((tile, cols), F32)
        for j, block in enumerate(blocks):
            source = lax.bitwise_xor(row_pos, j) * ratio
            left = jnp.concatenate(
                [panel_ref[source + i, pl.ds(start, tile), :] for i in range(ratio)], axis=1
            )
            acc += jnp.dot(left, block[...], preferred_element_type=F32)
        own = own_ref[pl.ds(start, tile), :].astype(F32)
        total = 0.1275 * own + (0.85 * 0.1275 if first else 0.85) * acc
        keep = jnp.concatenate(
            [
                jnp.broadcast_to(
                    keep_rows(pattern_ref, t * (tile // BLK) + b, block_cols), (BLK, cols)
                )
                for b in range(tile // BLK)
            ],
            axis=0,
        )
        if not first:
            row_ids = row_pos * rows + start + lax.broadcasted_iota(jnp.int32, (tile, cols), 0)
            col_ids = col_pos * cols + lax.broadcasted_iota(jnp.int32, (tile, cols), 1)
            total = jnp.where(row_ids == col_ids, total + 0.15, total)
        out_ref[pl.ds(start, tile), :] = jnp.where(keep > 0, total, 0.0).astype(out_ref.dtype)
        return carry

    lax.fori_loop(0, rows // tile, step, 0)


def sweep(first, place, pattern, own, panel, blocks, dtype):
    rows, cols = own.shape
    flops = 2 * rows * panel.shape[0] * cols * cols
    return pl.pallas_call(
        functools.partial(sweep_kernel, first, rows // cols),
        out_shape=jax.ShapeDtypeStruct((rows, cols), dtype),
        in_specs=[SMEM, SMEM] + [VMEM] * (2 + len(blocks)),
        out_specs=VMEM,
        compiler_params=params(),
        cost_estimate=cost(flops, 2 * panel.size + 4 * rows * cols * len(blocks)),
        name="rank_sweep",
    )(place, pattern, own, panel, *blocks)


def split_heads(keys):
    lane = lax.broadcasted_iota(jnp.int32, keys.shape, 1)
    zero = jnp.zeros_like(keys)
    return jnp.concatenate(
        [jnp.where(lane < HDIM, keys, zero), jnp.where(lane >= HDIM, keys, zero)], axis=0
    )


def peak_kernel(pattern_ref, q_ref, k_ref, out_ref):
    rows, cols = q_ref.shape[0], k_ref.shape[0]
    block_rows, block_cols = rows // BLK, cols // BLK
    masks = []
    for b in range(block_cols):
        masks.append(
            jnp.concatenate(
                [
                    jnp.full((1, BLK), jnp.where(pattern_ref[i, b] > 0, 0.0, -1e30), F32)
                    for i in range(block_rows)
                ],
                axis=1,
            )
        )
    for p in range(PAIRS):
        lanes = slice(p * LANES, (p + 1) * LANES)
        both = split_heads(k_ref[:, lanes])
        for side in range(2):
            peak = jnp.full((1, rows), -1e30, F32)
            for b in range(block_cols):
                start = side * cols + b * BLK
                s = lax.dot_general(
                    both[start : start + BLK, :],
                    q_ref[:, lanes],
                    (((1,), (1,)), ((), ())),
                    preferred_element_type=F32,
                )
                peak = jnp.maximum(peak, jnp.max(s, axis=0, keepdims=True) + masks[b])
            out_ref[2 * p + side : 2 * p + side + 1, :] = peak


def local_peak(pattern, queries, keys):
    rows, cols = queries.shape[0], keys.shape[0]
    return pl.pallas_call(
        peak_kernel,
        out_shape=jax.ShapeDtypeStruct((HEADS, rows), F32),
        in_specs=[SMEM, VMEM, VMEM],
        out_specs=VMEM,
        compiler_params=params(),
        cost_estimate=cost(4 * rows * cols * D, 2 * rows * D + 2 * cols * D),
        name="local_peak",
    )(pattern, queries, keys)


def expo_kernel(pattern_ref, q_ref, k_ref, peak_ref, out_ref):
    rows, cols = q_ref.shape[0], k_ref.shape[0]
    block_rows, block_cols = rows // BLK, cols // BLK
    extra = [peak_ref[...].astype(F32)]
    for b in range(block_cols):
        extra.append(
            jnp.concatenate(
                [
                    jnp.full((1, BLK), jnp.where(pattern_ref[i, b] > 0, 0.0, -1e30), F32)
                    for i in range(block_rows)
                ],
                axis=1,
            )
        )
    extra.append(jnp.zeros((LANES - HEADS - block_cols, rows), F32))
    extra = jnp.concatenate(extra, axis=0).T.astype(BF16)
    lane = lax.broadcasted_iota(jnp.int32, (2 * cols, LANES), 1)
    key = lax.broadcasted_iota(jnp.int32, (2 * cols, LANES), 0)
    block_of = jnp.where(key >= cols, key - cols, key) // BLK
    in_block = jnp.where(lane - HEADS == block_of, 1.0, 0.0)
    side = jnp.where(key >= cols, 1, 0)
    for p in range(PAIRS):
        lanes = slice(p * LANES, (p + 1) * LANES)
        head_lane = jnp.where(lane == 2 * p + side, -1.0, in_block).astype(BF16)
        right = jnp.concatenate([split_heads(k_ref[:, lanes]), head_lane], axis=1)

        for t in range(block_rows):
            left = jnp.concatenate(
                [q_ref[t * BLK : (t + 1) * BLK, lanes], extra[t * BLK : (t + 1) * BLK, :]], axis=1
            )
            s = lax.dot_general(
                left, right, (((1,), (1,)), ((), ())), preferred_element_type=F32
            )
            out_ref[p, t * BLK : (t + 1) * BLK, :] = jnp.exp(s).astype(BF16)


def exponentials(pattern, queries, keys, peak):
    rows, cols = queries.shape[0], keys.shape[0]
    return pl.pallas_call(
        expo_kernel,
        out_shape=jax.ShapeDtypeStruct((PAIRS, rows, 2 * cols), BF16),
        in_specs=[SMEM, VMEM, VMEM, VMEM],
        out_specs=VMEM,
        compiler_params=params(),
        cost_estimate=cost(
            8 * rows * cols * D, 2 * HEADS * rows * cols, HEADS * rows * cols
        ),
        name="expo",
    )(pattern, queries, keys, peak)


def weigh_kernel(root, place_ref, gain_ref, rate_ref, ranks_ref, expo_ref, v_ref, out_ref, p_ref):
    rows, cols = ranks_ref.shape
    chip, side = place_ref[0], place_ref[1]
    chips = place_ref.shape[0] - 2
    seg = out_ref.shape[0] // chips
    lane = lax.broadcasted_iota(jnp.int32, (cols, LANES), 1)
    zero = jnp.zeros((cols, LANES), BF16)
    low = jnp.where(lane < HDIM, 1.0, 0.0).astype(BF16)
    high = jnp.where(lane < HDIM, 0.0, 1.0).astype(BF16)
    out_lane = lax.broadcasted_iota(jnp.int32, (out_ref.shape[0], LANES), 1)
    totals = jnp.zeros((out_ref.shape[0], LANES), F32)
    for p in range(PAIRS):
        lanes = slice(p * LANES, (p + 1) * LANES)
        values = v_ref[:, lanes]
        right = jnp.concatenate(
            [
                jnp.concatenate([jnp.where(lane < HDIM, values, zero), low], axis=1),
                jnp.concatenate([jnp.where(lane < HDIM, zero, values), high], axis=1),
            ],
            axis=0,
        )
        for k in range(chips):
            start = pl.multiple_of((2 * lax.bitwise_xor(chip, k) + side) * seg, seg)
            ranks = ranks_ref[pl.ds(start, seg), :]
            for head_side in range(2):
                head = 2 * p + head_side
                rate = jnp.full((1, cols), rate_ref[head] * root, F32).astype(BF16)
                gain = jnp.full((1, cols), gain_ref[head] * math.log2(math.e), F32).astype(BF16)
                bias = gain * jnp.tanh(rate * ranks)
                at = slice(head_side * cols, (head_side + 1) * cols)
                p_ref[k * seg : (k + 1) * seg, at] = (
                    expo_ref[p, pl.ds(start, seg), at] * jnp.exp2(bias)
                )
        sums = jnp.dot(p_ref[...], right, preferred_element_type=F32)
        out_ref[:, lanes] = sums[:, :LANES].astype(BF16)
        totals = jnp.where(out_lane % HDIM == p, sums[:, LANES:], totals)
    out_ref[:, D:] = totals.astype(BF16)


def weigh(root, place, chips, gain, rate, ranks, expo, values):
    rows, cols = ranks.shape
    return pl.pallas_call(
        functools.partial(weigh_kernel, root),
        out_shape=jax.ShapeDtypeStruct((rows // 2, D + LANES), BF16),
        in_specs=[SMEM, SMEM, SMEM, VMEM, VMEM, VMEM],
        out_specs=VMEM,
        scratch_shapes=[pltpu.VMEM((rows // 2, 2 * cols), BF16)],
        compiler_params=params(),
        cost_estimate=cost(
            4 * rows * cols * D, HEADS * rows * cols, HEADS * rows * cols
        ),
        name="weigh",
    )(place, gain, rate, ranks, expo, values)


def project_kernel(*refs):
    parts, w_ref, out_ref = refs[:-2], refs[-2], refs[-1]
    total = parts[0][...].astype(F32)
    for part in parts[1:]:
        total += part[...].astype(F32)
    seg = total.shape[0]
    inverse = 1.0 / total[:, D:]
    lane = lax.broadcasted_iota(jnp.int32, (seg, LANES), 1)
    attended = []
    for p in range(PAIRS):
        scale = jnp.where(
            lane < HDIM,
            jnp.broadcast_to(inverse[:, p : p + 1], (seg, LANES)),
            jnp.broadcast_to(inverse[:, HDIM + p : HDIM + p + 1], (seg, LANES)),
        )
        attended.append((total[:, p * LANES : (p + 1) * LANES] * scale).astype(BF16))
    attended = jnp.concatenate(attended, axis=1)
    for c in range(w_ref.shape[0]):
        out_ref[c] = jnp.dot(attended, w_ref[c], preferred_element_type=F32).astype(BF16)


def project(parts, w_all):
    seg = parts[0].shape[0]
    return pl.pallas_call(
        project_kernel,
        out_shape=jax.ShapeDtypeStruct((w_all.shape[0], seg, w_all.shape[2]), BF16),
        in_specs=[VMEM] * (len(parts) + 1),
        out_specs=VMEM,
        compiler_params=params(),
        cost_estimate=cost(2 * seg * w_all.size, 2 * w_all.size),
        name="project",
    )(*parts, w_all)


def gather_rows(block, count):
    return [block] + [lax.ppermute(block, "row", xor_pairs(count, j)) for j in range(1, count)]


def fetch_key_rows(features, cols, row_count, col_count):
    ratio = features.shape[0] // cols
    col_pos, row_pos = lax.axis_index("col"), lax.axis_index("row")
    half = lax.dynamic_slice_in_dim(features, col_pos % ratio * cols, cols, 0)
    away = lax.bitwise_xor(row_pos, col_pos // ratio)

    def pairs(sends):
        found = []
        for c in range(col_count):
            source = c // ratio
            for a, b in sends:
                found.append(((source ^ a) * col_count + c, (source ^ b) * col_count + c))
        return found

    axes = ("row", "col")
    if row_count != 4:
        got = half
        for j in range(1, row_count):
            got = jnp.where(away == j, lax.ppermute(half, axes, pairs([(0, j)])), got)
        return got
    near = lax.ppermute(half, axes, pairs([(0, 1)]))
    side = lax.ppermute(half, axes, pairs([(0, 2)]))
    mid = cols // 2
    first = lax.ppermute(near[:mid], axes, pairs([(1, 3)]))
    second = lax.ppermute(side[mid:], axes, pairs([(2, 3)]))
    return jnp.where(
        away == 0,
        half,
        jnp.where(
            away == 1,
            near,
            jnp.where(away == 2, side, jnp.concatenate([first, second], axis=0)),
        ),
    )


def expand_blocks(pattern):
    block_rows, block_cols = pattern.shape
    grid = jnp.broadcast_to(pattern[:, None, :, None] > 0, (block_rows, BLK, block_cols, BLK))
    return grid.reshape(block_rows * BLK, block_cols * BLK)


def shards(node_features, edge_weight, pattern, w_qkv, w_out, bias_gain, bias_rate):
    rows, cols = edge_weight.shape
    row_count, col_count = lax.axis_size("row"), lax.axis_size("col")
    row_pos, col_pos = lax.axis_index("row"), lax.axis_index("col")
    chips = col_count // 2
    chip, core = col_pos // 2, col_pos % 2
    root = math.sqrt(rows * row_count)
    place = jnp.stack([row_pos, col_pos]).astype(jnp.int32)

    adjacency = jnp.where(expand_blocks(pattern), edge_weight, jnp.zeros_like(edge_weight))
    panel = lax.all_gather(adjacency, "col", axis=0, tiled=False)
    w_all = lax.all_gather(w_out, "col", axis=0, tiled=False)
    columns = gather_rows(adjacency, row_count)
    key_rows = fetch_key_rows(node_features, cols, row_count, col_count)

    queries = jnp.dot(node_features, w_qkv[:, :D], preferred_element_type=F32).astype(BF16)
    queries = queries * jnp.asarray(1.0 / math.sqrt(HDIM), BF16)
    keys = jnp.dot(key_rows, w_qkv[:, D : 2 * D], preferred_element_type=F32).astype(BF16)
    values = jnp.dot(key_rows, w_qkv[:, 2 * D :], preferred_element_type=F32).astype(BF16)

    peak = local_peak(pattern, queries, keys).astype(BF16)
    step = 1
    while step < col_count:
        peak = jnp.maximum(peak, lax.ppermute(peak, "col", xor_pairs(col_count, step)))
        step *= 2
    expo = exponentials(pattern, queries, keys, peak)

    ranks = sweep(True, place, pattern, adjacency, panel, columns, BF16)
    columns = gather_rows(ranks, row_count)
    ranks = sweep(False, place, pattern, adjacency, panel, columns, BF16)

    def part(side):
        where = jnp.concatenate(
            [jnp.stack([chip, side]).astype(jnp.int32), jnp.zeros((chips,), jnp.int32)]
        )
        return weigh(root, where, chips, bias_gain, bias_rate, ranks, expo, values)

    other = lax.ppermute(part(1 - core), "col", xor_pairs(col_count, 1))
    mine = part(core)
    seg = rows // col_count
    parts = []
    for k in range(chips):
        at = slice(k * seg, (k + 1) * seg)
        both = (mine[at].astype(F32) + other[at].astype(F32)).astype(BF16)
        parts.append(both if k == 0 else lax.ppermute(both, "col", xor_pairs(col_count, 2 * k)))
    mixed = project(parts, w_all)
    mixed = lax.all_to_all(mixed, "col", split_axis=0, concat_axis=0, tiled=True)
    return mixed.reshape(rows, w_out.shape[1])


def solution(mesh):
    in_specs = (P("row", None), P("row", "col"), P("row", "col"), P(), P(None, "col"), P(), P())
    out_specs = P("row", "col")
    return jax.shard_map(shards, mesh=mesh, in_specs=in_specs, out_specs=out_specs, check_vma=False)
```

```python
import functools
import math

import jax
import jax.numpy as jnp
from jax import lax
from jax.experimental import pallas as pl
from jax.experimental.pallas import tpu as pltpu
from jax.sharding import PartitionSpec as P

D = 1024
HEADS = 16
BLK = 128
HDIM = 64
CORES = 2
PAIRS = HEADS // 2 // CORES
WIDTH = D // CORES
STEP = 8
LANES = 128
VMEM_LIMIT = 58 * 2**20
SMALL_LIMIT = 16 * 2**20

VMEM = pl.BlockSpec(memory_space=pltpu.VMEM)
SMEM = pl.BlockSpec(memory_space=pltpu.SMEM)
HBM = pl.BlockSpec(memory_space=pltpu.HBM)
BF16 = jnp.bfloat16
F32 = jnp.float32


def params(limit=VMEM_LIMIT):
    return pltpu.CompilerParams(vmem_limit_bytes=limit)


def cost(flops, nbytes, trans=0):
    return pl.CostEstimate(flops=int(flops), bytes_accessed=int(nbytes), transcendentals=int(trans))


def xor_pairs(n, j):
    return [(i, i ^ j) for i in range(n)]


def keep_tile(pattern_ref, first_row, block_rows):
    block_cols = pattern_ref.shape[0]
    tiles = []
    for i in range(block_rows):
        parts = [
            jnp.full((1, BLK), jnp.where(pattern_ref[b, first_row + i] > 0, 1.0, 0.0), F32)
            for b in range(block_cols)
        ]
        tiles.append(
            jnp.broadcast_to(jnp.concatenate(parts, axis=1), (BLK, block_cols * BLK))
        )
    return jnp.concatenate(tiles, axis=0)


def mask_kernel(pattern_ref, weight_ref, out_ref):
    for i in range(out_ref.shape[0] // BLK):
        at = slice(i * BLK, (i + 1) * BLK)
        keep = keep_tile(pattern_ref, i, 1)
        out_ref[at, :] = jnp.where(keep > 0, weight_ref[at, :].astype(F32), 0.0).astype(BF16)


def mask(pattern, weight):
    rows, cols = weight.shape
    return pl.pallas_call(
        mask_kernel,
        out_shape=jax.ShapeDtypeStruct((rows, cols), BF16),
        in_specs=[SMEM, VMEM],
        out_specs=VMEM,
        compiler_params=params(SMALL_LIMIT),
        cost_estimate=cost(rows * cols, 4 * rows * cols),
        name="mask",
    )(pattern, weight)


def project_in_kernel(scale, place_ref, *refs):
    xs, (w_ref, out_ref) = refs[:-2], refs[-2:]
    rows = xs[0].shape[0]
    for i, x_ref in enumerate(xs):
        out = jnp.dot(x_ref[...], w_ref[...], preferred_element_type=F32).astype(BF16)
        if scale is not None:
            out = out * jnp.asarray(scale, BF16)
        out_ref[i * rows : (i + 1) * rows, :] = out


def project_in(core, xs, w, firsts, scale=None, tile=256):
    rows, depth = xs[0].shape
    steps = WIDTH // tile

    def column(i, core_ref):
        first = firsts[0] // tile
        for n, start in enumerate(firsts[1:], 1):
            first = jnp.where(i >= n * steps, start // tile, first)
        return 0, first + core_ref[0] * steps + lax.rem(i, steps)

    return pl.pallas_call(
        functools.partial(project_in_kernel, scale),
        out_shape=jax.ShapeDtypeStruct((rows * len(xs), WIDTH * len(firsts)), BF16),
        grid_spec=pltpu.PrefetchScalarGridSpec(
            num_scalar_prefetch=1,
            grid=(steps * len(firsts),),
            in_specs=[pl.BlockSpec((rows, depth), lambda i, c: (0, 0))] * len(xs)
            + [pl.BlockSpec((depth, tile), column)],
            out_specs=pl.BlockSpec((rows * len(xs), tile), lambda i, c: (0, i)),
        ),
        compiler_params=params(),
        cost_estimate=cost(
            2 * rows * len(xs) * depth * WIDTH * len(firsts),
            2 * depth * (rows * len(xs) + WIDTH * len(firsts)),
        ),
        name="project_in",
    )(core, *xs, w)


def sweep_kernel(first, ks, n_right, place_ref, pattern_ref, panel_ref, *refs):
    rights, (out_ref, left_ref, right_ref, acc_ref, sem) = refs[:n_right], refs[-5:]
    count, rows, cols = panel_ref.shape
    ratio = count // n_right
    seg = out_ref.shape[0] // len(ks)
    row_pos, col_pos = place_ref[0], place_ref[1]
    starts = [
        pl.multiple_of(lax.bitwise_xor(lax.div(col_pos, CORES), k) * seg, seg) for k in ks
    ]
    if len(ks) == count // CORES:
        starts = [n * seg for n in range(len(ks))]

    def left_copies(j):
        for i in range(ratio):
            c = lax.bitwise_xor(row_pos, j) * ratio + i
            for n, start in enumerate(starts):
                yield pltpu.make_async_copy(
                    panel_ref.at[c, pl.ds(start, seg), :],
                    left_ref.at[j, pl.ds(n * seg, seg), i * cols : (i + 1) * cols],
                    sem.at[j, i * len(ks) + n],
                )

    def right_copy(j):
        return pltpu.make_async_copy(rights[j], right_ref.at[j], sem.at[j, ratio * len(ks)])

    for j in range(n_right):
        right_copy(j).start()
        for copy in left_copies(j):
            copy.start()
    for j in range(n_right):
        right_copy(j).wait()
        for copy in left_copies(j):
            copy.wait()
        product = jnp.dot(left_ref[j], right_ref[j], preferred_element_type=F32)
        if j == 0:
            acc_ref[...] = product
        elif j < n_right - 1:
            acc_ref[...] += product
    product = product + acc_ref[...]
    home = lax.bitwise_xor(row_pos, lax.div(col_pos, ratio))
    at = pl.multiple_of(lax.rem(col_pos, ratio) * cols, cols)
    own = left_ref[home, :, pl.ds(at, cols)].astype(F32)
    total = 0.1275 * own + (0.85 * 0.1275 if first else 0.85) * product
    diagonal = lax.broadcasted_iota(jnp.int32, (seg, cols), 1) - lax.broadcasted_iota(
        jnp.int32, (seg, cols), 0
    )
    lane_block = lax.broadcasted_iota(jnp.int32, (1, cols), 1) // BLK
    for n, start in enumerate(starts):
        at = slice(n * seg, (n + 1) * seg)
        part = total[at, :]
        if not first:
            here = diagonal == row_pos * rows + start - col_pos * cols
            part = jnp.where(here, part + 0.15, part)
        size = math.gcd(seg, BLK)
        for i in range(seg // size):
            keep = jnp.zeros((1, cols), F32)
            for b in range(cols // BLK):
                kept = pattern_ref[b, lax.div(start + i * size, BLK)] > 0
                keep = jnp.where(lane_block == b, jnp.where(kept, 1.0, 0.0), keep)
            piece = part[i * size : (i + 1) * size, :]
            out_ref[n * seg + i * size : n * seg + (i + 1) * size, :] = jnp.where(
                keep > 0, piece, 0.0
            ).astype(BF16)


def sweep(first, ks, place, pattern, panel, blocks, follows, limit=VMEM_LIMIT):
    count, rows, cols = panel.shape
    ratio = count // len(blocks)
    n_rows = rows * CORES // count * len(ks)
    return pl.pallas_call(
        functools.partial(sweep_kernel, first, ks, len(blocks)),
        out_shape=jax.ShapeDtypeStruct((n_rows, cols), BF16),
        in_specs=[SMEM, SMEM] + [HBM] * (2 + len(blocks)),
        out_specs=VMEM,
        scratch_shapes=[
            pltpu.VMEM((len(blocks), n_rows, ratio * cols), BF16),
            pltpu.VMEM((len(blocks), rows, cols), BF16),
            pltpu.VMEM((n_rows, cols), F32),
            pltpu.SemaphoreType.DMA((len(blocks), ratio * len(ks) + 1)),
        ],
        compiler_params=params(limit),
        cost_estimate=cost(2 * n_rows * count * cols * cols, 2 * (n_rows + rows) * count * cols),
        name="rank_sweep",
    )(place, pattern, panel, *blocks, follows)


def split_heads(keys):
    lane = lax.broadcasted_iota(jnp.int32, keys.shape, 1)
    zero = jnp.zeros_like(keys)
    return jnp.concatenate(
        [jnp.where(lane < HDIM, keys, zero), jnp.where(lane >= HDIM, keys, zero)], axis=0
    )


def expo_kernel(own_ref, other_ref, q_ref, k_ref, out_ref, peak_ref, mask_ref):
    p = pl.program_id(0)
    rows, keys = q_ref.shape[0], k_ref.shape[0]
    block_rows, block_cols = rows // BLK, keys // BLK
    tile = BLK

    @pl.when(p == 0)
    def _():
        lane = lax.broadcasted_iota(jnp.int32, (BLK, LANES), 1)
        for i in range(block_rows):
            excluded = jnp.zeros((BLK, LANES), F32)
            for b in range(block_cols):
                ref, at = (own_ref, b) if b < block_cols // 2 else (other_ref, b - block_cols // 2)
                excluded = jnp.where(lane == b, jnp.where(ref[at, i] > 0, 0.0, -1e30), excluded)
            mask_ref[i * BLK : (i + 1) * BLK, :] = excluded.astype(BF16)
        peak_ref[...] = jnp.zeros_like(peak_ref)

    lane = lax.broadcasted_iota(jnp.int32, (2 * keys, LANES), 1)
    key = lax.broadcasted_iota(jnp.int32, (2 * keys, LANES), 0)
    block_of = jnp.where(key >= keys, key - keys, key) // BLK
    in_block = jnp.where(lane == block_of, 1.0, 0.0).astype(BF16)
    right = jnp.concatenate([split_heads(k_ref[...]), in_block], axis=1)
    peak_lane = lax.broadcasted_iota(jnp.int32, (tile, LANES), 1)
    for t in range(rows // tile):
        at = slice(t * tile, (t + 1) * tile)
        left = jnp.concatenate([q_ref[at, :], mask_ref[at, :]], axis=1)
        s = lax.dot_general(left, right, (((1,), (1,)), ((), ())), preferred_element_type=F32)
        peaks = peak_ref[at, :]
        for side in range(2):
            part = s[:, side * keys : (side + 1) * keys]
            peak = jnp.max(part, axis=1, keepdims=True)
            peaks = jnp.where(peak_lane == HDIM * side + p, peak, peaks)
            out_ref[0, at, side * keys : (side + 1) * keys] = jnp.exp(part - peak).astype(BF16)
        peak_ref[at, :] = peaks


def exponentials(own, other, queries, keys_values):
    rows, keys = queries.shape[0], keys_values.shape[0]
    work = rows * keys * 2 * PAIRS
    return pl.pallas_call(
        expo_kernel,
        out_shape=(
            jax.ShapeDtypeStruct((PAIRS, rows, 2 * keys), BF16),
            jax.ShapeDtypeStruct((rows, LANES), F32),
        ),
        grid=(PAIRS,),
        in_specs=[
            SMEM,
            SMEM,
            pl.BlockSpec((rows, LANES), lambda p: (0, p)),
            pl.BlockSpec((keys, LANES), lambda p: (0, p)),
        ],
        out_specs=(
            pl.BlockSpec((1, rows, 2 * keys), lambda p: (p, 0, 0)),
            pl.BlockSpec((rows, LANES), lambda p: (0, 0)),
        ),
        scratch_shapes=[pltpu.VMEM((rows, LANES), BF16)],
        compiler_params=params(),
        cost_estimate=cost(512 * work, 2 * work, work),
        name="expo",
    )(own, other, queries, keys_values)


def weigh_kernel(
    root, ks, seg, place_ref, gain_ref, rate_ref, own_ref, other_ref, expo_ref, v_ref, peak_ref,
    *refs,
):
    out_refs, (e_ref, p_ref, ranks_ref, right_ref, sem) = refs[: len(ks)], refs[len(ks) :]
    cols = own_ref.shape[1]
    keys = 2 * cols
    chip = lax.div(place_ref[1], CORES)
    first_head = lax.rem(place_ref[1], CORES) * 2 * PAIRS
    starts = [pl.multiple_of(lax.bitwise_xor(chip, k) * seg, seg) for k in ks]

    def copy(p, i):
        return pltpu.make_async_copy(
            expo_ref.at[p, pl.ds(starts[i], seg), :],
            e_ref.at[p, pl.ds(i * seg, seg), :],
            sem.at[p, i],
        )

    for p in range(PAIRS):
        for i in range(len(ks)):
            copy(p, i).start()
    for i in range(len(ks)):
        at = slice(i * seg, (i + 1) * seg)
        ranks_ref[at, :cols] = own_ref[at, :].astype(F32)
        ranks_ref[at, cols:] = other_ref[at, :].astype(F32)
    lane = lax.broadcasted_iota(jnp.int32, (keys, LANES), 1)
    zero = jnp.zeros((keys, LANES), BF16)
    right_ref[:keys, LANES:] = jnp.where(lane < HDIM, 1.0, 0.0).astype(BF16)
    right_ref[keys:, LANES:] = jnp.where(lane < HDIM, 0.0, 1.0).astype(BF16)
    out_lane = lax.broadcasted_iota(jnp.int32, (seg, LANES), 1)

    def pair(p, totals):
        lanes = pl.ds(pl.multiple_of(p * LANES, LANES), LANES)
        values = v_ref[:, lanes]
        right_ref[:keys, :LANES] = jnp.where(lane < HDIM, values, zero)
        right_ref[keys:, :LANES] = jnp.where(lane < HDIM, zero, values)
        for i in range(len(ks)):
            copy(p, i).wait()
        for i in range(len(ks)):
            rows_at = slice(i * seg, (i + 1) * seg)
            for half in range(2):
                ranks = ranks_ref[rows_at, half * cols : (half + 1) * cols]
                for side in range(2):
                    rate = rate_ref[first_head + 2 * p + side] * root
                    gain = gain_ref[first_head + 2 * p + side] * math.log2(math.e)
                    at = slice(side * keys + half * cols, side * keys + (half + 1) * cols)
                    weight = e_ref[p, rows_at, at].astype(F32) * jnp.exp2(
                        gain * jnp.tanh(rate * ranks)
                    )
                    p_ref[rows_at, at] = weight.astype(BF16)
        sums = jnp.dot(p_ref[...], right_ref[...], preferred_element_type=F32)
        now = []
        for i, out_ref in enumerate(out_refs):
            part = sums[i * seg : (i + 1) * seg, :]
            out_ref[:, lanes] = part[:, :LANES].astype(BF16)
            now.append(jnp.where(out_lane % HDIM == p, part[:, LANES:], totals[i]))
        return tuple(now)

    totals = lax.fori_loop(
        0, PAIRS, pair, tuple(jnp.zeros((seg, LANES), F32) for _ in ks)
    )
    for i, out_ref in enumerate(out_refs):
        extra = totals[i]
        rest = peak_ref[pl.ds(starts[i], seg), :]
        for n in range(1, 4):
            piece = rest.astype(BF16).astype(F32)
            rest = rest - piece
            here = (out_lane % HDIM >= n * STEP) & (out_lane % HDIM < n * STEP + PAIRS)
            extra = jnp.where(here, pltpu.roll(piece, n * STEP, 1), extra)
        out_ref[:, WIDTH:] = extra.astype(BF16)


def weigh(root, chips, ks, place, gain, rate, own, other, expo, values, peak):
    n_rows, cols = own.shape
    seg = n_rows // len(ks)
    rows, keys = seg * chips, 2 * cols
    work = n_rows * keys * 2 * PAIRS
    return pl.pallas_call(
        functools.partial(weigh_kernel, root, ks, seg),
        out_shape=(jax.ShapeDtypeStruct((seg, WIDTH + LANES), BF16),) * len(ks),
        grid=(1,),
        in_specs=[
            SMEM,
            SMEM,
            SMEM,
            pl.BlockSpec((n_rows, cols), lambda i: (0, 0)),
            pl.BlockSpec((n_rows, cols), lambda i: (0, 0)),
            HBM,
            pl.BlockSpec((keys, WIDTH), lambda i: (0, 1)),
            pl.BlockSpec((rows, LANES), lambda i: (0, 0)),
        ],
        out_specs=(pl.BlockSpec((seg, WIDTH + LANES), lambda i: (0, 0)),) * len(ks),
        scratch_shapes=[
            pltpu.VMEM((PAIRS, n_rows, 2 * keys), BF16),
            pltpu.VMEM((n_rows, 2 * keys), BF16),
            pltpu.VMEM((n_rows, keys), F32),
            pltpu.VMEM((2 * keys, 2 * LANES), BF16),
            pltpu.SemaphoreType.DMA((PAIRS, len(ks))),
        ],
        compiler_params=params(),
        cost_estimate=cost(512 * work, 2 * work, 2 * work),
        name="weigh",
    )(place, gain, rate, own, other, expo, values, peak)


def divide_kernel(*refs):
    parts, out_ref = refs[:-1], refs[-1]
    extras = [part[:, WIDTH:].astype(F32) for part in parts]
    seg = extras[0].shape[0]
    peaks = [sum(pltpu.roll(x, LANES - n * STEP, 1) for n in range(1, 4)) for x in extras]
    largest = functools.reduce(jnp.maximum, peaks)
    weights = [jnp.exp(peak - largest) for peak in peaks]
    inverse = 1.0 / sum(w * x for w, x in zip(weights, extras, strict=True))
    scales = [w * inverse for w in weights]
    lane = lax.broadcasted_iota(jnp.int32, (seg, LANES), 1)
    for p in range(PAIRS):
        lanes = slice(p * LANES, (p + 1) * LANES)
        total = jnp.zeros((seg, LANES), F32)
        for part, scale in zip(parts, scales, strict=True):
            both = jnp.where(lane < HDIM, scale[:, p : p + 1], scale[:, HDIM + p : HDIM + p + 1])
            total += part[:, lanes].astype(F32) * both
        out_ref[:, lanes] = total.astype(BF16)


def divide(parts):
    seg = parts[0].shape[0]
    return pl.pallas_call(
        divide_kernel,
        out_shape=jax.ShapeDtypeStruct((seg, WIDTH), BF16),
        in_specs=[VMEM] * len(parts),
        out_specs=VMEM,
        compiler_params=params(SMALL_LIMIT),
        cost_estimate=cost(8 * seg * D, 8 * seg * D),
        name="divide",
    )(*parts)


def project_out_kernel(place_ref, own_ref, other_ref, w_ref, *out_refs):
    chip, core = lax.div(place_ref[1], CORES), lax.rem(place_ref[1], CORES)
    for k, out_ref in enumerate(out_refs):
        slot = CORES * lax.bitwise_xor(chip, k) + core
        total = jnp.dot(
            own_ref[...],
            w_ref[slot, pl.ds(pl.multiple_of(core * WIDTH, WIDTH), WIDTH), :],
            preferred_element_type=F32,
        ) + jnp.dot(
            other_ref[...],
            w_ref[slot, pl.ds(pl.multiple_of((1 - core) * WIDTH, WIDTH), WIDTH), :],
            preferred_element_type=F32,
        )
        out_ref[...] = total.astype(BF16)


def project_out(place, own, other, w_all, chips):
    seg = own.shape[0]
    return pl.pallas_call(
        project_out_kernel,
        out_shape=(jax.ShapeDtypeStruct((seg, w_all.shape[2]), BF16),) * chips,
        in_specs=[SMEM] + [VMEM] * 3,
        out_specs=(VMEM,) * chips,
        compiler_params=params(SMALL_LIMIT),
        cost_estimate=cost(seg * w_all.size, 2 * w_all.size),
        name="project_out",
    )(place, own, other, w_all)


def assemble_kernel(place_ref, *refs):
    parts, out_ref = refs[:-1], refs[-1]
    chip = lax.div(place_ref[1], CORES)
    seg = parts[0].shape[0]
    for k, part in enumerate(parts):
        at = pl.multiple_of(lax.bitwise_xor(chip, k) * seg, seg)
        out_ref[pl.ds(at, seg), :] = part[...]


def assemble(place, parts):
    seg, width = parts[0].shape
    return pl.pallas_call(
        assemble_kernel,
        out_shape=jax.ShapeDtypeStruct((seg * len(parts), width), BF16),
        in_specs=[SMEM] + [VMEM] * len(parts),
        out_specs=VMEM,
        compiler_params=params(SMALL_LIMIT),
        name="assemble",
    )(place, *parts)


def from_rows(value, row_count):
    return [value] + [
        lax.ppermute(value, "row", xor_pairs(row_count, j)) for j in range(1, row_count)
    ]


def key_features(features, cols, row_count, col_count, beside):
    ratio = features.shape[0] // cols
    col_pos, row_pos = lax.axis_index("col"), lax.axis_index("row")
    own = lax.dynamic_slice_in_dim(features, col_pos % ratio * cols, cols, 0)
    away = lax.bitwise_xor(row_pos, col_pos // ratio)

    def send(value, a, b):
        pairs = [
            (((c // ratio) ^ a) * col_count + c, ((c // ratio) ^ b) * col_count + c)
            for c in range(col_count)
        ]
        return lax.ppermute(value, ("row", "col"), pairs)

    if row_count != 4:
        got = own
        for j in range(1, row_count):
            got = jnp.where(away == j, send(own, 0, j), got)
        return got, beside
    near, side = send(own, 0, 1), send(own, 0, 2)
    near, side, beside = lax.optimization_barrier((near, side, beside))
    mid = cols // 2
    low, high = send(near[:mid], 1, 3), send(side[mid:], 2, 3)
    got = jnp.where(away == 1, near, jnp.where(away == 2, side, own))
    return jnp.where(away == 3, jnp.concatenate([low, high], axis=0), got), beside


def shards(node_features, edge_weight, pattern, w_qkv, w_out, bias_gain, bias_rate):
    rows, cols = edge_weight.shape
    row_count, col_count = lax.axis_size("row"), lax.axis_size("col")
    row_pos, col_pos = lax.axis_index("row"), lax.axis_index("col")
    chips = col_count // CORES
    root = math.sqrt(rows * row_count)
    place = jnp.stack([row_pos, col_pos]).astype(jnp.int32)
    core = (col_pos % CORES).astype(jnp.int32).reshape(1)
    pattern = pattern.T

    def along_col(value, j):
        return lax.ppermute(value, "col", xor_pairs(col_count, j))

    adjacency = mask(pattern, edge_weight)
    panel = lax.all_gather(adjacency, "col", axis=0, tiled=False)
    w_all = lax.all_gather(w_out, "col", axis=0, tiled=False)
    columns = from_rows(adjacency, row_count)
    queries = project_in(core, [node_features], w_qkv, [0], 1.0 / math.sqrt(HDIM))
    key_rows, queries = key_features(node_features, cols, row_count, col_count, queries)

    other_rows = along_col(key_rows, 1)
    other_pattern = along_col(pattern.astype(F32), 1).astype(jnp.int32)
    keys_values = project_in(core, [key_rows, other_rows], w_qkv, [D, 2 * D])
    expo, peak = exponentials(pattern, other_pattern, queries, keys_values)

    ranks = sweep(True, range(chips), place, pattern, panel, columns, node_features)
    columns = from_rows(ranks, row_count)

    parts = [None] * chips
    for ks in (list(range(chips // 2, chips)), list(range(chips // 2))):
        ranks = sweep(False, ks, place, pattern, panel, columns, peak)
        sums = weigh(
            root, chips, ks, place, bias_gain, bias_rate, ranks, along_col(ranks, 1), expo,
            keys_values, peak,
        )
        for k, part in zip(ks, sums, strict=True):
            parts[k] = part if k == 0 else along_col(part, CORES * k)
    attended = divide(parts)
    mixed = project_out(place, attended, along_col(attended, 1), w_all, chips)
    mixed = [x if k == 0 else along_col(x, CORES * k) for k, x in enumerate(mixed)]
    return assemble(place, mixed)


def solution(mesh):
    in_specs = (P("row", None), P("row", "col"), P("row", "col"), P(), P(None, "col"), P(), P())
    out_specs = P("row", "col")
    return jax.shard_map(shards, mesh=mesh, in_specs=in_specs, out_specs=out_specs, check_vma=False)
```

```python
import functools
import math

import jax
import jax.numpy as jnp
from jax import lax
from jax.experimental import pallas as pl
from jax.experimental.pallas import tpu as pltpu
from jax.sharding import PartitionSpec as P

D = 1024
HEADS = 16
BLK = 128
HDIM = 64
CORES = 2
PAIRS = HEADS // 2 // CORES
WIDTH = D // CORES
STEP = 8
LANES = 128
VMEM_LIMIT = 58 * 2**20
SMALL_LIMIT = 16 * 2**20

VMEM = pl.BlockSpec(memory_space=pltpu.VMEM)
SMEM = pl.BlockSpec(memory_space=pltpu.SMEM)
HBM = pl.BlockSpec(memory_space=pltpu.HBM)
BF16 = jnp.bfloat16
F32 = jnp.float32


def params(limit=VMEM_LIMIT):
    return pltpu.CompilerParams(vmem_limit_bytes=limit)


def cost(flops, nbytes, trans=0):
    return pl.CostEstimate(flops=int(flops), bytes_accessed=int(nbytes), transcendentals=int(trans))


def xor_pairs(n, j):
    return [(i, i ^ j) for i in range(n)]


def keep_tile(pattern_ref, first_row, block_rows):
    block_cols = pattern_ref.shape[0]
    tiles = []
    for i in range(block_rows):
        parts = [
            jnp.full((1, BLK), jnp.where(pattern_ref[b, first_row + i] > 0, 1.0, 0.0), F32)
            for b in range(block_cols)
        ]
        tiles.append(
            jnp.broadcast_to(jnp.concatenate(parts, axis=1), (BLK, block_cols * BLK))
        )
    return jnp.concatenate(tiles, axis=0)


def mask_kernel(pattern_ref, weight_ref, out_ref):
    for i in range(out_ref.shape[0] // BLK):
        at = slice(i * BLK, (i + 1) * BLK)
        keep = keep_tile(pattern_ref, i, 1)
        out_ref[at, :] = jnp.where(keep > 0, weight_ref[at, :].astype(F32), 0.0).astype(BF16)


def mask(pattern, weight):
    rows, cols = weight.shape
    return pl.pallas_call(
        mask_kernel,
        out_shape=jax.ShapeDtypeStruct((rows, cols), BF16),
        in_specs=[SMEM, VMEM],
        out_specs=VMEM,
        compiler_params=params(SMALL_LIMIT),
        cost_estimate=cost(rows * cols, 4 * rows * cols),
        name="mask",
    )(pattern, weight)


def project_in_kernel(scale, place_ref, *refs):
    xs, (w_ref, out_ref) = refs[:-2], refs[-2:]
    rows = xs[0].shape[0]
    for i, x_ref in enumerate(xs):
        out = jnp.dot(x_ref[...], w_ref[...], preferred_element_type=F32).astype(BF16)
        if scale is not None:
            out = out * jnp.asarray(scale, BF16)
        out_ref[i * rows : (i + 1) * rows, :] = out


def project_in(core, xs, w, firsts, scale=None, tile=256, limit=VMEM_LIMIT):
    rows, depth = xs[0].shape
    steps = WIDTH // tile

    def column(i, core_ref):
        first = firsts[0] // tile
        for n, start in enumerate(firsts[1:], 1):
            first = jnp.where(i >= n * steps, start // tile, first)
        return 0, first + core_ref[0] * steps + lax.rem(i, steps)

    return pl.pallas_call(
        functools.partial(project_in_kernel, scale),
        out_shape=jax.ShapeDtypeStruct((rows * len(xs), WIDTH * len(firsts)), BF16),
        grid_spec=pltpu.PrefetchScalarGridSpec(
            num_scalar_prefetch=1,
            grid=(steps * len(firsts),),
            in_specs=[pl.BlockSpec((rows, depth), lambda i, c: (0, 0))] * len(xs)
            + [pl.BlockSpec((depth, tile), column)],
            out_specs=pl.BlockSpec((rows * len(xs), tile), lambda i, c: (0, i)),
        ),
        compiler_params=params(limit),
        cost_estimate=cost(
            2 * rows * len(xs) * depth * WIDTH * len(firsts),
            2 * depth * (rows * len(xs) + WIDTH * len(firsts)),
        ),
        name="project_in",
    )(core, *xs, w)


def sweep_kernel(first, ks, chips, left_at, right_at, place_ref, pattern_ref, *refs):
    n_right = len(right_at)
    panel, rights = refs[: len(left_at)], refs[len(left_at) : len(left_at) + n_right]
    out_ref, left_ref, right_ref, acc_ref, left_sem, right_sem = refs[-6:]
    rows, cols = panel[0].shape[-2:]
    seg = rows // chips
    row_pos, col_pos = place_ref[0], place_ref[1]
    chip, core = lax.div(col_pos, CORES), lax.rem(col_pos, CORES)
    starts = [pl.multiple_of(lax.bitwise_xor(chip, k) * seg, seg) for k in ks]
    if len(ks) == chips:
        starts = [n * seg for n in range(chips)]

    def right_copy(i):
        xor, offset = right_at[i]
        slot = lax.bitwise_xor(lax.bitwise_xor(row_pos, chip), xor)
        target = right_ref.at[slot, pl.ds(offset, rights[i].shape[0]), :]
        return pltpu.make_async_copy(rights[i], target, right_sem.at[i])

    def left_copies(k):
        for ref, (j, index) in zip(panel, left_at, strict=True):
            if j // CORES != k:
                continue
            block = ref if index is None else ref.at[index]
            at = pl.multiple_of(lax.bitwise_xor(core, j % CORES) * cols, cols)
            for n, start in enumerate(starts):
                yield pltpu.make_async_copy(
                    block.at[pl.ds(start, seg), :],
                    left_ref.at[k, pl.ds(n * seg, seg), pl.ds(at, cols)],
                    left_sem.at[k, j % CORES * len(ks) + n],
                )

    for j in range(n_right):
        right_copy(j).start()
    for k in range(chips):
        for copy in left_copies(k):
            copy.start()
    for j in range(n_right):
        right_copy(j).wait()
    for k in range(chips):
        for copy in left_copies(k):
            copy.wait()
        product = jnp.dot(
            left_ref[k], right_ref[k], preferred_element_type=F32
        )
        if k == 0:
            acc_ref[...] = product
        elif k < chips - 1:
            acc_ref[...] += product
    product = product + acc_ref[...]
    own = left_ref[0, :, pl.ds(pl.multiple_of(core * cols, cols), cols)].astype(F32)
    total = 0.1275 * own + (0.85 * 0.1275 if first else 0.85) * product
    diagonal = lax.broadcasted_iota(jnp.int32, (seg, cols), 1) - lax.broadcasted_iota(
        jnp.int32, (seg, cols), 0
    )
    lane_block = lax.broadcasted_iota(jnp.int32, (1, cols), 1) // BLK
    for n, start in enumerate(starts):
        at = slice(n * seg, (n + 1) * seg)
        part = total[at, :]
        if not first:
            here = diagonal == row_pos * rows + start - col_pos * cols
            part = jnp.where(here, part + 0.15, part)
        size = math.gcd(seg, BLK)
        for i in range(seg // size):
            keep = jnp.zeros((1, cols), F32)
            for b in range(cols // BLK):
                kept = pattern_ref[b, lax.div(start + i * size, BLK)] > 0
                keep = jnp.where(lane_block == b, jnp.where(kept, 1.0, 0.0), keep)
            piece = part[i * size : (i + 1) * size, :]
            out_ref[n * seg + i * size : n * seg + (i + 1) * size, :] = jnp.where(
                keep > 0, piece, 0.0
            ).astype(BF16)


def sweep(first, ks, place, pattern, panel, blocks, follows, limit=VMEM_LIMIT):
    rows, cols = panel[0][0].shape[-2:]
    chips = len(panel) // CORES
    n_rows = rows // chips * len(ks)
    depth = len(panel) * cols
    return pl.pallas_call(
        functools.partial(
            sweep_kernel,
            first,
            ks,
            chips,
            [at for _, *at in panel],
            [(j, at) for j, at, _ in blocks],
        ),
        out_shape=jax.ShapeDtypeStruct((n_rows, cols), BF16),
        in_specs=[SMEM, SMEM] + [HBM] * (len(panel) + len(blocks) + len(follows)),
        out_specs=VMEM,
        scratch_shapes=[
            pltpu.VMEM((chips, n_rows, CORES * cols), BF16),
            pltpu.VMEM((depth // rows, rows, cols), BF16),
            pltpu.VMEM((n_rows, cols), F32),
            pltpu.SemaphoreType.DMA((chips, CORES * len(ks))),
            pltpu.SemaphoreType.DMA((len(blocks),)),
        ],
        compiler_params=params(limit),
        cost_estimate=cost(2 * n_rows * depth * cols, 2 * (n_rows + rows) * depth),
        name="rank_sweep",
    )(place, pattern, *[x for x, *_ in panel], *[x for *_, x in blocks], *follows)


def split_heads(keys):
    lane = lax.broadcasted_iota(jnp.int32, keys.shape, 1)
    zero = jnp.zeros_like(keys)
    return jnp.concatenate(
        [jnp.where(lane < HDIM, keys, zero), jnp.where(lane >= HDIM, keys, zero)], axis=0
    )


def expo_kernel(own_ref, other_ref, q_ref, k_ref, out_ref, peak_ref, mask_ref):
    p = pl.program_id(0)
    rows, keys = q_ref.shape[0], k_ref.shape[0]
    block_rows, block_cols = rows // BLK, keys // BLK
    tile = BLK

    @pl.when(p == 0)
    def _():
        lane = lax.broadcasted_iota(jnp.int32, (BLK, LANES), 1)
        for i in range(block_rows):
            excluded = jnp.zeros((BLK, LANES), F32)
            for b in range(block_cols):
                ref, at = (own_ref, b) if b < block_cols // 2 else (other_ref, b - block_cols // 2)
                excluded = jnp.where(lane == b, jnp.where(ref[at, i] > 0, 0.0, -1e30), excluded)
            mask_ref[i * BLK : (i + 1) * BLK, :] = excluded.astype(BF16)
        peak_ref[...] = jnp.zeros_like(peak_ref)

    lane = lax.broadcasted_iota(jnp.int32, (2 * keys, LANES), 1)
    key = lax.broadcasted_iota(jnp.int32, (2 * keys, LANES), 0)
    block_of = jnp.where(key >= keys, key - keys, key) // BLK
    in_block = jnp.where(lane == block_of, 1.0, 0.0).astype(BF16)
    right = jnp.concatenate([split_heads(k_ref[...]), in_block], axis=1)
    peak_lane = lax.broadcasted_iota(jnp.int32, (tile, LANES), 1)
    for t in range(rows // tile):
        at = slice(t * tile, (t + 1) * tile)
        left = jnp.concatenate([q_ref[at, :], mask_ref[at, :]], axis=1)
        s = lax.dot_general(left, right, (((1,), (1,)), ((), ())), preferred_element_type=F32)
        peaks = peak_ref[at, :]
        for side in range(2):
            part = s[:, side * keys : (side + 1) * keys]
            peak = jnp.max(part, axis=1, keepdims=True)
            peaks = jnp.where(peak_lane == HDIM * side + p, peak, peaks)
            out_ref[0, at, side * keys : (side + 1) * keys] = jnp.exp(part - peak).astype(BF16)
        peak_ref[at, :] = peaks


def exponentials(own, other, queries, keys_values):
    rows, keys = queries.shape[0], keys_values.shape[0]
    work = rows * keys * 2 * PAIRS
    return pl.pallas_call(
        expo_kernel,
        out_shape=(
            jax.ShapeDtypeStruct((PAIRS, rows, 2 * keys), BF16),
            jax.ShapeDtypeStruct((rows, LANES), F32),
        ),
        grid=(PAIRS,),
        in_specs=[
            SMEM,
            SMEM,
            pl.BlockSpec((rows, LANES), lambda p: (0, p)),
            pl.BlockSpec((keys, LANES), lambda p: (0, p)),
        ],
        out_specs=(
            pl.BlockSpec((1, rows, 2 * keys), lambda p: (p, 0, 0)),
            pl.BlockSpec((rows, LANES), lambda p: (0, 0)),
        ),
        scratch_shapes=[pltpu.VMEM((rows, LANES), BF16)],
        compiler_params=params(28 * 2**20),
        cost_estimate=cost(512 * work, 2 * work, work),
        name="expo",
    )(own, other, queries, keys_values)


def weigh_kernel(
    root, ks, seg, place_ref, gain_ref, rate_ref, own_ref, other_ref, expo_ref, v_ref, peak_ref,
    *refs,
):
    out_refs, (e_ref, p_ref, ranks_ref, right_ref, sem) = refs[-5 - len(ks) : -5], refs[-5:]
    cols = own_ref.shape[1]
    keys = 2 * cols
    chip = lax.div(place_ref[1], CORES)
    first_head = lax.rem(place_ref[1], CORES) * 2 * PAIRS
    starts = [pl.multiple_of(lax.bitwise_xor(chip, k) * seg, seg) for k in ks]

    def copy(p, i):
        return pltpu.make_async_copy(
            expo_ref.at[p, pl.ds(starts[i], seg), :],
            e_ref.at[p, pl.ds(i * seg, seg), :],
            sem.at[p, i],
        )

    for p in range(PAIRS):
        for i in range(len(ks)):
            copy(p, i).start()
    for i in range(len(ks)):
        at = slice(i * seg, (i + 1) * seg)
        ranks_ref[at, :cols] = own_ref[at, :].astype(F32)
        ranks_ref[at, cols:] = other_ref[at, :].astype(F32)
    lane = lax.broadcasted_iota(jnp.int32, (keys, LANES), 1)
    zero = jnp.zeros((keys, LANES), BF16)
    right_ref[:keys, LANES:] = jnp.where(lane < HDIM, 1.0, 0.0).astype(BF16)
    right_ref[keys:, LANES:] = jnp.where(lane < HDIM, 0.0, 1.0).astype(BF16)
    out_lane = lax.broadcasted_iota(jnp.int32, (seg, LANES), 1)

    def pair(p, totals):
        lanes = pl.ds(pl.multiple_of(p * LANES, LANES), LANES)
        values = v_ref[:, lanes]
        right_ref[:keys, :LANES] = jnp.where(lane < HDIM, values, zero)
        right_ref[keys:, :LANES] = jnp.where(lane < HDIM, zero, values)
        for i in range(len(ks)):
            copy(p, i).wait()
        for i in range(len(ks)):
            rows_at = slice(i * seg, (i + 1) * seg)
            for half in range(2):
                ranks = ranks_ref[rows_at, half * cols : (half + 1) * cols]
                for side in range(2):
                    rate = rate_ref[first_head + 2 * p + side] * root
                    gain = gain_ref[first_head + 2 * p + side] * math.log2(math.e)
                    at = slice(side * keys + half * cols, side * keys + (half + 1) * cols)
                    weight = e_ref[p, rows_at, at].astype(F32) * jnp.exp2(
                        gain * jnp.tanh(rate * ranks)
                    )
                    p_ref[rows_at, at] = weight.astype(BF16)
        sums = jnp.dot(p_ref[...], right_ref[...], preferred_element_type=F32)
        now = []
        for i, out_ref in enumerate(out_refs):
            part = sums[i * seg : (i + 1) * seg, :]
            out_ref[:, lanes] = part[:, :LANES].astype(BF16)
            now.append(jnp.where(out_lane % HDIM == p, part[:, LANES:], totals[i]))
        return tuple(now)

    totals = lax.fori_loop(
        0, PAIRS, pair, tuple(jnp.zeros((seg, LANES), F32) for _ in ks)
    )
    for i, out_ref in enumerate(out_refs):
        extra = totals[i]
        rest = peak_ref[pl.ds(starts[i], seg), :]
        for n in range(1, 4):
            piece = rest.astype(BF16).astype(F32)
            rest = rest - piece
            here = (out_lane % HDIM >= n * STEP) & (out_lane % HDIM < n * STEP + PAIRS)
            extra = jnp.where(here, pltpu.roll(piece, n * STEP, 1), extra)
        out_ref[:, WIDTH:] = extra.astype(BF16)


def weigh(root, chips, ks, place, gain, rate, own, other, expo, values, peak, follows):
    n_rows, cols = own.shape
    seg = n_rows // len(ks)
    rows, keys = seg * chips, 2 * cols
    work = n_rows * keys * 2 * PAIRS
    return pl.pallas_call(
        functools.partial(weigh_kernel, root, ks, seg),
        out_shape=(jax.ShapeDtypeStruct((seg, WIDTH + LANES), BF16),) * len(ks),
        grid=(1,),
        in_specs=[
            SMEM,
            SMEM,
            SMEM,
            pl.BlockSpec((n_rows, cols), lambda i: (0, 0)),
            pl.BlockSpec((n_rows, cols), lambda i: (0, 0)),
            HBM,
            pl.BlockSpec((keys, WIDTH), lambda i: (0, 1)),
            pl.BlockSpec((rows, LANES), lambda i: (0, 0)),
            HBM,
        ],
        out_specs=(pl.BlockSpec((seg, WIDTH + LANES), lambda i: (0, 0)),) * len(ks),
        scratch_shapes=[
            pltpu.VMEM((PAIRS, n_rows, 2 * keys), BF16),
            pltpu.VMEM((n_rows, 2 * keys), BF16),
            pltpu.VMEM((n_rows, keys), F32),
            pltpu.VMEM((2 * keys, 2 * LANES), BF16),
            pltpu.SemaphoreType.DMA((PAIRS, len(ks))),
        ],
        compiler_params=params(28 * 2**20),
        cost_estimate=cost(512 * work, 2 * work, 2 * work),
        name="weigh",
    )(place, gain, rate, own, other, expo, values, peak, follows)


def divide_kernel(*refs):
    parts, out_ref = refs[:-1], refs[-1]
    extras = [part[:, WIDTH:].astype(F32) for part in parts]
    seg = extras[0].shape[0]
    peaks = [sum(pltpu.roll(x, LANES - n * STEP, 1) for n in range(1, 4)) for x in extras]
    largest = functools.reduce(jnp.maximum, peaks)
    weights = [jnp.exp(peak - largest) for peak in peaks]
    inverse = 1.0 / sum(w * x for w, x in zip(weights, extras, strict=True))
    scales = [w * inverse for w in weights]
    lane = lax.broadcasted_iota(jnp.int32, (seg, LANES), 1)
    for p in range(PAIRS):
        lanes = slice(p * LANES, (p + 1) * LANES)
        total = jnp.zeros((seg, LANES), F32)
        for part, scale in zip(parts, scales, strict=True):
            both = jnp.where(lane < HDIM, scale[:, p : p + 1], scale[:, HDIM + p : HDIM + p + 1])
            total += part[:, lanes].astype(F32) * both
        out_ref[:, lanes] = total.astype(BF16)


def divide(parts):
    seg = parts[0].shape[0]
    return pl.pallas_call(
        divide_kernel,
        out_shape=jax.ShapeDtypeStruct((seg, WIDTH), BF16),
        in_specs=[VMEM] * len(parts),
        out_specs=VMEM,
        compiler_params=params(SMALL_LIMIT),
        cost_estimate=cost(8 * seg * D, 8 * seg * D),
        name="divide",
    )(*parts)


def project_out_kernel(place_ref, own_ref, other_ref, *refs):
    n = len(refs) // 2
    core = lax.rem(place_ref[1], CORES)
    mine = pl.ds(pl.multiple_of(core * WIDTH, WIDTH), WIDTH)
    others = pl.ds(pl.multiple_of((1 - core) * WIDTH, WIDTH), WIDTH)
    for w_ref, out_ref in zip(refs[:n], refs[n:], strict=True):
        total = jnp.dot(own_ref[...], w_ref[mine, :], preferred_element_type=F32)
        total += jnp.dot(other_ref[...], w_ref[others, :], preferred_element_type=F32)
        out_ref[...] = total.astype(BF16)


def project_out(place, own, other, w_all):
    seg, (depth, width) = own.shape[0], w_all[0].shape
    chips = len(w_all)
    return pl.pallas_call(
        project_out_kernel,
        out_shape=(jax.ShapeDtypeStruct((seg, width), BF16),) * chips,
        in_specs=[SMEM] + [VMEM] * (2 + chips),
        out_specs=(VMEM,) * chips,
        compiler_params=params(SMALL_LIMIT),
        cost_estimate=cost(2 * seg * depth * width * chips, 2 * depth * width * chips),
        name="project_out",
    )(place, own, other, *w_all)


def assemble_kernel(place_ref, *refs):
    parts, out_ref = refs[:-1], refs[-1]
    chip = lax.div(place_ref[1], CORES)
    seg = parts[0].shape[0]
    for k, part in enumerate(parts):
        at = pl.multiple_of(lax.bitwise_xor(chip, k) * seg, seg)
        out_ref[pl.ds(at, seg), :] = part[...]


def assemble(place, parts):
    seg, width = parts[0].shape
    return pl.pallas_call(
        assemble_kernel,
        out_shape=jax.ShapeDtypeStruct((seg * len(parts), width), BF16),
        in_specs=[SMEM] + [VMEM] * len(parts),
        out_specs=VMEM,
        compiler_params=params(SMALL_LIMIT),
        name="assemble",
    )(place, *parts)


def shards(node_features, edge_weight, pattern, w_qkv, w_out, bias_gain, bias_rate):
    rows, cols = edge_weight.shape
    row_count, col_count = lax.axis_size("row"), lax.axis_size("col")
    row_pos, col_pos = lax.axis_index("row"), lax.axis_index("col")
    ratio = rows // cols
    chips = col_count // CORES
    root = math.sqrt(rows * row_count)
    place = jnp.stack([row_pos, col_pos]).astype(jnp.int32)
    core = (col_pos % CORES).astype(jnp.int32).reshape(1)
    pattern = pattern.T
    together = lax.optimization_barrier

    def along_col(value, j):
        return lax.ppermute(value, "col", xor_pairs(col_count, j))

    def along_row(value, j):
        return lax.ppermute(value, "row", xor_pairs(row_count, j))

    def from_rows(value):
        return [value] + [along_row(value, j) for j in range(1, row_count)]

    def spread(blocks, bits):
        new = dict(blocks)
        for k in range(chips - 1, 0, -1):
            if k.bit_count() == bits:
                low = k & -k
                new[k] = along_col(blocks[k ^ low], CORES * low)
        return new

    ring = [0, 1, 3, 2] if row_count == 4 else list(range(row_count))
    def place_of(r):
        return r ^ (r >> 1) if row_count == 4 else r

    steps_away = (
        (place_of(row_pos) - place_of(col_pos // ratio)) * (1 - 2 * (col_pos % CORES))
    ) % row_count

    def feature_step(value, s):
        pairs = []
        for c in range(col_count):
            way = 1 - 2 * (c % CORES)
            i = ring.index(c // ratio) + way * (s - 1)
            here, there = ring[i % row_count], ring[(i + way) % row_count]
            pairs.append((here * col_count + c, there * col_count + c))
        return lax.ppermute(value, ("row", "col"), pairs)

    adjacency = mask(pattern, edge_weight)
    adjacency, node_features = together((adjacency, node_features))
    blocks = spread({0: adjacency}, 1)
    other_pattern = along_col(pattern, 1)
    other_pattern, node_features = together((other_pattern, node_features))
    near = [1, 2] if row_count == 4 else list(range(1, row_count))
    columns = {j: along_row(adjacency, j) for j in near}
    queries = project_in(core, [node_features], w_qkv, [0], 1.0 / math.sqrt(HDIM))
    queries, node_features = together((queries, node_features))
    features = lax.dynamic_slice_in_dim(node_features, col_pos % ratio * cols, cols, 0)
    moved = [features, feature_step(features, 1)]
    queries, moved, columns, blocks = together((queries, moved, columns, blocks))

    order = sorted(blocks)
    swapped = along_col(jnp.stack([blocks[k] for k in order]), 1)
    far = []
    if row_count == 4:
        half = rows // 2
        far = [along_row(columns[2][:half], 1), along_row(columns[1][half:], 2)]
    moved.append(feature_step(moved[-1], 2))
    for bits in range(2, chips.bit_length()):
        blocks = spread(blocks, bits)
    moved, far, swapped, blocks = together((moved, far, swapped, blocks))
    for s in range(3, row_count):
        moved.append(feature_step(moved[-1], s))
    panel = [(x, CORES * k, None) for k, x in blocks.items()]
    panel += [(swapped, CORES * k + 1, i) for i, k in enumerate(order)]
    panel += [(along_col(x, 1), CORES * k + 1, None) for k, x in blocks.items() if k not in order]
    columns = [(0, 0, adjacency)] + [(j, 0, x) for j, x in columns.items()]
    columns += [(3, i * x.shape[0], x) for i, x in enumerate(far)]
    ranks = sweep(True, range(chips), place, pattern, panel, columns, [], 24 * 2**20)
    columns = [(j, 0, x) for j, x in enumerate(from_rows(ranks))]

    ranks, moved = together((ranks, moved))
    key_rows = features
    for s in range(1, row_count):
        key_rows = jnp.where(steps_away == s, moved[s], key_rows)
    keys_values = project_in(core, [key_rows, along_col(key_rows, 1)], w_qkv, [D, 2 * D], limit=28 * 2**20)
    keys_values, w_out = together((keys_values, w_out))
    w_all = spread({0: w_out}, 1)
    expo, peak = exponentials(pattern, other_pattern, queries, keys_values)
    w_all, peak = together((w_all, peak))
    for bits in range(2, chips.bit_length()):
        w_all = spread(w_all, bits)
    w_all = [w_all[k] for k in range(chips)]

    groups = [list(range(chips // 2, chips)), list(range(chips // 2))]
    ranks = [sweep(False, ks, place, pattern, panel, columns, [peak], 24 * 2**20) for ks in groups]
    others = [along_col(x, 1) for x in ranks]
    parts, follows = [None] * chips, ranks[1]
    for ks, own, other in zip(groups, ranks, others, strict=True):
        sums = weigh(
            root, chips, ks, place, bias_gain, bias_rate, own, other, expo, keys_values, peak,
            follows,
        )
        for k, part in zip(ks, sums, strict=True):
            parts[k] = part if k == 0 else along_col(part, CORES * k)
        follows = sums[0]
    attended = divide(parts)
    mixed = project_out(place, attended, along_col(attended, 1), w_all)
    mixed = [x if k == 0 else along_col(x, CORES * k) for k, x in enumerate(mixed)]
    return assemble(place, mixed)


def solution(mesh):
    in_specs = (P("row", None), P("row", "col"), P("row", "col"), P(), P(None, "col"), P(), P())
    out_specs = P("row", "col")
    return jax.shard_map(shards, mesh=mesh, in_specs=in_specs, out_specs=out_specs, check_vma=False)
```

```python
import functools
import math

import jax
import jax.numpy as jnp
from jax import lax
from jax.experimental import pallas as pl
from jax.experimental.pallas import tpu as pltpu
from jax.sharding import PartitionSpec as P

D = 1024
HEADS = 16
BLK = 128
HDIM = 64
CORES = 2
PAIRS = HEADS // 2 // CORES
WIDTH = D // CORES
EXTRA = 4 * PAIRS
LANES = 128
VMEM_LIMIT = 58 * 2**20
SMALL_LIMIT = 16 * 2**20

VMEM = pl.BlockSpec(memory_space=pltpu.VMEM)
SMEM = pl.BlockSpec(memory_space=pltpu.SMEM)
HBM = pl.BlockSpec(memory_space=pltpu.HBM)
BF16 = jnp.bfloat16
F32 = jnp.float32


def params(limit=VMEM_LIMIT):
    return pltpu.CompilerParams(vmem_limit_bytes=limit)


def cost(flops, nbytes, trans=0):
    return pl.CostEstimate(flops=int(flops), bytes_accessed=int(nbytes), transcendentals=int(trans))


def xor_pairs(n, j):
    return [(i, i ^ j) for i in range(n)]


def keep_tile(pattern_ref, first_row, block_rows):
    block_cols = pattern_ref.shape[0]
    tiles = []
    for i in range(block_rows):
        parts = [
            jnp.full((1, BLK), jnp.where(pattern_ref[b, first_row + i] > 0, 1.0, 0.0), F32)
            for b in range(block_cols)
        ]
        tiles.append(
            jnp.broadcast_to(jnp.concatenate(parts, axis=1), (BLK, block_cols * BLK))
        )
    return jnp.concatenate(tiles, axis=0)


def start_kernel(place_ref, pattern_ref, weight_ref, features_ref, out_ref, cut_ref, sem):
    cols = cut_ref.shape[0]
    ratio = features_ref.shape[0] // cols
    at = pl.multiple_of(lax.rem(place_ref[1], ratio) * cols, cols)
    copy = pltpu.make_async_copy(features_ref.at[pl.ds(at, cols), :], cut_ref, sem)
    copy.start()
    for i in range(out_ref.shape[0] // BLK):
        at = slice(i * BLK, (i + 1) * BLK)
        keep = keep_tile(pattern_ref, i, 1)
        out_ref[at, :] = jnp.where(keep > 0, weight_ref[at, :].astype(F32), 0.0).astype(BF16)
    copy.wait()


def start(place, pattern, weight, features):
    rows, cols = weight.shape
    return pl.pallas_call(
        start_kernel,
        out_shape=(
            jax.ShapeDtypeStruct((rows, cols), BF16),
            jax.ShapeDtypeStruct((cols, features.shape[1]), BF16),
        ),
        in_specs=[SMEM, SMEM, VMEM, HBM],
        out_specs=(VMEM, VMEM),
        scratch_shapes=[pltpu.SemaphoreType.DMA],
        compiler_params=params(),
        cost_estimate=cost(rows * cols, 4 * rows * cols),
        name="start",
    )(place, pattern, weight, features)


def project_in_kernel(scale, place_ref, *refs):
    xs, (w_ref, out_ref) = refs[:-2], refs[-2:]
    rows = xs[0].shape[0]
    for i, x_ref in enumerate(xs):
        out = jnp.dot(x_ref[...], w_ref[...], preferred_element_type=F32).astype(BF16)
        if scale is not None:
            out = out * jnp.asarray(scale, BF16)
        out_ref[i * rows : (i + 1) * rows, :] = out


def project_in(core, xs, w, firsts, scale=None, tile=256, limit=VMEM_LIMIT):
    rows, depth = xs[0].shape
    steps = WIDTH // tile

    def column(i, core_ref):
        first = firsts[0] // tile
        for n, start in enumerate(firsts[1:], 1):
            first = jnp.where(i >= n * steps, start // tile, first)
        return 0, first + core_ref[0] * steps + lax.rem(i, steps)

    return pl.pallas_call(
        functools.partial(project_in_kernel, scale),
        out_shape=jax.ShapeDtypeStruct((rows * len(xs), WIDTH * len(firsts)), BF16),
        grid_spec=pltpu.PrefetchScalarGridSpec(
            num_scalar_prefetch=1,
            grid=(steps * len(firsts),),
            in_specs=[pl.BlockSpec((rows, depth), lambda i, c: (0, 0))] * len(xs)
            + [pl.BlockSpec((depth, tile), column)],
            out_specs=pl.BlockSpec((rows * len(xs), tile), lambda i, c: (0, i)),
        ),
        compiler_params=params(limit),
        cost_estimate=cost(
            2 * rows * len(xs) * depth * WIDTH * len(firsts),
            2 * depth * (rows * len(xs) + WIDTH * len(firsts)),
        ),
        name="project_in",
    )(core, *xs, w)


def sweep_kernel(first, ks, chips, left_at, right_at, place_ref, pattern_ref, *refs):
    n_right = len(right_at)
    panel, rights = refs[: len(left_at)], refs[len(left_at) : len(left_at) + n_right]
    out_ref, left_ref, right_ref, acc_ref, left_sem, right_sem = refs[-6:]
    rows, cols = panel[0].shape[-2:]
    seg = rows // chips
    row_pos, col_pos = place_ref[0], place_ref[1]
    chip, core = lax.div(col_pos, CORES), lax.rem(col_pos, CORES)
    starts = [pl.multiple_of(lax.bitwise_xor(chip, k) * seg, seg) for k in ks]
    if len(ks) == chips:
        starts, seg = [0], rows

    def right_copy(i):
        xor, offset = right_at[i]
        slot = lax.bitwise_xor(lax.bitwise_xor(row_pos, chip), xor)
        target = right_ref.at[slot, pl.ds(offset, rights[i].shape[0]), :]
        return pltpu.make_async_copy(rights[i], target, right_sem.at[i])

    def left_copies(k):
        for ref, (j, index) in zip(panel, left_at, strict=True):
            if j // CORES != k:
                continue
            block = ref if index is None else ref.at[index]
            at = pl.multiple_of(lax.bitwise_xor(core, j % CORES) * cols, cols)
            for n, start in enumerate(starts):
                yield pltpu.make_async_copy(
                    block.at[pl.ds(start, seg), :],
                    left_ref.at[k, pl.ds(n * seg, seg), pl.ds(at, cols)],
                    left_sem.at[k, j % CORES * len(starts) + n],
                )

    for j in range(n_right):
        right_copy(j).start()
    for k in range(chips):
        for copy in left_copies(k):
            copy.start()
    for j in range(n_right):
        right_copy(j).wait()
    for k in range(chips):
        for copy in left_copies(k):
            copy.wait()
        product = jnp.dot(left_ref[k], right_ref[k], preferred_element_type=F32)
        if k == 0:
            acc_ref[...] = product
        elif k < chips - 1:
            acc_ref[...] += product
    product = product + acc_ref[...]
    own = left_ref[0, :, pl.ds(pl.multiple_of(core * cols, cols), cols)].astype(F32)
    total = 0.1275 * own + (0.85 * 0.1275 if first else 0.85) * product
    diagonal = lax.broadcasted_iota(jnp.int32, (seg, cols), 1) - lax.broadcasted_iota(
        jnp.int32, (seg, cols), 0
    )
    lane_block = lax.broadcasted_iota(jnp.int32, (1, cols), 1) // BLK
    for n, start in enumerate(starts):
        at = slice(n * seg, (n + 1) * seg)
        part = total[at, :]
        if not first:
            here = diagonal == row_pos * rows + start - col_pos * cols
            part = jnp.where(here, part + 0.15, part)
        size = math.gcd(seg, BLK)
        for i in range(seg // size):
            keep = jnp.zeros((1, cols), F32)
            for b in range(cols // BLK):
                kept = pattern_ref[b, lax.div(start + i * size, BLK)] > 0
                keep = jnp.where(lane_block == b, jnp.where(kept, 1.0, 0.0), keep)
            piece = part[i * size : (i + 1) * size, :]
            out_ref[n * seg + i * size : n * seg + (i + 1) * size, :] = jnp.where(
                keep > 0, piece, 0.0
            ).astype(BF16)


def sweep(first, ks, place, pattern, panel, blocks, follows, limit=VMEM_LIMIT):
    rows, cols = panel[0][0].shape[-2:]
    chips = len(panel) // CORES
    n_rows = rows // chips * len(ks)
    depth = len(panel) * cols
    return pl.pallas_call(
        functools.partial(
            sweep_kernel,
            first,
            ks,
            chips,
            [at for _, *at in panel],
            [(j, at) for j, at, _ in blocks],
        ),
        out_shape=jax.ShapeDtypeStruct((n_rows, cols), BF16),
        in_specs=[SMEM, SMEM] + [HBM] * (len(panel) + len(blocks) + len(follows)),
        out_specs=VMEM,
        scratch_shapes=[
            pltpu.VMEM((chips, n_rows, CORES * cols), BF16),
            pltpu.VMEM((depth // rows, rows, cols), BF16),
            pltpu.VMEM((n_rows, cols), F32),
            pltpu.SemaphoreType.DMA((chips, CORES * len(ks))),
            pltpu.SemaphoreType.DMA((len(blocks),)),
        ],
        compiler_params=params(limit),
        cost_estimate=cost(2 * n_rows * depth * cols, 2 * (n_rows + rows) * depth),
        name="rank_sweep",
    )(place, pattern, *[x for x, *_ in panel], *[x for *_, x in blocks], *follows)


def split_heads(keys):
    lane = lax.broadcasted_iota(jnp.int32, keys.shape, 1)
    zero = jnp.zeros_like(keys)
    return jnp.concatenate(
        [jnp.where(lane < HDIM, keys, zero), jnp.where(lane >= HDIM, keys, zero)], axis=0
    )


def expo_kernel(own_ref, other_ref, q_ref, k_ref, out_ref, peak_ref, mask_ref):
    p = pl.program_id(0)
    rows, keys = q_ref.shape[0], k_ref.shape[0]
    block_rows, block_cols = rows // BLK, keys // BLK
    tile = BLK

    @pl.when(p == 0)
    def _():
        lane = lax.broadcasted_iota(jnp.int32, (BLK, LANES), 1)
        for i in range(block_rows):
            excluded = jnp.zeros((BLK, LANES), F32)
            for b in range(block_cols):
                ref, at = (own_ref, b) if b < block_cols // 2 else (other_ref, b - block_cols // 2)
                excluded = jnp.where(lane == b, jnp.where(ref[at, i] > 0, 0.0, -1e30), excluded)
            mask_ref[i * BLK : (i + 1) * BLK, :] = excluded.astype(BF16)
        peak_ref[...] = jnp.zeros_like(peak_ref)

    lane = lax.broadcasted_iota(jnp.int32, (2 * keys, LANES), 1)
    key = lax.broadcasted_iota(jnp.int32, (2 * keys, LANES), 0)
    block_of = jnp.where(key >= keys, key - keys, key) // BLK
    in_block = jnp.where(lane == block_of, 1.0, 0.0).astype(BF16)
    right = jnp.concatenate([split_heads(k_ref[...]), in_block], axis=1)
    peak_lane = lax.broadcasted_iota(jnp.int32, (tile, LANES), 1)
    for t in range(rows // tile):
        at = slice(t * tile, (t + 1) * tile)
        left = jnp.concatenate([q_ref[at, :], mask_ref[at, :]], axis=1)
        s = lax.dot_general(left, right, (((1,), (1,)), ((), ())), preferred_element_type=F32)
        peaks = peak_ref[at, :]
        for side in range(2):
            part = s[:, side * keys : (side + 1) * keys]
            peak = jnp.max(part, axis=1, keepdims=True)
            peaks = jnp.where(peak_lane == HDIM * side + p, peak, peaks)
            out_ref[0, at, side * keys : (side + 1) * keys] = jnp.exp(part - peak).astype(BF16)
        peak_ref[at, :] = peaks


def exponentials(own, other, queries, keys_values):
    rows, keys = queries.shape[0], keys_values.shape[0]
    work = rows * keys * 2 * PAIRS
    return pl.pallas_call(
        expo_kernel,
        out_shape=(
            jax.ShapeDtypeStruct((PAIRS, rows, 2 * keys), BF16),
            jax.ShapeDtypeStruct((rows, LANES), F32),
        ),
        grid=(PAIRS,),
        in_specs=[
            SMEM,
            SMEM,
            pl.BlockSpec((rows, LANES), lambda p: (0, p)),
            pl.BlockSpec((keys, LANES), lambda p: (0, p)),
        ],
        out_specs=(
            pl.BlockSpec((1, rows, 2 * keys), lambda p: (p, 0, 0)),
            pl.BlockSpec((rows, LANES), lambda p: (0, 0)),
        ),
        scratch_shapes=[pltpu.VMEM((rows, LANES), BF16)],
        compiler_params=params(28 * 2**20),
        cost_estimate=cost(512 * work, 2 * work, work),
        name="expo",
    )(own, other, queries, keys_values)


def weigh_kernel(
    root, ks, seg, place_ref, gain_ref, rate_ref, own_ref, other_ref, expo_ref, v_ref, peak_ref,
    *refs,
):
    out_refs, (e_ref, p_ref, ranks_ref, right_ref, sem) = refs[-5 - len(ks) : -5], refs[-5:]
    cols = own_ref.shape[1]
    keys = 2 * cols
    chip = lax.div(place_ref[1], CORES)
    first_head = lax.rem(place_ref[1], CORES) * 2 * PAIRS
    starts = [pl.multiple_of(lax.bitwise_xor(chip, k) * seg, seg) for k in ks]

    def copy(p, i):
        return pltpu.make_async_copy(
            expo_ref.at[p, pl.ds(starts[i], seg), :],
            e_ref.at[p, pl.ds(i * seg, seg), :],
            sem.at[p, i],
        )

    for p in range(PAIRS):
        for i in range(len(ks)):
            copy(p, i).start()
    for i in range(len(ks)):
        at = slice(i * seg, (i + 1) * seg)
        ranks_ref[at, :cols] = own_ref[at, :].astype(F32)
        ranks_ref[at, cols:] = other_ref[at, :].astype(F32)
    lane = lax.broadcasted_iota(jnp.int32, (keys, LANES), 1)
    zero = jnp.zeros((keys, LANES), BF16)
    right_ref[:keys, LANES:] = jnp.where(lane < HDIM, 1.0, 0.0).astype(BF16)
    right_ref[keys:, LANES:] = jnp.where(lane < HDIM, 0.0, 1.0).astype(BF16)
    out_lane = lax.broadcasted_iota(jnp.int32, (seg, LANES), 1)

    def pair(p, totals):
        lanes = pl.ds(pl.multiple_of(p * LANES, LANES), LANES)
        values = v_ref[:, lanes]
        right_ref[:keys, :LANES] = jnp.where(lane < HDIM, values, zero)
        right_ref[keys:, :LANES] = jnp.where(lane < HDIM, zero, values)
        for i in range(len(ks)):
            copy(p, i).wait()
        for i in range(len(ks)):
            rows_at = slice(i * seg, (i + 1) * seg)
            for half in range(2):
                ranks = ranks_ref[rows_at, half * cols : (half + 1) * cols]
                for side in range(2):
                    rate = rate_ref[first_head + 2 * p + side] * root
                    gain = gain_ref[first_head + 2 * p + side] * math.log2(math.e)
                    at = slice(side * keys + half * cols, side * keys + (half + 1) * cols)
                    weight = e_ref[p, rows_at, at].astype(F32) * jnp.exp2(
                        gain * jnp.tanh(rate * ranks)
                    )
                    p_ref[rows_at, at] = weight.astype(BF16)
        sums = jnp.dot(p_ref[...], right_ref[...], preferred_element_type=F32)
        now = []
        for i, out_ref in enumerate(out_refs):
            part = sums[i * seg : (i + 1) * seg, :]
            out_ref[:seg, lanes] = part[:, :LANES].astype(BF16)
            now.append(jnp.where(out_lane % HDIM == p, part[:, LANES:], totals[i]))
        return tuple(now)

    totals = lax.fori_loop(
        0, PAIRS, pair, tuple(jnp.zeros((seg, LANES), F32) for _ in ks)
    )
    half = WIDTH // 2
    for i, out_ref in enumerate(out_refs):
        extra = totals[i]
        rest = peak_ref[pl.ds(starts[i], seg), :]
        for n in range(1, 4):
            piece = rest.astype(BF16).astype(F32)
            rest = rest - piece
            here = (out_lane % HDIM >= n * PAIRS) & (out_lane % HDIM < (n + 1) * PAIRS)
            extra = jnp.where(here, pltpu.roll(piece, n * PAIRS, 1), extra)
        extra = jnp.concatenate([extra, jnp.zeros((half - seg, LANES), F32)], axis=0).T
        for side in range(2):
            out_ref[seg:, side * half : (side + 1) * half] = extra[
                side * HDIM : side * HDIM + EXTRA
            ].astype(BF16)


def weigh(root, chips, ks, place, gain, rate, own, other, expo, values, peak, follows):
    n_rows, cols = own.shape
    seg = n_rows // len(ks)
    rows, keys = seg * chips, 2 * cols
    work = n_rows * keys * 2 * PAIRS
    return pl.pallas_call(
        functools.partial(weigh_kernel, root, ks, seg),
        out_shape=(jax.ShapeDtypeStruct((seg + EXTRA, WIDTH), BF16),) * len(ks),
        grid=(1,),
        in_specs=[
            SMEM,
            SMEM,
            SMEM,
            pl.BlockSpec((n_rows, cols), lambda i: (0, 0)),
            pl.BlockSpec((n_rows, cols), lambda i: (0, 0)),
            HBM,
            pl.BlockSpec((keys, WIDTH), lambda i: (0, 1)),
            pl.BlockSpec((rows, LANES), lambda i: (0, 0)),
            HBM,
        ],
        out_specs=(pl.BlockSpec((seg + EXTRA, WIDTH), lambda i: (0, 0)),) * len(ks),
        scratch_shapes=[
            pltpu.VMEM((PAIRS, n_rows, 2 * keys), BF16),
            pltpu.VMEM((n_rows, 2 * keys), BF16),
            pltpu.VMEM((n_rows, keys), F32),
            pltpu.VMEM((2 * keys, 2 * LANES), BF16),
            pltpu.SemaphoreType.DMA((PAIRS, len(ks))),
        ],
        compiler_params=params(28 * 2**20),
        cost_estimate=cost(512 * work, 2 * work, 2 * work),
        name="weigh",
    )(place, gain, rate, own, other, expo, values, peak, follows)


def divide_kernel(*refs):
    parts, out_ref = refs[:-1], refs[-1]
    seg, half = out_ref.shape[0], WIDTH // 2
    lane = lax.broadcasted_iota(jnp.int32, (seg, LANES), 1)
    fit = LANES // (2 * EXTRA)
    totals, peaks, largest = [], [], None
    for first in range(0, len(parts), fit):
        group = parts[first : first + fit]
        extra = [
            part[seg:, side * half : (side + 1) * half].astype(F32)
            for part in group
            for side in range(2)
        ]
        spare = LANES - EXTRA * len(extra)
        if spare:
            extra.append(jnp.zeros((spare, half), F32))
        extra = jnp.concatenate(extra, axis=0).T[:seg]
        totals.append(extra)
        peak = sum(pltpu.roll(extra, LANES - n * PAIRS, 1) for n in range(1, 4))
        if spare:
            peak = jnp.where(lane < LANES - spare, peak, -jnp.inf)
        peaks.append(peak)
        largest = peak if largest is None else jnp.maximum(largest, peak)

    def over_parts(value, combine):
        step = 2 * EXTRA
        while step < LANES:
            value = combine(value, pltpu.roll(value, step, 1))
            step *= 2
        return value

    largest = over_parts(largest, jnp.maximum)
    weights = [jnp.exp(peak - largest) for peak in peaks]
    inverse = 1.0 / over_parts(
        sum(w * x for w, x in zip(weights, totals, strict=True)), lambda x, y: x + y
    )
    scales = [w * inverse for w in weights]
    for p in range(PAIRS):
        lanes = slice(p * LANES, (p + 1) * LANES)
        total = jnp.zeros((seg, LANES), F32)
        for i, part in enumerate(parts):
            at = i % fit * 2 * EXTRA + p
            scale = scales[i // fit]
            both = jnp.where(
                lane < HDIM, scale[:, at : at + 1], scale[:, at + EXTRA : at + EXTRA + 1]
            )
            total += part[:seg, lanes].astype(F32) * both
        out_ref[:, lanes] = total.astype(BF16)


def divide(parts):
    seg = parts[0].shape[0] - EXTRA
    return pl.pallas_call(
        divide_kernel,
        out_shape=jax.ShapeDtypeStruct((seg, WIDTH), BF16),
        in_specs=[VMEM] * len(parts),
        out_specs=VMEM,
        compiler_params=params(SMALL_LIMIT),
        cost_estimate=cost(8 * seg * D, 8 * seg * D),
        name="divide",
    )(*parts)


def project_out_kernel(place_ref, own_ref, other_ref, *refs):
    n = len(refs) // 2
    core = lax.rem(place_ref[1], CORES)
    mine = pl.ds(pl.multiple_of(core * WIDTH, WIDTH), WIDTH)
    others = pl.ds(pl.multiple_of((1 - core) * WIDTH, WIDTH), WIDTH)
    for w_ref, out_ref in zip(refs[:n], refs[n:], strict=True):
        total = jnp.dot(own_ref[...], w_ref[mine, :], preferred_element_type=F32)
        total += jnp.dot(other_ref[...], w_ref[others, :], preferred_element_type=F32)
        out_ref[...] = total.astype(BF16)


def project_out(place, own, other, w_all):
    seg, (depth, width) = own.shape[0], w_all[0].shape
    chips = len(w_all)
    return pl.pallas_call(
        project_out_kernel,
        out_shape=(jax.ShapeDtypeStruct((seg, width), BF16),) * chips,
        in_specs=[SMEM] + [VMEM] * (2 + chips),
        out_specs=(VMEM,) * chips,
        compiler_params=params(SMALL_LIMIT),
        cost_estimate=cost(2 * seg * depth * width * chips, 2 * depth * width * chips),
        name="project_out",
    )(place, own, other, *w_all)


def assemble_kernel(place_ref, *refs):
    parts, out_ref = refs[:-1], refs[-1]
    chip = lax.div(place_ref[1], CORES)
    seg = parts[0].shape[0]
    for k, part in enumerate(parts):
        at = pl.multiple_of(lax.bitwise_xor(chip, k) * seg, seg)
        out_ref[pl.ds(at, seg), :] = part[...]


def assemble(place, parts):
    seg, width = parts[0].shape
    return pl.pallas_call(
        assemble_kernel,
        out_shape=jax.ShapeDtypeStruct((seg * len(parts), width), BF16),
        in_specs=[SMEM] + [VMEM] * len(parts),
        out_specs=VMEM,
        compiler_params=params(SMALL_LIMIT),
        name="assemble",
    )(place, *parts)


def shards(node_features, edge_weight, pattern, w_qkv, w_out, bias_gain, bias_rate):
    rows, cols = edge_weight.shape
    row_count, col_count = lax.axis_size("row"), lax.axis_size("col")
    row_pos, col_pos = lax.axis_index("row"), lax.axis_index("col")
    ratio = rows // cols
    chips = col_count // CORES
    root = math.sqrt(rows * row_count)
    place = jnp.stack([row_pos, col_pos]).astype(jnp.int32)
    core = (col_pos % CORES).astype(jnp.int32).reshape(1)
    pattern = pattern.T
    together = lax.optimization_barrier

    def along_col(value, j):
        return lax.ppermute(value, "col", xor_pairs(col_count, j))

    def along_row(value, j):
        return lax.ppermute(value, "row", xor_pairs(row_count, j))

    def from_rows(value):
        return [value] + [along_row(value, j) for j in range(1, row_count)]

    def spread(blocks, bits):
        new = dict(blocks)
        for k in range(chips - 1, 0, -1):
            if k.bit_count() == bits:
                low = k & -k
                new[k] = along_col(blocks[k ^ low], CORES * low)
        return new

    ring = [0, 1, 3, 2] if row_count == 4 else list(range(row_count))
    def place_of(r):
        return r ^ (r >> 1) if row_count == 4 else r

    steps_away = (
        (place_of(row_pos) - place_of(col_pos // ratio)) * (1 - 2 * (col_pos % CORES))
    ) % row_count

    def feature_step(value, s):
        pairs = []
        for c in range(col_count):
            way = 1 - 2 * (c % CORES)
            i = ring.index(c // ratio) + way * (s - 1)
            here, there = ring[i % row_count], ring[(i + way) % row_count]
            pairs.append((here * col_count + c, there * col_count + c))
        return lax.ppermute(value, ("row", "col"), pairs)

    adjacency, features = start(place, pattern, edge_weight, node_features)
    blocks = spread({0: adjacency}, 1)
    near = [1, 2] if row_count == 4 else list(range(1, row_count))
    columns = {j: along_row(adjacency, j) for j in near}
    other_pattern = along_col(pattern, 1)
    queries = project_in(core, [node_features], w_qkv, [0], 1.0 / math.sqrt(HDIM))
    moved = [features, feature_step(features, 1)]
    raw_columns = columns
    queries, moved, columns, blocks = together((queries, moved, columns, blocks))

    order = sorted(blocks)
    swapped = along_col(jnp.stack([blocks[k] for k in order]), 1)
    far = []
    if row_count == 4:
        half = rows // 2
        far = [along_row(columns[2][:half], 1), along_row(columns[1][half:], 2)]
    moved.append(feature_step(moved[-1], 2))
    for bits in range(2, chips.bit_length()):
        blocks = spread(blocks, bits)
    raw_far = far
    far, swapped, blocks = together((far, swapped, blocks))
    for s in range(3, row_count):
        moved.append(feature_step(moved[-1], s))
    panel = [(x, CORES * k, None) for k, x in blocks.items()]
    panel += [(swapped, CORES * k + 1, i) for i, k in enumerate(order)]
    panel += [(along_col(x, 1), CORES * k + 1, None) for k, x in blocks.items() if k not in order]
    columns = [(0, 0, adjacency)] + [(j, 0, x) for j, x in raw_columns.items()]
    columns += [(3, i * x.shape[0], x) for i, x in enumerate(raw_far)]
    ranks = sweep(True, range(chips), place, pattern, panel, columns, [], 24 * 2**20)
    columns = [(j, 0, x) for j, x in enumerate(from_rows(ranks))]

    ranks, moved = together((ranks, moved))
    key_rows = features
    for s in range(1, row_count):
        key_rows = jnp.where(steps_away == s, moved[s], key_rows)
    keys_values = project_in(core, [key_rows, along_col(key_rows, 1)], w_qkv, [D, 2 * D], limit=28 * 2**20)
    keys_values, w_out = together((keys_values, w_out))
    w_all = spread({0: w_out}, 1)
    expo, peak = exponentials(pattern, other_pattern, queries, keys_values)
    w_all, peak = together((w_all, peak))
    for bits in range(2, chips.bit_length()):
        w_all = spread(w_all, bits)
    w_all = [w_all[k] for k in range(chips)]

    groups = [list(range(chips // 2, chips)), list(range(chips // 2))]
    ranks = [sweep(False, ks, place, pattern, panel, columns, [peak], 24 * 2**20) for ks in groups]
    others = [along_col(x, 1) for x in ranks]
    parts, follows = [None] * chips, ranks[1]
    for ks, own, other in zip(groups, ranks, others, strict=True):
        sums = weigh(
            root, chips, ks, place, bias_gain, bias_rate, own, other, expo, keys_values, peak,
            follows,
        )
        for k, part in zip(ks, sums, strict=True):
            parts[k] = part if k == 0 else along_col(part, CORES * k)
        follows = sums[0]
    attended = divide(parts)
    mixed = project_out(place, attended, along_col(attended, 1), w_all)
    mixed = [x if k == 0 else along_col(x, CORES * k) for k, x in enumerate(mixed)]
    return assemble(place, mixed)


def solution(mesh):
    in_specs = (P("row", None), P("row", "col"), P("row", "col"), P(), P(None, "col"), P(), P())
    out_specs = P("row", "col")
    return jax.shard_map(shards, mesh=mesh, in_specs=in_specs, out_specs=out_specs, check_vma=False)
```

```python
import functools
import math

import jax
import jax.numpy as jnp
from jax import lax
from jax.experimental import pallas as pl
from jax.experimental.pallas import tpu as pltpu
from jax.sharding import PartitionSpec as P

D = 1024
HEADS = 16
BLK = 128
HDIM = 64
CORES = 2
PAIRS = HEADS // 2 // CORES
WIDTH = D // CORES
EXTRA = 4 * PAIRS
LANES = 128
VMEM_LIMIT = 58 * 2**20
SMALL_LIMIT = 16 * 2**20

VMEM = pl.BlockSpec(memory_space=pltpu.VMEM)
SMEM = pl.BlockSpec(memory_space=pltpu.SMEM)
HBM = pl.BlockSpec(memory_space=pltpu.HBM)
BF16 = jnp.bfloat16
F32 = jnp.float32


def params(limit=VMEM_LIMIT):
    return pltpu.CompilerParams(vmem_limit_bytes=limit)


def cost(flops, nbytes, trans=0):
    return pl.CostEstimate(flops=int(flops), bytes_accessed=int(nbytes), transcendentals=int(trans))


def xor_pairs(n, j):
    return [(i, i ^ j) for i in range(n)]


def keep_tile(pattern_ref, first_row, block_rows):
    block_cols = pattern_ref.shape[0]
    tiles = []
    for i in range(block_rows):
        parts = [
            jnp.full((1, BLK), jnp.where(pattern_ref[b, first_row + i] > 0, 1.0, 0.0), F32)
            for b in range(block_cols)
        ]
        tiles.append(
            jnp.broadcast_to(jnp.concatenate(parts, axis=1), (BLK, block_cols * BLK))
        )
    return jnp.concatenate(tiles, axis=0)


def start_kernel(place_ref, pattern_ref, weight_ref, features_ref, out_ref, cut_ref, sem):
    cols = cut_ref.shape[0]
    ratio = features_ref.shape[0] // cols
    at = pl.multiple_of(lax.rem(place_ref[1], ratio) * cols, cols)
    copy = pltpu.make_async_copy(features_ref.at[pl.ds(at, cols), :], cut_ref, sem)
    copy.start()
    for i in range(out_ref.shape[0] // BLK):
        at = slice(i * BLK, (i + 1) * BLK)
        keep = keep_tile(pattern_ref, i, 1)
        out_ref[at, :] = jnp.where(keep > 0, weight_ref[at, :].astype(F32), 0.0).astype(BF16)
    copy.wait()


def start(place, pattern, weight, features):
    rows, cols = weight.shape
    return pl.pallas_call(
        start_kernel,
        out_shape=(
            jax.ShapeDtypeStruct((rows, cols), BF16),
            jax.ShapeDtypeStruct((cols, features.shape[1]), BF16),
        ),
        in_specs=[SMEM, SMEM, VMEM, HBM],
        out_specs=(VMEM, VMEM),
        scratch_shapes=[pltpu.SemaphoreType.DMA],
        compiler_params=params(),
        cost_estimate=cost(rows * cols, 4 * rows * cols),
        name="start",
    )(place, pattern, weight, features)


def project_in_kernel(scale, place_ref, *refs):
    xs, (w_ref, out_ref) = refs[:-2], refs[-2:]
    rows = xs[0].shape[0]
    for i, x_ref in enumerate(xs):
        out = jnp.dot(x_ref[...], w_ref[...], preferred_element_type=F32).astype(BF16)
        if scale is not None:
            out = out * jnp.asarray(scale, BF16)
        out_ref[i * rows : (i + 1) * rows, :] = out


def project_in(core, xs, w, firsts, scale=None, tile=256, limit=VMEM_LIMIT):
    rows, depth = xs[0].shape
    steps = WIDTH // tile

    def column(i, core_ref):
        first = firsts[0] // tile
        for n, start in enumerate(firsts[1:], 1):
            first = jnp.where(i >= n * steps, start // tile, first)
        return 0, first + core_ref[0] * steps + lax.rem(i, steps)

    return pl.pallas_call(
        functools.partial(project_in_kernel, scale),
        out_shape=jax.ShapeDtypeStruct((rows * len(xs), WIDTH * len(firsts)), BF16),
        grid_spec=pltpu.PrefetchScalarGridSpec(
            num_scalar_prefetch=1,
            grid=(steps * len(firsts),),
            in_specs=[pl.BlockSpec((rows, depth), lambda i, c: (0, 0))] * len(xs)
            + [pl.BlockSpec((depth, tile), column)],
            out_specs=pl.BlockSpec((rows * len(xs), tile), lambda i, c: (0, i)),
        ),
        compiler_params=params(limit),
        cost_estimate=cost(
            2 * rows * len(xs) * depth * WIDTH * len(firsts),
            2 * depth * (rows * len(xs) + WIDTH * len(firsts)),
        ),
        name="project_in",
    )(core, *xs, w)


def sweep_kernel(first, ks, chips, left_at, right_at, place_ref, pattern_ref, *refs):
    n_right = len(right_at)
    panel, rights = refs[: len(left_at)], refs[len(left_at) : len(left_at) + n_right]
    out_ref, left_ref, right_ref, acc_ref, left_sem, right_sem = refs[-6:]
    rows, cols = panel[0].shape[-2:]
    seg = rows // chips
    row_pos, col_pos = place_ref[0], place_ref[1]
    chip, core = lax.div(col_pos, CORES), lax.rem(col_pos, CORES)
    starts = [pl.multiple_of(lax.bitwise_xor(chip, k) * seg, seg) for k in ks]
    if len(ks) == chips:
        starts, seg = [0], rows

    part = min(ref.shape[0] for ref in rights)

    def right_copies(i, slot):
        xor, offset = right_at[i]
        for at in range(0, rights[i].shape[0], part):
            target = right_ref.at[slot, pl.ds(offset + at, part), :]
            source = rights[i].at[pl.ds(at, part), :]
            yield pltpu.make_async_copy(source, target, right_sem.at[slot, (offset + at) // part])

    def left_copies(k):
        for ref, (j, index) in zip(panel, left_at, strict=True):
            if j // CORES != k:
                continue
            block = ref if index is None else ref.at[index]
            at = pl.multiple_of(lax.bitwise_xor(core, j % CORES) * cols, cols)
            for n, start in enumerate(starts):
                yield pltpu.make_async_copy(
                    block.at[pl.ds(start, seg), :],
                    left_ref.at[k, pl.ds(n * seg, seg), pl.ds(at, cols)],
                    left_sem.at[k, j % CORES * len(starts) + n],
                )

    for k in range(chips):
        for copy in left_copies(k):
            copy.start()
        for xor in sorted({at[0] for at in right_at}):

            @pl.when(lax.bitwise_xor(row_pos, chip) == xor ^ k)
            def _():
                for i in range(n_right):
                    if right_at[i][0] == xor:
                        for copy in right_copies(i, k):
                            copy.start()

    for k in range(chips):
        for at in range(0, rows, part):
            half = right_ref.at[k, pl.ds(at, part), :]
            pltpu.make_async_copy(half, half, right_sem.at[k, at // part]).wait()
        for copy in left_copies(k):
            copy.wait()
        product = jnp.dot(left_ref[k], right_ref[k], preferred_element_type=F32)
        if k == 0:
            acc_ref[...] = product
        elif k < chips - 1:
            acc_ref[...] += product
    product = product + acc_ref[...]
    own = left_ref[0, :, pl.ds(pl.multiple_of(core * cols, cols), cols)].astype(F32)
    total = 0.1275 * own + (0.85 * 0.1275 if first else 0.85) * product
    diagonal = lax.broadcasted_iota(jnp.int32, (seg, cols), 1) - lax.broadcasted_iota(
        jnp.int32, (seg, cols), 0
    )
    lane_block = lax.broadcasted_iota(jnp.int32, (1, cols), 1) // BLK
    for n, start in enumerate(starts):
        at = slice(n * seg, (n + 1) * seg)
        part = total[at, :]
        if not first:
            here = diagonal == row_pos * rows + start - col_pos * cols
            part = jnp.where(here, part + 0.15, part)
        size = math.gcd(seg, BLK)
        for i in range(seg // size):
            keep = jnp.zeros((1, cols), F32)
            for b in range(cols // BLK):
                kept = pattern_ref[b, lax.div(start + i * size, BLK)] > 0
                keep = jnp.where(lane_block == b, jnp.where(kept, 1.0, 0.0), keep)
            piece = part[i * size : (i + 1) * size, :]
            out_ref[n * seg + i * size : n * seg + (i + 1) * size, :] = jnp.where(
                keep > 0, piece, 0.0
            ).astype(BF16)


def sweep(first, ks, place, pattern, panel, blocks, follows, limit=VMEM_LIMIT):
    rows, cols = panel[0][0].shape[-2:]
    chips = len(panel) // CORES
    n_rows = rows // chips * len(ks)
    depth = len(panel) * cols
    return pl.pallas_call(
        functools.partial(
            sweep_kernel,
            first,
            ks,
            chips,
            [at for _, *at in panel],
            [(j, at) for j, at, _ in blocks],
        ),
        out_shape=jax.ShapeDtypeStruct((n_rows, cols), BF16),
        in_specs=[SMEM, SMEM] + [HBM] * (len(panel) + len(blocks) + len(follows)),
        out_specs=VMEM,
        scratch_shapes=[
            pltpu.VMEM((chips, n_rows, CORES * cols), BF16),
            pltpu.VMEM((depth // rows, rows, cols), BF16),
            pltpu.VMEM((n_rows, cols), F32),
            pltpu.SemaphoreType.DMA((chips, CORES * len(ks))),
            pltpu.SemaphoreType.DMA((chips, rows // min(x.shape[0] for *_, x in blocks))),
        ],
        compiler_params=params(limit),
        cost_estimate=cost(2 * n_rows * depth * cols, 2 * (n_rows + rows) * depth),
        name="rank_sweep",
    )(place, pattern, *[x for x, *_ in panel], *[x for *_, x in blocks], *follows)


def split_heads(keys):
    lane = lax.broadcasted_iota(jnp.int32, keys.shape, 1)
    zero = jnp.zeros_like(keys)
    return jnp.concatenate(
        [jnp.where(lane < HDIM, keys, zero), jnp.where(lane >= HDIM, keys, zero)], axis=0
    )


def expo_kernel(own_ref, other_ref, q_ref, k_ref, out_ref, peak_ref, mask_ref):
    p = pl.program_id(0)
    rows, keys = q_ref.shape[0], k_ref.shape[0]
    block_rows, block_cols = rows // BLK, keys // BLK
    tile = BLK

    @pl.when(p == 0)
    def _():
        lane = lax.broadcasted_iota(jnp.int32, (BLK, LANES), 1)
        for i in range(block_rows):
            excluded = jnp.zeros((BLK, LANES), F32)
            for b in range(block_cols):
                ref, at = (own_ref, b) if b < block_cols // 2 else (other_ref, b - block_cols // 2)
                excluded = jnp.where(lane == b, jnp.where(ref[at, i] > 0, 0.0, -1e30), excluded)
            mask_ref[i * BLK : (i + 1) * BLK, :] = excluded.astype(BF16)
        peak_ref[...] = jnp.zeros_like(peak_ref)

    lane = lax.broadcasted_iota(jnp.int32, (2 * keys, LANES), 1)
    key = lax.broadcasted_iota(jnp.int32, (2 * keys, LANES), 0)
    block_of = jnp.where(key >= keys, key - keys, key) // BLK
    in_block = jnp.where(lane == block_of, 1.0, 0.0).astype(BF16)
    right = jnp.concatenate([split_heads(k_ref[...]), in_block], axis=1)
    peak_lane = lax.broadcasted_iota(jnp.int32, (tile, LANES), 1)
    for t in range(rows // tile):
        at = slice(t * tile, (t + 1) * tile)
        left = jnp.concatenate([q_ref[at, :], mask_ref[at, :]], axis=1)
        s = lax.dot_general(left, right, (((1,), (1,)), ((), ())), preferred_element_type=F32)
        peaks = peak_ref[at, :]
        for side in range(2):
            part = s[:, side * keys : (side + 1) * keys]
            peak = jnp.max(part, axis=1, keepdims=True)
            peaks = jnp.where(peak_lane == HDIM * side + p, peak, peaks)
            out_ref[0, at, side * keys : (side + 1) * keys] = jnp.exp(part - peak).astype(BF16)
        peak_ref[at, :] = peaks


def exponentials(own, other, queries, keys_values):
    rows, keys = queries.shape[0], keys_values.shape[0]
    work = rows * keys * 2 * PAIRS
    return pl.pallas_call(
        expo_kernel,
        out_shape=(
            jax.ShapeDtypeStruct((PAIRS, rows, 2 * keys), BF16),
            jax.ShapeDtypeStruct((rows, LANES), F32),
        ),
        grid=(PAIRS,),
        in_specs=[
            SMEM,
            SMEM,
            pl.BlockSpec((rows, LANES), lambda p: (0, p)),
            pl.BlockSpec((keys, LANES), lambda p: (0, p)),
        ],
        out_specs=(
            pl.BlockSpec((1, rows, 2 * keys), lambda p: (p, 0, 0)),
            pl.BlockSpec((rows, LANES), lambda p: (0, 0)),
        ),
        scratch_shapes=[pltpu.VMEM((rows, LANES), BF16)],
        compiler_params=params(28 * 2**20),
        cost_estimate=cost(512 * work, 2 * work, work),
        name="expo",
    )(own, other, queries, keys_values)


def weigh_kernel(
    root, ks, seg, place_ref, gain_ref, rate_ref, own_ref, other_ref, expo_ref, v_ref, peak_ref,
    *refs,
):
    out_refs, (p_ref, ranks_ref, right_ref) = refs[-3 - len(ks) : -3], refs[-3:]
    cols = own_ref.shape[1]
    keys = 2 * cols
    chip = lax.div(place_ref[1], CORES)
    first_head = lax.rem(place_ref[1], CORES) * 2 * PAIRS
    starts = [pl.multiple_of(lax.bitwise_xor(chip, k) * seg, seg) for k in ks]

    for i in range(len(ks)):
        at = slice(i * seg, (i + 1) * seg)
        ranks_ref[at, :cols] = own_ref[at, :].astype(F32)
        ranks_ref[at, cols:] = other_ref[at, :].astype(F32)
    lane = lax.broadcasted_iota(jnp.int32, (keys, LANES), 1)
    zero = jnp.zeros((keys, LANES), BF16)
    right_ref[:keys, LANES:] = jnp.where(lane < HDIM, 1.0, 0.0).astype(BF16)
    right_ref[keys:, LANES:] = jnp.where(lane < HDIM, 0.0, 1.0).astype(BF16)
    out_lane = lax.broadcasted_iota(jnp.int32, (seg, LANES), 1)

    def pair(p, totals):
        lanes = pl.ds(pl.multiple_of(p * LANES, LANES), LANES)
        values = v_ref[:, lanes]
        right_ref[:keys, :LANES] = jnp.where(lane < HDIM, values, zero)
        right_ref[keys:, :LANES] = jnp.where(lane < HDIM, zero, values)
        for i in range(len(ks)):
            rows_at = slice(i * seg, (i + 1) * seg)
            for half in range(2):
                ranks = ranks_ref[rows_at, half * cols : (half + 1) * cols]
                for side in range(2):
                    rate = rate_ref[first_head + 2 * p + side] * root
                    gain = gain_ref[first_head + 2 * p + side] * math.log2(math.e)
                    at = slice(side * keys + half * cols, side * keys + (half + 1) * cols)
                    weight = expo_ref[p, pl.ds(starts[i], seg), at].astype(F32) * jnp.exp2(
                        gain * jnp.tanh(rate * ranks)
                    )
                    p_ref[rows_at, at] = weight.astype(BF16)
        sums = jnp.dot(p_ref[...], right_ref[...], preferred_element_type=F32)
        now = []
        for i, out_ref in enumerate(out_refs):
            part = sums[i * seg : (i + 1) * seg, :]
            out_ref[:seg, lanes] = part[:, :LANES].astype(BF16)
            now.append(jnp.where(out_lane % HDIM == p, part[:, LANES:], totals[i]))
        return tuple(now)

    totals = lax.fori_loop(
        0, PAIRS, pair, tuple(jnp.zeros((seg, LANES), F32) for _ in ks)
    )
    half = WIDTH // 2
    for i, out_ref in enumerate(out_refs):
        extra = totals[i]
        rest = peak_ref[pl.ds(starts[i], seg), :]
        for n in range(1, 4):
            piece = rest.astype(BF16).astype(F32)
            rest = rest - piece
            here = (out_lane % HDIM >= n * PAIRS) & (out_lane % HDIM < (n + 1) * PAIRS)
            extra = jnp.where(here, pltpu.roll(piece, n * PAIRS, 1), extra)
        extra = jnp.concatenate([extra, jnp.zeros((half - seg, LANES), F32)], axis=0).T
        for side in range(2):
            out_ref[seg:, side * half : (side + 1) * half] = extra[
                side * HDIM : side * HDIM + EXTRA
            ].astype(BF16)


def weigh(root, chips, ks, place, gain, rate, own, other, expo, values, peak, follows):
    n_rows, cols = own.shape
    seg = n_rows // len(ks)
    rows, keys = seg * chips, 2 * cols
    work = n_rows * keys * 2 * PAIRS
    return pl.pallas_call(
        functools.partial(weigh_kernel, root, ks, seg),
        out_shape=(jax.ShapeDtypeStruct((seg + EXTRA, WIDTH), BF16),) * len(ks),
        grid=(1,),
        in_specs=[
            SMEM,
            SMEM,
            SMEM,
            pl.BlockSpec((n_rows, cols), lambda i: (0, 0)),
            pl.BlockSpec((n_rows, cols), lambda i: (0, 0)),
            VMEM,
            pl.BlockSpec((keys, WIDTH), lambda i: (0, 1)),
            pl.BlockSpec((rows, LANES), lambda i: (0, 0)),
            *[HBM] * len(follows),
        ],
        out_specs=(pl.BlockSpec((seg + EXTRA, WIDTH), lambda i: (0, 0)),) * len(ks),
        scratch_shapes=[
            pltpu.VMEM((n_rows, 2 * keys), BF16),
            pltpu.VMEM((n_rows, keys), F32),
            pltpu.VMEM((2 * keys, 2 * LANES), BF16),
        ],
        compiler_params=params(28 * 2**20),
        cost_estimate=cost(512 * work, 2 * work, 2 * work),
        name="weigh",
    )(place, gain, rate, own, other, expo, values, peak, *follows)


def divide_kernel(*refs):
    parts, out_ref = refs[:-1], refs[-1]
    seg, half = out_ref.shape[0], WIDTH // 2
    lane = lax.broadcasted_iota(jnp.int32, (seg, LANES), 1)
    fit = LANES // (2 * EXTRA)
    totals, peaks, largest = [], [], None
    for first in range(0, len(parts), fit):
        group = parts[first : first + fit]
        extra = [
            part[seg:, side * half : (side + 1) * half].astype(F32)
            for part in group
            for side in range(2)
        ]
        spare = LANES - EXTRA * len(extra)
        if spare:
            extra.append(jnp.zeros((spare, half), F32))
        extra = jnp.concatenate(extra, axis=0).T[:seg]
        totals.append(extra)
        peak = sum(pltpu.roll(extra, LANES - n * PAIRS, 1) for n in range(1, 4))
        if spare:
            peak = jnp.where(lane < LANES - spare, peak, -jnp.inf)
        peaks.append(peak)
        largest = peak if largest is None else jnp.maximum(largest, peak)

    def over_parts(value, combine):
        step = 2 * EXTRA
        while step < LANES:
            value = combine(value, pltpu.roll(value, step, 1))
            step *= 2
        return value

    largest = over_parts(largest, jnp.maximum)
    weights = [jnp.exp(peak - largest) for peak in peaks]
    inverse = 1.0 / over_parts(
        sum(w * x for w, x in zip(weights, totals, strict=True)), lambda x, y: x + y
    )
    scales = [w * inverse for w in weights]
    for p in range(PAIRS):
        lanes = slice(p * LANES, (p + 1) * LANES)
        total = jnp.zeros((seg, LANES), F32)
        for i, part in enumerate(parts):
            at = i % fit * 2 * EXTRA + p
            scale = scales[i // fit]
            both = jnp.where(
                lane < HDIM, scale[:, at : at + 1], scale[:, at + EXTRA : at + EXTRA + 1]
            )
            total += part[:seg, lanes].astype(F32) * both
        out_ref[:, lanes] = total.astype(BF16)


def divide(parts):
    seg = parts[0].shape[0] - EXTRA
    return pl.pallas_call(
        divide_kernel,
        out_shape=jax.ShapeDtypeStruct((seg, WIDTH), BF16),
        in_specs=[VMEM] * len(parts),
        out_specs=VMEM,
        compiler_params=params(SMALL_LIMIT),
        cost_estimate=cost(8 * seg * D, 8 * seg * D),
        name="divide",
    )(*parts)


def project_out_kernel(place_ref, own_ref, other_ref, *refs):
    n = len(refs) // 2
    core = lax.rem(place_ref[1], CORES)
    mine = pl.ds(pl.multiple_of(core * WIDTH, WIDTH), WIDTH)
    others = pl.ds(pl.multiple_of((1 - core) * WIDTH, WIDTH), WIDTH)
    for w_ref, out_ref in zip(refs[:n], refs[n:], strict=True):
        total = jnp.dot(own_ref[...], w_ref[mine, :], preferred_element_type=F32)
        total += jnp.dot(other_ref[...], w_ref[others, :], preferred_element_type=F32)
        out_ref[...] = total.astype(BF16)


def project_out(place, own, other, w_all):
    seg, (depth, width) = own.shape[0], w_all[0].shape
    chips = len(w_all)
    return pl.pallas_call(
        project_out_kernel,
        out_shape=(jax.ShapeDtypeStruct((seg, width), BF16),) * chips,
        in_specs=[SMEM] + [VMEM] * (2 + chips),
        out_specs=(VMEM,) * chips,
        compiler_params=params(SMALL_LIMIT),
        cost_estimate=cost(2 * seg * depth * width * chips, 2 * depth * width * chips),
        name="project_out",
    )(place, own, other, *w_all)


def assemble_kernel(place_ref, *refs):
    parts, out_ref = refs[:-1], refs[-1]
    chip = lax.div(place_ref[1], CORES)
    seg = parts[0].shape[0]
    for k, part in enumerate(parts):
        at = pl.multiple_of(lax.bitwise_xor(chip, k) * seg, seg)
        out_ref[pl.ds(at, seg), :] = part[...]


def assemble(place, parts):
    seg, width = parts[0].shape
    return pl.pallas_call(
        assemble_kernel,
        out_shape=jax.ShapeDtypeStruct((seg * len(parts), width), BF16),
        in_specs=[SMEM] + [VMEM] * len(parts),
        out_specs=VMEM,
        compiler_params=params(SMALL_LIMIT),
        name="assemble",
    )(place, *parts)


def shards(node_features, edge_weight, pattern, w_qkv, w_out, bias_gain, bias_rate):
    rows, cols = edge_weight.shape
    row_count, col_count = lax.axis_size("row"), lax.axis_size("col")
    row_pos, col_pos = lax.axis_index("row"), lax.axis_index("col")
    ratio = rows // cols
    chips = col_count // CORES
    root = math.sqrt(rows * row_count)
    place = jnp.stack([row_pos, col_pos]).astype(jnp.int32)
    core = (col_pos % CORES).astype(jnp.int32).reshape(1)
    pattern = pattern.T
    together = lax.optimization_barrier

    def along_col(value, j):
        return lax.ppermute(value, "col", xor_pairs(col_count, j))

    def along_row(value, j):
        return lax.ppermute(value, "row", xor_pairs(row_count, j))

    def from_rows(value):
        return [value] + [along_row(value, j) for j in range(1, row_count)]

    def spread(blocks, bits):
        new = dict(blocks)
        for k in range(chips - 1, 0, -1):
            if k.bit_count() == bits:
                low = k & -k
                new[k] = along_col(blocks[k ^ low], CORES * low)
        return new

    ring = [0, 1, 3, 2] if row_count == 4 else list(range(row_count))
    def place_of(r):
        return r ^ (r >> 1) if row_count == 4 else r

    steps_away = (
        (place_of(row_pos) - place_of(col_pos // ratio)) * (1 - 2 * (col_pos % CORES))
    ) % row_count

    def feature_step(value, s):
        pairs = []
        for c in range(col_count):
            way = 1 - 2 * (c % CORES)
            i = ring.index(c // ratio) + way * (s - 1)
            here, there = ring[i % row_count], ring[(i + way) % row_count]
            pairs.append((here * col_count + c, there * col_count + c))
        return lax.ppermute(value, ("row", "col"), pairs)

    adjacency, features = start(place, pattern, edge_weight, node_features)
    blocks = spread({0: adjacency}, 1)
    near = [1, 2] if row_count == 4 else list(range(1, row_count))
    columns = {j: along_row(adjacency, j) for j in near}
    other_pattern = along_col(pattern, 1)
    queries = project_in(core, [node_features], w_qkv, [0], 1.0 / math.sqrt(HDIM))
    moved = [features, feature_step(features, 1)]
    raw_columns = columns
    queries, moved, columns, blocks = together((queries, moved, columns, blocks))

    order = sorted(blocks)
    swapped = along_col(jnp.stack([blocks[k] for k in order]), 1)
    far = []
    if row_count == 4:
        half = rows // 2
        far = [along_row(columns[2][:half], 1), along_row(columns[1][half:], 2)]
    moved.append(feature_step(moved[-1], 2))
    for bits in range(2, chips.bit_length()):
        blocks = spread(blocks, bits)
    raw_far = far
    far, swapped, blocks = together((far, swapped, blocks))
    for s in range(3, row_count):
        moved.append(feature_step(moved[-1], s))
    panel = [(x, CORES * k, None) for k, x in blocks.items()]
    panel += [(swapped, CORES * k + 1, i) for i, k in enumerate(order)]
    panel += [(along_col(x, 1), CORES * k + 1, None) for k, x in blocks.items() if k not in order]
    columns = [(0, 0, adjacency)] + [(j, 0, x) for j, x in raw_columns.items()]
    columns += [(3, i * x.shape[0], x) for i, x in enumerate(raw_far)]
    ranks = sweep(True, range(chips), place, pattern, panel, columns, [], 58 * 2**20)
    columns = [(j, 0, x) for j, x in enumerate(from_rows(ranks))]

    ranks, moved = together((ranks, moved))
    key_rows = features
    for s in range(1, row_count):
        key_rows = jnp.where(steps_away == s, moved[s], key_rows)
    keys_values = project_in(core, [key_rows, along_col(key_rows, 1)], w_qkv, [D, 2 * D], limit=28 * 2**20)
    keys_values, w_out = together((keys_values, w_out))
    w_all = spread({0: w_out}, 1)
    expo, peak = exponentials(pattern, other_pattern, queries, keys_values)
    w_all, peak = together((w_all, peak))
    for bits in range(2, chips.bit_length()):
        w_all = spread(w_all, bits)
    w_all = [w_all[k] for k in range(chips)]

    groups = [list(range(chips // 2, chips)), list(range(chips // 2))]
    ranks = [
        sweep(False, ks, place, pattern, panel, columns, follow, 24 * 2**20)
        for ks, follow in zip(groups, [[peak], [peak, *w_all[1:]]], strict=True)
    ]
    others = [along_col(x, 1) for x in ranks]
    parts, follows = [None] * chips, [ranks[1]]
    for ks, own, other in zip(groups, ranks, others, strict=True):
        sums = weigh(
            root, chips, ks, place, bias_gain, bias_rate, own, other, expo, keys_values, peak,
            follows,
        )
        for k, part in zip(ks, sums, strict=True):
            parts[k] = part if k == 0 else along_col(part, CORES * k)
        follows = [sums[0]]
    attended = divide(parts)
    mixed = project_out(place, attended, along_col(attended, 1), w_all)
    mixed = [x if k == 0 else along_col(x, CORES * k) for k, x in enumerate(mixed)]
    return assemble(place, mixed)


def solution(mesh):
    in_specs = (P("row", None), P("row", "col"), P("row", "col"), P(), P(None, "col"), P(), P())
    out_specs = P("row", "col")
    return jax.shard_map(shards, mesh=mesh, in_specs=in_specs, out_specs=out_specs, check_vma=False)
```

```python
import functools
import math

import jax
import jax.numpy as jnp
from jax import lax
from jax.experimental import pallas as pl
from jax.experimental.pallas import tpu as pltpu
from jax.sharding import PartitionSpec as P

D = 1024
HEADS = 16
BLK = 128
HDIM = 64
CORES = 2
PAIRS = HEADS // 2 // CORES
WIDTH = D // CORES
EXTRA = 4 * PAIRS
LANES = 128
VMEM_LIMIT = 58 * 2**20
SMALL_LIMIT = 16 * 2**20

VMEM = pl.BlockSpec(memory_space=pltpu.VMEM)
SMEM = pl.BlockSpec(memory_space=pltpu.SMEM)
HBM = pl.BlockSpec(memory_space=pltpu.HBM)
BF16 = jnp.bfloat16
F32 = jnp.float32


def params(limit=VMEM_LIMIT):
    return pltpu.CompilerParams(vmem_limit_bytes=limit)


def cost(flops, nbytes, trans=0):
    return pl.CostEstimate(flops=int(flops), bytes_accessed=int(nbytes), transcendentals=int(trans))


def xor_pairs(n, j):
    return [(i, i ^ j) for i in range(n)]


def keep_tile(pattern_ref, first_row, block_rows):
    block_cols = pattern_ref.shape[0]
    tiles = []
    for i in range(block_rows):
        parts = [
            jnp.full((1, BLK), jnp.where(pattern_ref[b, first_row + i] > 0, 1.0, 0.0), F32)
            for b in range(block_cols)
        ]
        tiles.append(
            jnp.broadcast_to(jnp.concatenate(parts, axis=1), (BLK, block_cols * BLK))
        )
    return jnp.concatenate(tiles, axis=0)


def start_kernel(place_ref, pattern_ref, weight_ref, features_ref, out_ref, cut_ref, sem):
    cols = cut_ref.shape[0]
    ratio = features_ref.shape[0] // cols
    at = pl.multiple_of(lax.rem(place_ref[1], ratio) * cols, cols)
    copy = pltpu.make_async_copy(features_ref.at[pl.ds(at, cols), :], cut_ref, sem)
    copy.start()
    for i in range(out_ref.shape[0] // BLK):
        at = slice(i * BLK, (i + 1) * BLK)
        keep = keep_tile(pattern_ref, i, 1)
        out_ref[at, :] = jnp.where(keep > 0, weight_ref[at, :].astype(F32), 0.0).astype(BF16)
    copy.wait()


def start(place, pattern, weight, features):
    rows, cols = weight.shape
    return pl.pallas_call(
        start_kernel,
        out_shape=(
            jax.ShapeDtypeStruct((rows, cols), BF16),
            jax.ShapeDtypeStruct((cols, features.shape[1]), BF16),
        ),
        in_specs=[SMEM, SMEM, VMEM, HBM],
        out_specs=(VMEM, VMEM),
        scratch_shapes=[pltpu.SemaphoreType.DMA],
        compiler_params=params(),
        cost_estimate=cost(rows * cols, 4 * rows * cols),
        name="start",
    )(place, pattern, weight, features)


def project_in_kernel(scale, place_ref, *refs):
    xs, (w_ref, out_ref) = refs[:-2], refs[-2:]
    rows = xs[0].shape[0]
    for i, x_ref in enumerate(xs):
        out = jnp.dot(x_ref[...], w_ref[...], preferred_element_type=F32).astype(BF16)
        if scale is not None:
            out = out * jnp.asarray(scale, BF16)
        out_ref[i * rows : (i + 1) * rows, :] = out


def project_in(core, xs, w, firsts, scale=None, tile=256, limit=VMEM_LIMIT):
    rows, depth = xs[0].shape
    steps = WIDTH // tile

    def column(i, core_ref):
        first = firsts[0] // tile
        for n, start in enumerate(firsts[1:], 1):
            first = jnp.where(i >= n * steps, start // tile, first)
        return 0, first + core_ref[0] * steps + lax.rem(i, steps)

    return pl.pallas_call(
        functools.partial(project_in_kernel, scale),
        out_shape=jax.ShapeDtypeStruct((rows * len(xs), WIDTH * len(firsts)), BF16),
        grid_spec=pltpu.PrefetchScalarGridSpec(
            num_scalar_prefetch=1,
            grid=(steps * len(firsts),),
            in_specs=[pl.BlockSpec((rows, depth), lambda i, c: (0, 0))] * len(xs)
            + [pl.BlockSpec((depth, tile), column)],
            out_specs=pl.BlockSpec((rows * len(xs), tile), lambda i, c: (0, i)),
        ),
        compiler_params=params(limit),
        cost_estimate=cost(
            2 * rows * len(xs) * depth * WIDTH * len(firsts),
            2 * depth * (rows * len(xs) + WIDTH * len(firsts)),
        ),
        name="project_in",
    )(core, *xs, w)


def sweep_kernel(first, ks, chips, left_at, right_at, place_ref, pattern_ref, *refs):
    n_right = len(right_at)
    panel, rights = refs[: len(left_at)], refs[len(left_at) : len(left_at) + n_right]
    out_ref, left_ref, right_ref, acc_ref, left_sem, right_sem = refs[-6:]
    rows, cols = panel[0].shape[-2:]
    seg = rows // chips
    row_pos, col_pos = place_ref[0], place_ref[1]
    chip, core = lax.div(col_pos, CORES), lax.rem(col_pos, CORES)
    starts = [pl.multiple_of(lax.bitwise_xor(chip, k) * seg, seg) for k in ks]
    if len(ks) == chips:
        starts, seg = [0], rows

    part = min(ref.shape[0] for ref in rights)

    def right_copies(i, slot):
        xor, offset = right_at[i]
        for at in range(0, rights[i].shape[0], part):
            target = right_ref.at[slot, pl.ds(offset + at, part), :]
            source = rights[i].at[pl.ds(at, part), :]
            yield pltpu.make_async_copy(source, target, right_sem.at[slot, (offset + at) // part])

    def left_copies(k):
        for ref, (j, index) in zip(panel, left_at, strict=True):
            if j // CORES != k:
                continue
            block = ref if index is None else ref.at[index]
            at = pl.multiple_of(lax.bitwise_xor(core, j % CORES) * cols, cols)
            for n, start in enumerate(starts):
                yield pltpu.make_async_copy(
                    block.at[pl.ds(start, seg), :],
                    left_ref.at[k, pl.ds(n * seg, seg), pl.ds(at, cols)],
                    left_sem.at[k, j % CORES * len(starts) + n],
                )

    for k in range(chips):
        for copy in left_copies(k):
            copy.start()
        for xor in sorted({at[0] for at in right_at}):

            @pl.when(lax.bitwise_xor(row_pos, chip) == xor ^ k)
            def _():
                for i in range(n_right):
                    if right_at[i][0] == xor:
                        for copy in right_copies(i, k):
                            copy.start()

    for k in range(chips):
        for at in range(0, rows, part):
            half = right_ref.at[k, pl.ds(at, part), :]
            pltpu.make_async_copy(half, half, right_sem.at[k, at // part]).wait()
        for copy in left_copies(k):
            copy.wait()
        product = jnp.dot(left_ref[k], right_ref[k], preferred_element_type=F32)
        if k == 0:
            acc_ref[...] = product
        elif k < chips - 1:
            acc_ref[...] += product
    product = product + acc_ref[...]
    own = left_ref[0, :, pl.ds(pl.multiple_of(core * cols, cols), cols)].astype(F32)
    total = 0.1275 * own + (0.85 * 0.1275 if first else 0.85) * product
    diagonal = lax.broadcasted_iota(jnp.int32, (seg, cols), 1) - lax.broadcasted_iota(
        jnp.int32, (seg, cols), 0
    )
    lane_block = lax.broadcasted_iota(jnp.int32, (1, cols), 1) // BLK
    for n, start in enumerate(starts):
        at = slice(n * seg, (n + 1) * seg)
        part = total[at, :]
        if not first:
            here = diagonal == row_pos * rows + start - col_pos * cols
            part = jnp.where(here, part + 0.15, part)
        size = math.gcd(seg, BLK)
        for i in range(seg // size):
            keep = jnp.zeros((1, cols), F32)
            for b in range(cols // BLK):
                kept = pattern_ref[b, lax.div(start + i * size, BLK)] > 0
                keep = jnp.where(lane_block == b, jnp.where(kept, 1.0, 0.0), keep)
            piece = part[i * size : (i + 1) * size, :]
            out_ref[n * seg + i * size : n * seg + (i + 1) * size, :] = jnp.where(
                keep > 0, piece, 0.0
            ).astype(BF16)


def sweep(first, ks, place, pattern, panel, blocks, follows, limit=VMEM_LIMIT):
    rows, cols = panel[0][0].shape[-2:]
    chips = len(panel) // CORES
    n_rows = rows // chips * len(ks)
    depth = len(panel) * cols
    return pl.pallas_call(
        functools.partial(
            sweep_kernel,
            first,
            ks,
            chips,
            [at for _, *at in panel],
            [(j, at) for j, at, _ in blocks],
        ),
        out_shape=jax.ShapeDtypeStruct((n_rows, cols), BF16),
        in_specs=[SMEM, SMEM] + [HBM] * (len(panel) + len(blocks) + len(follows)),
        out_specs=VMEM,
        scratch_shapes=[
            pltpu.VMEM((chips, n_rows, CORES * cols), BF16),
            pltpu.VMEM((depth // rows, rows, cols), BF16),
            pltpu.VMEM((n_rows, cols), F32),
            pltpu.SemaphoreType.DMA((chips, CORES * len(ks))),
            pltpu.SemaphoreType.DMA((chips, rows // min(x.shape[0] for *_, x in blocks))),
        ],
        compiler_params=params(limit),
        cost_estimate=cost(2 * n_rows * depth * cols, 2 * (n_rows + rows) * depth),
        name="rank_sweep",
    )(place, pattern, *[x for x, *_ in panel], *[x for *_, x in blocks], *follows)


def split_heads(keys):
    lane = lax.broadcasted_iota(jnp.int32, keys.shape, 1)
    zero = jnp.zeros_like(keys)
    return jnp.concatenate(
        [jnp.where(lane < HDIM, keys, zero), jnp.where(lane >= HDIM, keys, zero)], axis=0
    )


def expo_kernel(own_ref, other_ref, q_ref, k_ref, out_ref, peak_ref, mask_ref):
    p = pl.program_id(0)
    rows, keys = q_ref.shape[0], k_ref.shape[0]
    block_rows, block_cols = rows // BLK, keys // BLK
    tile = BLK

    @pl.when(p == 0)
    def _():
        lane = lax.broadcasted_iota(jnp.int32, (BLK, LANES), 1)
        for i in range(block_rows):
            excluded = jnp.zeros((BLK, LANES), F32)
            for b in range(block_cols):
                ref, at = (own_ref, b) if b < block_cols // 2 else (other_ref, b - block_cols // 2)
                excluded = jnp.where(lane == b, jnp.where(ref[at, i] > 0, 0.0, -1e30), excluded)
            mask_ref[i * BLK : (i + 1) * BLK, :] = excluded.astype(BF16)
        peak_ref[...] = jnp.zeros_like(peak_ref)

    lane = lax.broadcasted_iota(jnp.int32, (2 * keys, LANES), 1)
    key = lax.broadcasted_iota(jnp.int32, (2 * keys, LANES), 0)
    block_of = jnp.where(key >= keys, key - keys, key) // BLK
    in_block = jnp.where(lane == block_of, 1.0, 0.0).astype(BF16)
    right = jnp.concatenate([split_heads(k_ref[...]), in_block], axis=1)
    peak_lane = lax.broadcasted_iota(jnp.int32, (tile, LANES), 1)
    for t in range(rows // tile):
        at = slice(t * tile, (t + 1) * tile)
        left = jnp.concatenate([q_ref[at, :], mask_ref[at, :]], axis=1)
        s = lax.dot_general(left, right, (((1,), (1,)), ((), ())), preferred_element_type=F32)
        peaks = peak_ref[at, :]
        for side in range(2):
            part = s[:, side * keys : (side + 1) * keys]
            peak = jnp.max(part, axis=1, keepdims=True)
            peaks = jnp.where(peak_lane == HDIM * side + p, peak, peaks)
            out_ref[0, at, side * keys : (side + 1) * keys] = jnp.exp(part - peak).astype(BF16)
        peak_ref[at, :] = peaks


def exponentials(own, other, queries, keys_values):
    rows, keys = queries.shape[0], keys_values.shape[0]
    work = rows * keys * 2 * PAIRS
    return pl.pallas_call(
        expo_kernel,
        out_shape=(
            jax.ShapeDtypeStruct((PAIRS, rows, 2 * keys), BF16),
            jax.ShapeDtypeStruct((rows, LANES), F32),
        ),
        grid=(PAIRS,),
        in_specs=[
            SMEM,
            SMEM,
            pl.BlockSpec((rows, LANES), lambda p: (0, p)),
            pl.BlockSpec((keys, LANES), lambda p: (0, p)),
        ],
        out_specs=(
            pl.BlockSpec((1, rows, 2 * keys), lambda p: (p, 0, 0)),
            pl.BlockSpec((rows, LANES), lambda p: (0, 0)),
        ),
        scratch_shapes=[pltpu.VMEM((rows, LANES), BF16)],
        compiler_params=params(28 * 2**20),
        cost_estimate=cost(512 * work, 2 * work, work),
        name="expo",
    )(own, other, queries, keys_values)


def weigh_kernel(
    root, ks, seg, place_ref, gain_ref, rate_ref, own_ref, other_ref, expo_ref, v_ref, peak_ref,
    *refs,
):
    out_refs, (p_ref, ranks_ref, right_ref) = refs[-3 - len(ks) : -3], refs[-3:]
    cols = own_ref.shape[1]
    keys = 2 * cols
    chip = lax.div(place_ref[1], CORES)
    first_head = lax.rem(place_ref[1], CORES) * 2 * PAIRS
    starts = [pl.multiple_of(lax.bitwise_xor(chip, k) * seg, seg) for k in ks]

    for i in range(len(ks)):
        at = slice(i * seg, (i + 1) * seg)
        ranks_ref[at, :cols] = own_ref[at, :].astype(F32)
        ranks_ref[at, cols:] = other_ref[at, :].astype(F32)
    lane = lax.broadcasted_iota(jnp.int32, (keys, LANES), 1)
    zero = jnp.zeros((keys, LANES), BF16)
    right_ref[:keys, LANES:] = jnp.where(lane < HDIM, 1.0, 0.0).astype(BF16)
    right_ref[keys:, LANES:] = jnp.where(lane < HDIM, 0.0, 1.0).astype(BF16)
    out_lane = lax.broadcasted_iota(jnp.int32, (seg, LANES), 1)

    def pair(p, totals):
        lanes = pl.ds(pl.multiple_of(p * LANES, LANES), LANES)
        values = v_ref[:, lanes]
        right_ref[:keys, :LANES] = jnp.where(lane < HDIM, values, zero)
        right_ref[keys:, :LANES] = jnp.where(lane < HDIM, zero, values)
        for i in range(len(ks)):
            rows_at = slice(i * seg, (i + 1) * seg)
            for half in range(2):
                ranks = ranks_ref[rows_at, half * cols : (half + 1) * cols]
                for side in range(2):
                    rate = rate_ref[first_head + 2 * p + side] * root
                    gain = gain_ref[first_head + 2 * p + side] * math.log2(math.e)
                    at = slice(side * keys + half * cols, side * keys + (half + 1) * cols)
                    weight = expo_ref[p, pl.ds(starts[i], seg), at].astype(F32) * jnp.exp2(
                        gain * jnp.tanh(rate * ranks)
                    )
                    p_ref[rows_at, at] = weight.astype(BF16)
        sums = jnp.dot(p_ref[...], right_ref[...], preferred_element_type=F32)
        now = []
        for i, out_ref in enumerate(out_refs):
            part = sums[i * seg : (i + 1) * seg, :]
            out_ref[:seg, lanes] = part[:, :LANES].astype(BF16)
            now.append(jnp.where(out_lane % HDIM == p, part[:, LANES:], totals[i]))
        return tuple(now)

    totals = lax.fori_loop(
        0, PAIRS, pair, tuple(jnp.zeros((seg, LANES), F32) for _ in ks)
    )
    half = WIDTH // 2
    for i, out_ref in enumerate(out_refs):
        extra = totals[i]
        rest = peak_ref[pl.ds(starts[i], seg), :]
        for n in range(1, 4):
            piece = rest.astype(BF16).astype(F32)
            rest = rest - piece
            here = (out_lane % HDIM >= n * PAIRS) & (out_lane % HDIM < (n + 1) * PAIRS)
            extra = jnp.where(here, pltpu.roll(piece, n * PAIRS, 1), extra)
        extra = jnp.concatenate([extra, jnp.zeros((half - seg, LANES), F32)], axis=0).T
        for side in range(2):
            out_ref[seg:, side * half : (side + 1) * half] = extra[
                side * HDIM : side * HDIM + EXTRA
            ].astype(BF16)


def weigh(root, chips, ks, first, place, gain, rate, own, other, expo, values, peak, follows):
    (_, rows, _), cols = expo.shape, own.shape[1]
    seg = rows // chips
    n_rows, keys = seg * len(ks), 2 * cols
    part = pl.BlockSpec((n_rows, cols), lambda i: (first // len(ks), 0))
    work = n_rows * keys * 2 * PAIRS
    return pl.pallas_call(
        functools.partial(weigh_kernel, root, ks, seg),
        out_shape=(jax.ShapeDtypeStruct((seg + EXTRA, WIDTH), BF16),) * len(ks),
        grid=(1,),
        in_specs=[
            SMEM,
            SMEM,
            SMEM,
            part,
            part,
            VMEM,
            pl.BlockSpec((keys, WIDTH), lambda i: (0, 1)),
            pl.BlockSpec((rows, LANES), lambda i: (0, 0)),
            *[HBM] * len(follows),
        ],
        out_specs=(pl.BlockSpec((seg + EXTRA, WIDTH), lambda i: (0, 0)),) * len(ks),
        scratch_shapes=[
            pltpu.VMEM((n_rows, 2 * keys), BF16),
            pltpu.VMEM((n_rows, keys), F32),
            pltpu.VMEM((2 * keys, 2 * LANES), BF16),
        ],
        compiler_params=params(28 * 2**20),
        cost_estimate=cost(512 * work, 2 * work, 2 * work),
        name="weigh",
    )(place, gain, rate, own, other, expo, values, peak, *follows)


def divide_kernel(*refs):
    parts, out_ref = refs[:-1], refs[-1]
    seg, half = out_ref.shape[0], WIDTH // 2
    lane = lax.broadcasted_iota(jnp.int32, (seg, LANES), 1)
    fit = LANES // (2 * EXTRA)
    totals, peaks, largest = [], [], None
    for first in range(0, len(parts), fit):
        group = parts[first : first + fit]
        extra = [
            part[seg:, side * half : (side + 1) * half].astype(F32)
            for part in group
            for side in range(2)
        ]
        spare = LANES - EXTRA * len(extra)
        if spare:
            extra.append(jnp.zeros((spare, half), F32))
        extra = jnp.concatenate(extra, axis=0).T[:seg]
        totals.append(extra)
        peak = sum(pltpu.roll(extra, LANES - n * PAIRS, 1) for n in range(1, 4))
        if spare:
            peak = jnp.where(lane < LANES - spare, peak, -jnp.inf)
        peaks.append(peak)
        largest = peak if largest is None else jnp.maximum(largest, peak)

    def over_parts(value, combine):
        step = 2 * EXTRA
        while step < LANES:
            value = combine(value, pltpu.roll(value, step, 1))
            step *= 2
        return value

    largest = over_parts(largest, jnp.maximum)
    weights = [jnp.exp(peak - largest) for peak in peaks]
    inverse = 1.0 / over_parts(
        sum(w * x for w, x in zip(weights, totals, strict=True)), lambda x, y: x + y
    )
    scales = [w * inverse for w in weights]
    for p in range(PAIRS):
        lanes = slice(p * LANES, (p + 1) * LANES)
        total = jnp.zeros((seg, LANES), F32)
        for i, part in enumerate(parts):
            at = i % fit * 2 * EXTRA + p
            scale = scales[i // fit]
            both = jnp.where(
                lane < HDIM, scale[:, at : at + 1], scale[:, at + EXTRA : at + EXTRA + 1]
            )
            total += part[:seg, lanes].astype(F32) * both
        out_ref[:, lanes] = total.astype(BF16)


def divide(parts):
    seg = parts[0].shape[0] - EXTRA
    return pl.pallas_call(
        divide_kernel,
        out_shape=jax.ShapeDtypeStruct((seg, WIDTH), BF16),
        in_specs=[VMEM] * len(parts),
        out_specs=VMEM,
        compiler_params=params(SMALL_LIMIT),
        cost_estimate=cost(8 * seg * D, 8 * seg * D),
        name="divide",
    )(*parts)


def project_out_kernel(place_ref, own_ref, other_ref, *refs):
    n = len(refs) // 2
    core = lax.rem(place_ref[1], CORES)
    mine = pl.ds(pl.multiple_of(core * WIDTH, WIDTH), WIDTH)
    others = pl.ds(pl.multiple_of((1 - core) * WIDTH, WIDTH), WIDTH)
    for w_ref, out_ref in zip(refs[:n], refs[n:], strict=True):
        total = jnp.dot(own_ref[...], w_ref[mine, :], preferred_element_type=F32)
        total += jnp.dot(other_ref[...], w_ref[others, :], preferred_element_type=F32)
        out_ref[...] = total.astype(BF16)


def project_out(place, own, other, w_all):
    seg, (depth, width) = own.shape[0], w_all[0].shape
    chips = len(w_all)
    return pl.pallas_call(
        project_out_kernel,
        out_shape=(jax.ShapeDtypeStruct((seg, width), BF16),) * chips,
        in_specs=[SMEM] + [VMEM] * (2 + chips),
        out_specs=(VMEM,) * chips,
        compiler_params=params(SMALL_LIMIT),
        cost_estimate=cost(2 * seg * depth * width * chips, 2 * depth * width * chips),
        name="project_out",
    )(place, own, other, *w_all)


def shards(node_features, edge_weight, pattern, w_qkv, w_out, bias_gain, bias_rate):
    rows, cols = edge_weight.shape
    row_count, col_count = lax.axis_size("row"), lax.axis_size("col")
    row_pos, col_pos = lax.axis_index("row"), lax.axis_index("col")
    ratio = rows // cols
    chips = col_count // CORES
    chip = col_pos // CORES
    root = math.sqrt(rows * row_count)
    place = jnp.stack([row_pos, col_pos]).astype(jnp.int32)
    core = (col_pos % CORES).astype(jnp.int32).reshape(1)
    pattern = pattern.T
    together = lax.optimization_barrier

    def along_col(value, j):
        return lax.ppermute(value, "col", xor_pairs(col_count, j))

    def along_row(value, j):
        return lax.ppermute(value, "row", xor_pairs(row_count, j))

    def from_rows(value):
        return [value] + [along_row(value, j) for j in range(1, row_count)]

    def spread(blocks, bits):
        new = dict(blocks)
        for k in range(chips - 1, 0, -1):
            if k.bit_count() == bits:
                low = k & -k
                new[k] = along_col(blocks[k ^ low], CORES * low)
        return new

    ring = [0, 1, 3, 2] if row_count == 4 else list(range(row_count))
    def place_of(r):
        return r ^ (r >> 1) if row_count == 4 else r

    steps_away = (
        (place_of(row_pos) - place_of(col_pos // ratio)) * (1 - 2 * (col_pos % CORES))
    ) % row_count

    def feature_step(value, s):
        pairs = []
        for c in range(col_count):
            way = 1 - 2 * (c % CORES)
            i = ring.index(c // ratio) + way * (s - 1)
            here, there = ring[i % row_count], ring[(i + way) % row_count]
            pairs.append((here * col_count + c, there * col_count + c))
        return lax.ppermute(value, ("row", "col"), pairs)

    adjacency, features = start(place, pattern, edge_weight, node_features)
    blocks = spread({0: adjacency}, 1)
    near = [1, 2] if row_count == 4 else list(range(1, row_count))
    columns = {j: along_row(adjacency, j) for j in near}
    other_pattern = along_col(pattern, 1)
    queries = project_in(core, [node_features], w_qkv, [0], 1.0 / math.sqrt(HDIM))
    moved = [features, feature_step(features, 1)]
    raw_columns = columns
    queries, moved, columns, blocks = together((queries, moved, columns, blocks))

    order = sorted(blocks)
    swapped = along_col(jnp.stack([blocks[k] for k in order]), 1)
    far = []
    if row_count == 4:
        half = rows // 2
        far = [along_row(columns[2][:half], 1), along_row(columns[1][half:], 2)]
    moved.append(feature_step(moved[-1], 2))
    for bits in range(2, chips.bit_length()):
        blocks = spread(blocks, bits)
    raw_far = far
    far, swapped, blocks = together((far, swapped, blocks))
    for s in range(3, row_count):
        moved.append(feature_step(moved[-1], s))
    panel = [(x, CORES * k, None) for k, x in blocks.items()]
    panel += [(swapped, CORES * k + 1, i) for i, k in enumerate(order)]
    panel += [(along_col(x, 1), CORES * k + 1, None) for k, x in blocks.items() if k not in order]
    columns = [(0, 0, adjacency)] + [(j, 0, x) for j, x in raw_columns.items()]
    columns += [(3, i * x.shape[0], x) for i, x in enumerate(raw_far)]
    key_rows = features
    for s in range(1, row_count - 1):
        key_rows = jnp.where(steps_away == s, moved[s], key_rows)
    ranks = sweep(True, range(chips), place, pattern, panel, columns, [key_rows], 50 * 2**20)
    columns = [(j, 0, x) for j, x in enumerate(from_rows(ranks))]

    ranks, last = together((ranks, moved[-1]))
    key_rows = jnp.where(steps_away == row_count - 1, last, key_rows)
    keys_values = project_in(core, [key_rows, along_col(key_rows, 1)], w_qkv, [D, 2 * D], limit=28 * 2**20)
    keys_values, w_out = together((keys_values, w_out))
    w_all = spread({0: w_out}, 1)
    expo, peak = exponentials(pattern, other_pattern, queries, keys_values)
    w_all, peak = together((w_all, peak))
    for bits in range(2, chips.bit_length()):
        w_all = spread(w_all, bits)
    w_all = [w_all[k] for k in range(chips)]

    groups = [list(range(chips // 2, chips)), list(range(chips // 2))]
    ranks = [
        sweep(False, ks, place, pattern, panel, columns, follow, 24 * 2**20)
        for ks, follow in zip(groups, [[peak], [peak, *w_all[1:]]], strict=True)
    ]
    others = [along_col(x, 1) for x in ranks]
    parts, follows = [None] * chips, [ranks[1]]
    cuts = [(0, n, n + 1) for n in reversed(range(len(groups[0])))] + [(1, 0, len(groups[1]))]
    for g, begin, end in cuts:
        ks = groups[g][begin:end]
        sums = weigh(
            root, chips, ks, begin, place, bias_gain, bias_rate, ranks[g], others[g], expo,
            keys_values, peak, follows,
        )
        for k, part in zip(ks, sums, strict=False):
            parts[k] = part if k == 0 else along_col(part, CORES * k)
        follows = [sums[0]]
    attended = divide(parts)
    mixed = project_out(place, attended, along_col(attended, 1), w_all)
    mixed = [x if k == 0 else along_col(x, CORES * k) for k, x in enumerate(mixed)]
    for bit in range(chips.bit_length() - 1):
        turned = chip >> bit & 1 == 1
        mixed = [jnp.where(turned, mixed[k ^ 1 << bit], mixed[k]) for k in range(chips)]
    return jnp.concatenate(mixed, axis=0)


def solution(mesh):
    in_specs = (P("row", None), P("row", "col"), P("row", "col"), P(), P(None, "col"), P(), P())
    out_specs = P("row", "col")
    return jax.shard_map(shards, mesh=mesh, in_specs=in_specs, out_specs=out_specs, check_vma=False)
```

```python
import functools
import math

import jax
import jax.numpy as jnp
from jax import lax
from jax.experimental import pallas as pl
from jax.experimental.pallas import tpu as pltpu
from jax.sharding import PartitionSpec as P

D = 1024
HEADS = 16
BLK = 128
HDIM = 64
CORES = 2
PAIRS = HEADS // 2 // CORES
WIDTH = D // CORES
EXTRA = 4 * PAIRS
LANES = 128
VMEM_LIMIT = 58 * 2**20
SMALL_LIMIT = 16 * 2**20

VMEM = pl.BlockSpec(memory_space=pltpu.VMEM)
SMEM = pl.BlockSpec(memory_space=pltpu.SMEM)
HBM = pl.BlockSpec(memory_space=pltpu.HBM)
BF16 = jnp.bfloat16
F32 = jnp.float32


def params(limit=VMEM_LIMIT):
    return pltpu.CompilerParams(vmem_limit_bytes=limit)


def cost(flops, nbytes, trans=0):
    return pl.CostEstimate(flops=int(flops), bytes_accessed=int(nbytes), transcendentals=int(trans))


def xor_pairs(n, j):
    return [(i, i ^ j) for i in range(n)]


def keep_tile(pattern_ref, first_row, block_rows):
    block_cols = pattern_ref.shape[0]
    tiles = []
    for i in range(block_rows):
        parts = [
            jnp.full((1, BLK), jnp.where(pattern_ref[b, first_row + i] > 0, 1.0, 0.0), F32)
            for b in range(block_cols)
        ]
        tiles.append(
            jnp.broadcast_to(jnp.concatenate(parts, axis=1), (BLK, block_cols * BLK))
        )
    return jnp.concatenate(tiles, axis=0)


def start_kernel(pattern_ref, weight_ref, features_ref, out_ref, cut_ref, sem):
    cols = cut_ref.shape[0]
    ratio = features_ref.shape[0] // cols
    at = pl.multiple_of(lax.rem(lax.axis_index("col"), ratio) * cols, cols)
    copy = pltpu.make_async_copy(features_ref.at[pl.ds(at, cols), :], cut_ref, sem)
    copy.start()
    for i in range(out_ref.shape[0] // BLK):
        at = slice(i * BLK, (i + 1) * BLK)
        keep = keep_tile(pattern_ref, i, 1)
        out_ref[at, :] = jnp.where(keep > 0, weight_ref[at, :].astype(F32), 0.0).astype(BF16)
    copy.wait()


def start(pattern, weight, features):
    rows, cols = weight.shape
    return pl.pallas_call(
        start_kernel,
        out_shape=(
            jax.ShapeDtypeStruct((rows, cols), BF16),
            jax.ShapeDtypeStruct((cols, features.shape[1]), BF16),
        ),
        in_specs=[SMEM, VMEM, HBM],
        out_specs=(VMEM, VMEM),
        scratch_shapes=[pltpu.SemaphoreType.DMA],
        compiler_params=params(),
        cost_estimate=cost(rows * cols, 4 * rows * cols),
        name="start",
    )(pattern, weight, features)


def project_in_kernel(scale, place_ref, *refs):
    xs, (w_ref, out_ref) = refs[:-2], refs[-2:]
    rows = xs[0].shape[0]
    for i, x_ref in enumerate(xs):
        out = jnp.dot(x_ref[...], w_ref[...], preferred_element_type=F32).astype(BF16)
        if scale is not None:
            out = out * jnp.asarray(scale, BF16)
        out_ref[i * rows : (i + 1) * rows, :] = out


def project_in(core, xs, w, firsts, scale=None, tile=256, limit=VMEM_LIMIT):
    rows, depth = xs[0].shape
    steps = WIDTH // tile

    def column(i, core_ref):
        first = firsts[0] // tile
        for n, start in enumerate(firsts[1:], 1):
            first = jnp.where(i >= n * steps, start // tile, first)
        return 0, first + core_ref[0] * steps + lax.rem(i, steps)

    return pl.pallas_call(
        functools.partial(project_in_kernel, scale),
        out_shape=jax.ShapeDtypeStruct((rows * len(xs), WIDTH * len(firsts)), BF16),
        grid_spec=pltpu.PrefetchScalarGridSpec(
            num_scalar_prefetch=1,
            grid=(steps * len(firsts),),
            in_specs=[pl.BlockSpec((rows, depth), lambda i, c: (0, 0))] * len(xs)
            + [pl.BlockSpec((depth, tile), column)],
            out_specs=pl.BlockSpec((rows * len(xs), tile), lambda i, c: (0, i)),
        ),
        compiler_params=params(limit),
        cost_estimate=cost(
            2 * rows * len(xs) * depth * WIDTH * len(firsts),
            2 * depth * (rows * len(xs) + WIDTH * len(firsts)),
        ),
        name="project_in",
    )(core, *xs, w)


def sweep_kernel(first, ks, chips, left_at, right_at, place_ref, pattern_ref, *refs):
    n_right = len(right_at)
    panel, rights = refs[: len(left_at)], refs[len(left_at) : len(left_at) + n_right]
    out_ref, left_ref, right_ref, acc_ref, left_sem, right_sem = refs[-6:]
    rows, cols = panel[0].shape[-2:]
    seg = rows // chips
    row_pos, col_pos = place_ref[0], place_ref[1]
    chip, core = lax.div(col_pos, CORES), lax.rem(col_pos, CORES)
    starts = [pl.multiple_of(lax.bitwise_xor(chip, k) * seg, seg) for k in ks]
    if len(ks) == chips:
        starts, seg = [0], rows

    part = min(ref.shape[0] for ref in rights)

    def right_copies(i, slot):
        xor, offset = right_at[i]
        for at in range(0, rights[i].shape[0], part):
            target = right_ref.at[slot, pl.ds(offset + at, part), :]
            source = rights[i].at[pl.ds(at, part), :]
            yield pltpu.make_async_copy(source, target, right_sem.at[slot, (offset + at) // part])

    def left_copies(k):
        for ref, (j, index) in zip(panel, left_at, strict=True):
            if j // CORES != k:
                continue
            block = ref if index is None else ref.at[index]
            at = pl.multiple_of(lax.bitwise_xor(core, j % CORES) * cols, cols)
            for n, start in enumerate(starts):
                yield pltpu.make_async_copy(
                    block.at[pl.ds(start, seg), :],
                    left_ref.at[k, pl.ds(n * seg, seg), pl.ds(at, cols)],
                    left_sem.at[k, j % CORES * len(starts) + n],
                )

    for k in range(chips):
        for copy in left_copies(k):
            copy.start()
        for xor in sorted({at[0] for at in right_at}):

            @pl.when(lax.bitwise_xor(row_pos, chip) == xor ^ k)
            def _():
                for i in range(n_right):
                    if right_at[i][0] == xor:
                        for copy in right_copies(i, k):
                            copy.start()

    for k in range(chips):
        for at in range(0, rows, part):
            half = right_ref.at[k, pl.ds(at, part), :]
            pltpu.make_async_copy(half, half, right_sem.at[k, at // part]).wait()
        for copy in left_copies(k):
            copy.wait()
        product = jnp.dot(left_ref[k], right_ref[k], preferred_element_type=F32)
        if k == 0:
            acc_ref[...] = product
        elif k < chips - 1:
            acc_ref[...] += product
    product = product + acc_ref[...]
    own = left_ref[0, :, pl.ds(pl.multiple_of(core * cols, cols), cols)].astype(F32)
    total = 0.1275 * own + (0.85 * 0.1275 if first else 0.85) * product
    diagonal = lax.broadcasted_iota(jnp.int32, (seg, cols), 1) - lax.broadcasted_iota(
        jnp.int32, (seg, cols), 0
    )
    lane_block = lax.broadcasted_iota(jnp.int32, (1, cols), 1) // BLK
    for n, start in enumerate(starts):
        at = slice(n * seg, (n + 1) * seg)
        part = total[at, :]
        if not first:
            here = diagonal == row_pos * rows + start - col_pos * cols
            part = jnp.where(here, part + 0.15, part)
        size = math.gcd(seg, BLK)
        for i in range(seg // size):
            keep = jnp.zeros((1, cols), F32)
            for b in range(cols // BLK):
                kept = pattern_ref[b, lax.div(start + i * size, BLK)] > 0
                keep = jnp.where(lane_block == b, jnp.where(kept, 1.0, 0.0), keep)
            piece = part[i * size : (i + 1) * size, :]
            out_ref[n * seg + i * size : n * seg + (i + 1) * size, :] = jnp.where(
                keep > 0, piece, 0.0
            ).astype(BF16)


def sweep(first, ks, place, pattern, panel, blocks, follows, limit=VMEM_LIMIT):
    rows, cols = panel[0][0].shape[-2:]
    chips = len(panel) // CORES
    n_rows = rows // chips * len(ks)
    depth = len(panel) * cols
    return pl.pallas_call(
        functools.partial(
            sweep_kernel,
            first,
            ks,
            chips,
            [at for _, *at in panel],
            [(j, at) for j, at, _ in blocks],
        ),
        out_shape=jax.ShapeDtypeStruct((n_rows, cols), BF16),
        in_specs=[SMEM, SMEM] + [HBM] * (len(panel) + len(blocks) + len(follows)),
        out_specs=VMEM,
        scratch_shapes=[
            pltpu.VMEM((chips, n_rows, CORES * cols), BF16),
            pltpu.VMEM((depth // rows, rows, cols), BF16),
            pltpu.VMEM((n_rows, cols), F32),
            pltpu.SemaphoreType.DMA((chips, CORES * len(ks))),
            pltpu.SemaphoreType.DMA((chips, rows // min(x.shape[0] for *_, x in blocks))),
        ],
        compiler_params=params(limit),
        cost_estimate=cost(2 * n_rows * depth * cols, 2 * (n_rows + rows) * depth),
        name="rank_sweep",
    )(place, pattern, *[x for x, *_ in panel], *[x for *_, x in blocks], *follows)


def split_heads(keys):
    lane = lax.broadcasted_iota(jnp.int32, keys.shape, 1)
    zero = jnp.zeros_like(keys)
    return jnp.concatenate(
        [jnp.where(lane < HDIM, keys, zero), jnp.where(lane >= HDIM, keys, zero)], axis=0
    )


def expo_kernel(own_ref, other_ref, q_ref, k_ref, out_ref, peak_ref, mask_ref):
    p = pl.program_id(0)
    rows, keys = q_ref.shape[0], k_ref.shape[0]
    block_rows, block_cols = rows // BLK, keys // BLK
    tile = BLK

    @pl.when(p == 0)
    def _():
        lane = lax.broadcasted_iota(jnp.int32, (BLK, LANES), 1)
        for i in range(block_rows):
            excluded = jnp.zeros((BLK, LANES), F32)
            for b in range(block_cols):
                ref, at = (own_ref, b) if b < block_cols // 2 else (other_ref, b - block_cols // 2)
                excluded = jnp.where(lane == b, jnp.where(ref[at, i] > 0, 0.0, -1e30), excluded)
            mask_ref[i * BLK : (i + 1) * BLK, :] = excluded.astype(BF16)
        peak_ref[...] = jnp.zeros_like(peak_ref)

    lane = lax.broadcasted_iota(jnp.int32, (2 * keys, LANES), 1)
    key = lax.broadcasted_iota(jnp.int32, (2 * keys, LANES), 0)
    block_of = jnp.where(key >= keys, key - keys, key) // BLK
    in_block = jnp.where(lane == block_of, 1.0, 0.0).astype(BF16)
    right = jnp.concatenate([split_heads(k_ref[...]), in_block], axis=1)
    peak_lane = lax.broadcasted_iota(jnp.int32, (tile, LANES), 1)
    for t in range(rows // tile):
        at = slice(t * tile, (t + 1) * tile)
        left = jnp.concatenate([q_ref[at, :], mask_ref[at, :]], axis=1)
        s = lax.dot_general(left, right, (((1,), (1,)), ((), ())), preferred_element_type=F32)
        peaks = peak_ref[at, :]
        for side in range(2):
            part = s[:, side * keys : (side + 1) * keys]
            peak = jnp.max(part, axis=1, keepdims=True)
            peaks = jnp.where(peak_lane == HDIM * side + p, peak, peaks)
            out_ref[0, at, side * keys : (side + 1) * keys] = jnp.exp(part - peak).astype(BF16)
        peak_ref[at, :] = peaks


def exponentials(own, other, queries, keys_values):
    rows, keys = queries.shape[0], keys_values.shape[0]
    work = rows * keys * 2 * PAIRS
    return pl.pallas_call(
        expo_kernel,
        out_shape=(
            jax.ShapeDtypeStruct((PAIRS, rows, 2 * keys), BF16),
            jax.ShapeDtypeStruct((rows, LANES), F32),
        ),
        grid=(PAIRS,),
        in_specs=[
            SMEM,
            SMEM,
            pl.BlockSpec((rows, LANES), lambda p: (0, p)),
            pl.BlockSpec((keys, LANES), lambda p: (0, p)),
        ],
        out_specs=(
            pl.BlockSpec((1, rows, 2 * keys), lambda p: (p, 0, 0)),
            pl.BlockSpec((rows, LANES), lambda p: (0, 0)),
        ),
        scratch_shapes=[pltpu.VMEM((rows, LANES), BF16)],
        compiler_params=params(28 * 2**20),
        cost_estimate=cost(512 * work, 2 * work, work),
        name="expo",
    )(own, other, queries, keys_values)


def weigh_kernel(
    root, ks, seg, place_ref, gain_ref, rate_ref, own_ref, other_ref, expo_ref, v_ref, peak_ref,
    *refs,
):
    out_refs, (p_ref, ranks_ref, right_ref) = refs[-3 - len(ks) : -3], refs[-3:]
    cols = own_ref.shape[1]
    keys = 2 * cols
    chip = lax.div(place_ref[1], CORES)
    first_head = lax.rem(place_ref[1], CORES) * 2 * PAIRS
    starts = [pl.multiple_of(lax.bitwise_xor(chip, k) * seg, seg) for k in ks]

    for i in range(len(ks)):
        at = slice(i * seg, (i + 1) * seg)
        ranks_ref[at, :cols] = own_ref[at, :].astype(F32)
        ranks_ref[at, cols:] = other_ref[at, :].astype(F32)
    lane = lax.broadcasted_iota(jnp.int32, (keys, LANES), 1)
    zero = jnp.zeros((keys, LANES), BF16)
    right_ref[:keys, LANES:] = jnp.where(lane < HDIM, 1.0, 0.0).astype(BF16)
    right_ref[keys:, LANES:] = jnp.where(lane < HDIM, 0.0, 1.0).astype(BF16)
    out_lane = lax.broadcasted_iota(jnp.int32, (seg, LANES), 1)

    def pair(p, totals):
        lanes = pl.ds(pl.multiple_of(p * LANES, LANES), LANES)
        values = v_ref[:, lanes]
        right_ref[:keys, :LANES] = jnp.where(lane < HDIM, values, zero)
        right_ref[keys:, :LANES] = jnp.where(lane < HDIM, zero, values)
        for i in range(len(ks)):
            rows_at = slice(i * seg, (i + 1) * seg)
            for half in range(2):
                ranks = ranks_ref[rows_at, half * cols : (half + 1) * cols]
                for side in range(2):
                    rate = rate_ref[first_head + 2 * p + side] * root
                    gain = gain_ref[first_head + 2 * p + side] * math.log2(math.e)
                    at = slice(side * keys + half * cols, side * keys + (half + 1) * cols)
                    weight = expo_ref[p, pl.ds(starts[i], seg), at].astype(F32) * jnp.exp2(
                        gain * jnp.tanh(rate * ranks)
                    )
                    p_ref[rows_at, at] = weight.astype(BF16)
        sums = jnp.dot(p_ref[...], right_ref[...], preferred_element_type=F32)
        now = []
        for i, out_ref in enumerate(out_refs):
            part = sums[i * seg : (i + 1) * seg, :]
            out_ref[:seg, lanes] = part[:, :LANES].astype(BF16)
            now.append(jnp.where(out_lane % HDIM == p, part[:, LANES:], totals[i]))
        return tuple(now)

    totals = lax.fori_loop(
        0, PAIRS, pair, tuple(jnp.zeros((seg, LANES), F32) for _ in ks)
    )
    half = WIDTH // 2
    for i, out_ref in enumerate(out_refs):
        extra = totals[i]
        rest = peak_ref[pl.ds(starts[i], seg), :]
        for n in range(1, 4):
            piece = rest.astype(BF16).astype(F32)
            rest = rest - piece
            here = (out_lane % HDIM >= n * PAIRS) & (out_lane % HDIM < (n + 1) * PAIRS)
            extra = jnp.where(here, pltpu.roll(piece, n * PAIRS, 1), extra)
        extra = jnp.concatenate([extra, jnp.zeros((half - seg, LANES), F32)], axis=0).T
        for side in range(2):
            out_ref[seg:, side * half : (side + 1) * half] = extra[
                side * HDIM : side * HDIM + EXTRA
            ].astype(BF16)


def weigh(root, chips, ks, first, place, gain, rate, own, other, expo, values, peak, follows):
    (_, rows, _), cols = expo.shape, own.shape[1]
    seg = rows // chips
    n_rows, keys = seg * len(ks), 2 * cols
    part = pl.BlockSpec((n_rows, cols), lambda i: (first // len(ks), 0))
    work = n_rows * keys * 2 * PAIRS
    return pl.pallas_call(
        functools.partial(weigh_kernel, root, ks, seg),
        out_shape=(jax.ShapeDtypeStruct((seg + EXTRA, WIDTH), BF16),) * len(ks),
        grid=(1,),
        in_specs=[
            SMEM,
            SMEM,
            SMEM,
            part,
            part,
            VMEM,
            pl.BlockSpec((keys, WIDTH), lambda i: (0, 1)),
            pl.BlockSpec((rows, LANES), lambda i: (0, 0)),
            *[HBM] * len(follows),
        ],
        out_specs=(pl.BlockSpec((seg + EXTRA, WIDTH), lambda i: (0, 0)),) * len(ks),
        scratch_shapes=[
            pltpu.VMEM((n_rows, 2 * keys), BF16),
            pltpu.VMEM((n_rows, keys), F32),
            pltpu.VMEM((2 * keys, 2 * LANES), BF16),
        ],
        compiler_params=params(28 * 2**20),
        cost_estimate=cost(512 * work, 2 * work, 2 * work),
        name="weigh",
    )(place, gain, rate, own, other, expo, values, peak, *follows)


def divide_kernel(*refs):
    parts, out_ref = refs[:-1], refs[-1]
    seg, half = out_ref.shape[0], WIDTH // 2
    lane = lax.broadcasted_iota(jnp.int32, (seg, LANES), 1)
    fit = LANES // (2 * EXTRA)
    totals, peaks, largest = [], [], None
    for first in range(0, len(parts), fit):
        group = parts[first : first + fit]
        extra = [
            part[seg:, side * half : (side + 1) * half].astype(F32)
            for part in group
            for side in range(2)
        ]
        spare = LANES - EXTRA * len(extra)
        if spare:
            extra.append(jnp.zeros((spare, half), F32))
        extra = jnp.concatenate(extra, axis=0).T[:seg]
        totals.append(extra)
        peak = sum(pltpu.roll(extra, LANES - n * PAIRS, 1) for n in range(1, 4))
        if spare:
            peak = jnp.where(lane < LANES - spare, peak, -jnp.inf)
        peaks.append(peak)
        largest = peak if largest is None else jnp.maximum(largest, peak)

    def over_parts(value, combine):
        step = 2 * EXTRA
        while step < LANES:
            value = combine(value, pltpu.roll(value, step, 1))
            step *= 2
        return value

    largest = over_parts(largest, jnp.maximum)
    weights = [jnp.exp(peak - largest) for peak in peaks]
    inverse = 1.0 / over_parts(
        sum(w * x for w, x in zip(weights, totals, strict=True)), lambda x, y: x + y
    )
    scales = [w * inverse for w in weights]
    for p in range(PAIRS):
        lanes = slice(p * LANES, (p + 1) * LANES)
        total = jnp.zeros((seg, LANES), F32)
        for i, part in enumerate(parts):
            at = i % fit * 2 * EXTRA + p
            scale = scales[i // fit]
            both = jnp.where(
                lane < HDIM, scale[:, at : at + 1], scale[:, at + EXTRA : at + EXTRA + 1]
            )
            total += part[:seg, lanes].astype(F32) * both
        out_ref[:, lanes] = total.astype(BF16)


def divide(parts):
    seg = parts[0].shape[0] - EXTRA
    return pl.pallas_call(
        divide_kernel,
        out_shape=jax.ShapeDtypeStruct((seg, WIDTH), BF16),
        in_specs=[VMEM] * len(parts),
        out_specs=VMEM,
        compiler_params=params(SMALL_LIMIT),
        cost_estimate=cost(8 * seg * D, 8 * seg * D),
        name="divide",
    )(*parts)


def project_out_kernel(place_ref, own_ref, other_ref, *refs):
    n = len(refs) // 2
    core = lax.rem(place_ref[1], CORES)
    mine = pl.ds(pl.multiple_of(core * WIDTH, WIDTH), WIDTH)
    others = pl.ds(pl.multiple_of((1 - core) * WIDTH, WIDTH), WIDTH)
    for w_ref, out_ref in zip(refs[:n], refs[n:], strict=True):
        total = jnp.dot(own_ref[...], w_ref[mine, :], preferred_element_type=F32)
        total += jnp.dot(other_ref[...], w_ref[others, :], preferred_element_type=F32)
        out_ref[...] = total.astype(BF16)


def project_out(place, own, other, w_all):
    seg, (depth, width) = own.shape[0], w_all[0].shape
    chips = len(w_all)
    return pl.pallas_call(
        project_out_kernel,
        out_shape=(jax.ShapeDtypeStruct((seg, width), BF16),) * chips,
        in_specs=[SMEM] + [VMEM] * (2 + chips),
        out_specs=(VMEM,) * chips,
        compiler_params=params(SMALL_LIMIT),
        cost_estimate=cost(2 * seg * depth * width * chips, 2 * depth * width * chips),
        name="project_out",
    )(place, own, other, *w_all)


def shards(node_features, edge_weight, pattern, w_qkv, w_out, bias_gain, bias_rate):
    rows, cols = edge_weight.shape
    row_count, col_count = lax.axis_size("row"), lax.axis_size("col")
    row_pos, col_pos = lax.axis_index("row"), lax.axis_index("col")
    ratio = rows // cols
    chips = col_count // CORES
    chip = col_pos // CORES
    root = math.sqrt(rows * row_count)
    place = jnp.stack([row_pos, col_pos]).astype(jnp.int32)
    core = (col_pos % CORES).astype(jnp.int32).reshape(1)
    pattern = pattern.T
    together = lax.optimization_barrier

    def along_col(value, j):
        return lax.ppermute(value, "col", xor_pairs(col_count, j))

    def along_row(value, j):
        return lax.ppermute(value, "row", xor_pairs(row_count, j))

    def from_rows(value):
        return [value] + [along_row(value, j) for j in range(1, row_count)]

    def spread(blocks, bits):
        new = dict(blocks)
        for k in range(chips - 1, 0, -1):
            if k.bit_count() == bits:
                low = k & -k
                new[k] = along_col(blocks[k ^ low], CORES * low)
        return new

    ring = [0, 1, 3, 2] if row_count == 4 else list(range(row_count))
    def place_of(r):
        return r ^ (r >> 1) if row_count == 4 else r

    steps_away = (
        (place_of(row_pos) - place_of(col_pos // ratio)) * (1 - 2 * (col_pos % CORES))
    ) % row_count

    def feature_step(value, s):
        pairs = []
        for c in range(col_count):
            way = 1 - 2 * (c % CORES)
            i = ring.index(c // ratio) + way * (s - 1)
            here, there = ring[i % row_count], ring[(i + way) % row_count]
            pairs.append((here * col_count + c, there * col_count + c))
        return lax.ppermute(value, ("row", "col"), pairs)

    adjacency, features = start(pattern, edge_weight, node_features)
    blocks = spread({0: adjacency}, 1)
    near = [1, 2] if row_count == 4 else list(range(1, row_count))
    columns = {j: along_row(adjacency, j) for j in near}
    other_pattern = along_col(pattern, 1)
    queries = project_in(core, [node_features], w_qkv, [0], 1.0 / math.sqrt(HDIM))
    moved = [features, feature_step(features, 1)]
    raw_columns = columns
    queries, moved, columns, blocks = together((queries, moved, columns, blocks))

    order = sorted(blocks)
    swapped = along_col(jnp.stack([blocks[k] for k in order]), 1)
    far = []
    if row_count == 4:
        half = rows // 2
        far = [along_row(columns[2][:half], 1), along_row(columns[1][half:], 2)]
    moved.append(feature_step(moved[-1], 2))
    for bits in range(2, chips.bit_length()):
        blocks = spread(blocks, bits)
    raw_far = far
    far, swapped, blocks = together((far, swapped, blocks))
    for s in range(3, row_count):
        moved.append(feature_step(moved[-1], s))
    panel = [(x, CORES * k, None) for k, x in blocks.items()]
    panel += [(swapped, CORES * k + 1, i) for i, k in enumerate(order)]
    panel += [(along_col(x, 1), CORES * k + 1, None) for k, x in blocks.items() if k not in order]
    columns = [(0, 0, adjacency)] + [(j, 0, x) for j, x in raw_columns.items()]
    columns += [(3, i * x.shape[0], x) for i, x in enumerate(raw_far)]
    key_rows = features
    for s in range(1, row_count - 1):
        key_rows = jnp.where(steps_away == s, moved[s], key_rows)
    ranks = sweep(True, range(chips), place, pattern, panel, columns, [key_rows], 50 * 2**20)
    columns = [(j, 0, x) for j, x in enumerate(from_rows(ranks))]

    ranks, last = together((ranks, moved[-1]))
    key_rows = jnp.where(steps_away == row_count - 1, last, key_rows)
    keys_values = project_in(core, [key_rows, along_col(key_rows, 1)], w_qkv, [D, 2 * D], limit=28 * 2**20)
    keys_values, w_out = together((keys_values, w_out))
    w_all = spread({0: w_out}, 1)
    expo, peak = exponentials(pattern, other_pattern, queries, keys_values)
    w_all, peak = together((w_all, peak))
    for bits in range(2, chips.bit_length()):
        w_all = spread(w_all, bits)
    w_all = [w_all[k] for k in range(chips)]

    groups = [list(range(chips // 2, chips)), list(range(chips // 2))]
    ranks = [
        sweep(False, ks, place, pattern, panel, columns, follow, 24 * 2**20)
        for ks, follow in zip(groups, [[peak], [peak, *w_all[1:]]], strict=True)
    ]
    others = [along_col(x, 1) for x in ranks]
    parts, follows = [None] * chips, [ranks[1]]
    cuts = [(0, n, n + 1) for n in reversed(range(len(groups[0])))] + [(1, 0, len(groups[1]))]
    for g, begin, end in cuts:
        ks = groups[g][begin:end]
        sums = weigh(
            root, chips, ks, begin, place, bias_gain, bias_rate, ranks[g], others[g], expo,
            keys_values, peak, follows,
        )
        for k, part in zip(ks, sums, strict=False):
            parts[k] = part if k == 0 else along_col(part, CORES * k)
        follows = [sums[0]]
    attended = divide(parts)
    mixed = project_out(place, attended, along_col(attended, 1), w_all)
    mixed = [x if k == 0 else along_col(x, CORES * k) for k, x in enumerate(mixed)]
    for bit in range(chips.bit_length() - 1):
        turned = chip >> bit & 1 == 1
        mixed = [jnp.where(turned, mixed[k ^ 1 << bit], mixed[k]) for k in range(chips)]
    return jnp.concatenate(mixed, axis=0)


def solution(mesh):
    in_specs = (P("row", None), P("row", "col"), P("row", "col"), P(), P(None, "col"), P(), P())
    out_specs = P("row", "col")
    return jax.shard_map(shards, mesh=mesh, in_specs=in_specs, out_specs=out_specs, check_vma=False)
```

```python
import functools
import math

import jax
import jax.numpy as jnp
from jax import lax
from jax.experimental import pallas as pl
from jax.experimental.pallas import tpu as pltpu
from jax.sharding import PartitionSpec as P

D = 1024
HEADS = 16
BLK = 128
HDIM = 64
CORES = 2
PAIRS = HEADS // 2 // CORES
WIDTH = D // CORES
EXTRA = 4 * PAIRS
LANES = 128
VMEM_LIMIT = 58 * 2**20
SMALL_LIMIT = 16 * 2**20

VMEM = pl.BlockSpec(memory_space=pltpu.VMEM)
SMEM = pl.BlockSpec(memory_space=pltpu.SMEM)
HBM = pl.BlockSpec(memory_space=pltpu.HBM)
BF16 = jnp.bfloat16
F32 = jnp.float32


def params(limit=VMEM_LIMIT):
    return pltpu.CompilerParams(vmem_limit_bytes=limit)


def cost(flops, nbytes, trans=0):
    return pl.CostEstimate(flops=int(flops), bytes_accessed=int(nbytes), transcendentals=int(trans))


def xor_pairs(n, j):
    return [(i, i ^ j) for i in range(n)]


def keep_tile(pattern_ref, first_row, block_rows):
    block_cols = pattern_ref.shape[0]
    tiles = []
    for i in range(block_rows):
        parts = [
            jnp.full((1, BLK), jnp.where(pattern_ref[b, first_row + i] > 0, 1.0, 0.0), F32)
            for b in range(block_cols)
        ]
        tiles.append(
            jnp.broadcast_to(jnp.concatenate(parts, axis=1), (BLK, block_cols * BLK))
        )
    return jnp.concatenate(tiles, axis=0)


def start_kernel(pattern_ref, weight_ref, features_ref, out_ref, cut_ref, kept_ref, held_ref, sem):
    cols = cut_ref.shape[0]
    rows = out_ref.shape[0] // 2
    ratio = features_ref.shape[0] // cols
    at = pl.multiple_of(lax.rem(lax.axis_index("col"), ratio) * cols, cols)
    halves = [slice(h * rows, (h + 1) * rows) for h in range(2)]
    come = [
        pltpu.make_async_copy(weight_ref.at[x, :], kept_ref.at[x, :], sem.at[h])
        for h, x in enumerate(halves)
    ]
    go = [
        pltpu.make_async_copy(kept_ref.at[x, :], out_ref.at[x, :], sem.at[2 + h])
        for h, x in enumerate(halves)
    ]
    cut_in = pltpu.make_async_copy(features_ref.at[pl.ds(at, cols), :], held_ref, sem.at[4])
    cut_out = pltpu.make_async_copy(held_ref, cut_ref, sem.at[5])
    for copy in (*come, cut_in):
        copy.start()
    for h in range(2):
        come[h].wait()
        for i in range(h * rows // BLK, (h + 1) * rows // BLK):
            x = slice(i * BLK, (i + 1) * BLK)
            keep = keep_tile(pattern_ref, i, 1)
            kept_ref[x, :] = jnp.where(keep > 0, kept_ref[x, :].astype(F32), 0.0).astype(BF16)
        go[h].start()
        if h == 0:
            cut_in.wait()
            cut_out.start()
    for copy in (*go, cut_out):
        copy.wait()


def start(pattern, weight, features):
    rows, cols = weight.shape
    depth = features.shape[1]
    return pl.pallas_call(
        start_kernel,
        out_shape=(
            jax.ShapeDtypeStruct((rows, cols), BF16),
            jax.ShapeDtypeStruct((cols, depth), BF16),
        ),
        in_specs=[SMEM, HBM, HBM],
        out_specs=(HBM, HBM),
        scratch_shapes=[
            pltpu.VMEM((rows, cols), BF16),
            pltpu.VMEM((cols, depth), BF16),
            pltpu.SemaphoreType.DMA((6,)),
        ],
        compiler_params=params(),
        cost_estimate=cost(rows * cols, 4 * rows * cols),
        name="start",
    )(pattern, weight, features)


def project_in_kernel(scale, place_ref, *refs):
    xs, (w_ref, out_ref) = refs[:-2], refs[-2:]
    rows = xs[0].shape[0]
    for i, x_ref in enumerate(xs):
        out = jnp.dot(x_ref[...], w_ref[...], preferred_element_type=F32).astype(BF16)
        if scale is not None:
            out = out * jnp.asarray(scale, BF16)
        out_ref[i * rows : (i + 1) * rows, :] = out


def project_in(core, xs, w, firsts, scale=None, tile=256, limit=VMEM_LIMIT):
    rows, depth = xs[0].shape
    steps = WIDTH // tile

    def column(i, core_ref):
        first = firsts[0] // tile
        for n, start in enumerate(firsts[1:], 1):
            first = jnp.where(i >= n * steps, start // tile, first)
        return 0, first + core_ref[0] * steps + lax.rem(i, steps)

    return pl.pallas_call(
        functools.partial(project_in_kernel, scale),
        out_shape=jax.ShapeDtypeStruct((rows * len(xs), WIDTH * len(firsts)), BF16),
        grid_spec=pltpu.PrefetchScalarGridSpec(
            num_scalar_prefetch=1,
            grid=(steps * len(firsts),),
            in_specs=[pl.BlockSpec((rows, depth), lambda i, c: (0, 0))] * len(xs)
            + [pl.BlockSpec((depth, tile), column)],
            out_specs=pl.BlockSpec((rows * len(xs), tile), lambda i, c: (0, i)),
        ),
        compiler_params=params(limit),
        cost_estimate=cost(
            2 * rows * len(xs) * depth * WIDTH * len(firsts),
            2 * depth * (rows * len(xs) + WIDTH * len(firsts)),
        ),
        name="project_in",
    )(core, *xs, w)


def sweep_kernel(first, ks, chips, left_at, right_at, place_ref, pattern_ref, *refs):
    n_right = len(right_at)
    panel, rights = refs[: len(left_at)], refs[len(left_at) : len(left_at) + n_right]
    out_ref, left_ref, right_ref, acc_ref, left_sem, right_sem = refs[-6:]
    rows, cols = panel[0].shape[-2:]
    seg = rows // chips
    row_pos, col_pos = place_ref[0], place_ref[1]
    chip, core = lax.div(col_pos, CORES), lax.rem(col_pos, CORES)
    starts = [pl.multiple_of(lax.bitwise_xor(chip, k) * seg, seg) for k in ks]
    if len(ks) == chips:
        starts, seg = [0], rows

    part = min(ref.shape[0] for ref in rights)

    def right_copies(i, slot):
        xor, offset = right_at[i]
        for at in range(0, rights[i].shape[0], part):
            target = right_ref.at[slot, pl.ds(offset + at, part), :]
            source = rights[i].at[pl.ds(at, part), :]
            yield pltpu.make_async_copy(source, target, right_sem.at[slot, (offset + at) // part])

    def left_copies(k):
        for ref, (j, index) in zip(panel, left_at, strict=True):
            if j // CORES != k:
                continue
            block = ref if index is None else ref.at[index]
            at = pl.multiple_of(lax.bitwise_xor(core, j % CORES) * cols, cols)
            for n, start in enumerate(starts):
                yield pltpu.make_async_copy(
                    block.at[pl.ds(start, seg), :],
                    left_ref.at[k, pl.ds(n * seg, seg), pl.ds(at, cols)],
                    left_sem.at[k, j % CORES * len(starts) + n],
                )

    for k in range(chips):
        for copy in left_copies(k):
            copy.start()
        for xor in sorted({at[0] for at in right_at}):

            @pl.when(lax.bitwise_xor(row_pos, chip) == xor ^ k)
            def _():
                for i in range(n_right):
                    if right_at[i][0] == xor:
                        for copy in right_copies(i, k):
                            copy.start()

    for k in range(chips):
        for at in range(0, rows, part):
            half = right_ref.at[k, pl.ds(at, part), :]
            pltpu.make_async_copy(half, half, right_sem.at[k, at // part]).wait()
        for copy in left_copies(k):
            copy.wait()
        product = jnp.dot(left_ref[k], right_ref[k], preferred_element_type=F32)
        if k == 0:
            acc_ref[...] = product
        elif k < chips - 1:
            acc_ref[...] += product
    product = product + acc_ref[...]
    own = left_ref[0, :, pl.ds(pl.multiple_of(core * cols, cols), cols)].astype(F32)
    total = 0.1275 * own + (0.85 * 0.1275 if first else 0.85) * product
    diagonal = lax.broadcasted_iota(jnp.int32, (seg, cols), 1) - lax.broadcasted_iota(
        jnp.int32, (seg, cols), 0
    )
    lane_block = lax.broadcasted_iota(jnp.int32, (1, cols), 1) // BLK
    for n, start in enumerate(starts):
        at = slice(n * seg, (n + 1) * seg)
        part = total[at, :]
        if not first:
            here = diagonal == row_pos * rows + start - col_pos * cols
            part = jnp.where(here, part + 0.15, part)
        size = math.gcd(seg, BLK)
        for i in range(seg // size):
            keep = jnp.zeros((1, cols), F32)
            for b in range(cols // BLK):
                kept = pattern_ref[b, lax.div(start + i * size, BLK)] > 0
                keep = jnp.where(lane_block == b, jnp.where(kept, 1.0, 0.0), keep)
            piece = part[i * size : (i + 1) * size, :]
            out_ref[n * seg + i * size : n * seg + (i + 1) * size, :] = jnp.where(
                keep > 0, piece, 0.0
            ).astype(BF16)


def sweep(first, ks, place, pattern, panel, blocks, follows, limit=VMEM_LIMIT):
    rows, cols = panel[0][0].shape[-2:]
    chips = len(panel) // CORES
    n_rows = rows // chips * len(ks)
    depth = len(panel) * cols
    return pl.pallas_call(
        functools.partial(
            sweep_kernel,
            first,
            ks,
            chips,
            [at for _, *at in panel],
            [(j, at) for j, at, _ in blocks],
        ),
        out_shape=jax.ShapeDtypeStruct((n_rows, cols), BF16),
        in_specs=[SMEM, SMEM] + [HBM] * (len(panel) + len(blocks) + len(follows)),
        out_specs=VMEM,
        scratch_shapes=[
            pltpu.VMEM((chips, n_rows, CORES * cols), BF16),
            pltpu.VMEM((depth // rows, rows, cols), BF16),
            pltpu.VMEM((n_rows, cols), F32),
            pltpu.SemaphoreType.DMA((chips, CORES * len(ks))),
            pltpu.SemaphoreType.DMA((chips, rows // min(x.shape[0] for *_, x in blocks))),
        ],
        compiler_params=params(limit),
        cost_estimate=cost(2 * n_rows * depth * cols, 2 * (n_rows + rows) * depth),
        name="rank_sweep",
    )(place, pattern, *[x for x, *_ in panel], *[x for *_, x in blocks], *follows)


def split_heads(keys):
    lane = lax.broadcasted_iota(jnp.int32, keys.shape, 1)
    zero = jnp.zeros_like(keys)
    return jnp.concatenate(
        [jnp.where(lane < HDIM, keys, zero), jnp.where(lane >= HDIM, keys, zero)], axis=0
    )


def expo_kernel(own_ref, other_ref, q_ref, k_ref, out_ref, peak_ref, mask_ref):
    p = pl.program_id(0)
    rows, keys = q_ref.shape[0], k_ref.shape[0]
    block_rows, block_cols = rows // BLK, keys // BLK
    tile = BLK

    @pl.when(p == 0)
    def _():
        lane = lax.broadcasted_iota(jnp.int32, (BLK, LANES), 1)
        for i in range(block_rows):
            excluded = jnp.zeros((BLK, LANES), F32)
            for b in range(block_cols):
                ref, at = (own_ref, b) if b < block_cols // 2 else (other_ref, b - block_cols // 2)
                excluded = jnp.where(lane == b, jnp.where(ref[at, i] > 0, 0.0, -1e30), excluded)
            mask_ref[i * BLK : (i + 1) * BLK, :] = excluded.astype(BF16)
        peak_ref[...] = jnp.zeros_like(peak_ref)

    lane = lax.broadcasted_iota(jnp.int32, (2 * keys, LANES), 1)
    key = lax.broadcasted_iota(jnp.int32, (2 * keys, LANES), 0)
    block_of = jnp.where(key >= keys, key - keys, key) // BLK
    in_block = jnp.where(lane == block_of, 1.0, 0.0).astype(BF16)
    right = jnp.concatenate([split_heads(k_ref[...]), in_block], axis=1)
    peak_lane = lax.broadcasted_iota(jnp.int32, (tile, LANES), 1)
    for t in range(rows // tile):
        at = slice(t * tile, (t + 1) * tile)
        left = jnp.concatenate([q_ref[at, :], mask_ref[at, :]], axis=1)
        s = lax.dot_general(left, right, (((1,), (1,)), ((), ())), preferred_element_type=F32)
        peaks = peak_ref[at, :]
        for side in range(2):
            part = s[:, side * keys : (side + 1) * keys]
            peak = jnp.max(part, axis=1, keepdims=True)
            peaks = jnp.where(peak_lane == HDIM * side + p, peak, peaks)
            out_ref[0, at, side * keys : (side + 1) * keys] = jnp.exp(part - peak).astype(BF16)
        peak_ref[at, :] = peaks


def exponentials(own, other, queries, keys_values):
    rows, keys = queries.shape[0], keys_values.shape[0]
    work = rows * keys * 2 * PAIRS
    return pl.pallas_call(
        expo_kernel,
        out_shape=(
            jax.ShapeDtypeStruct((PAIRS, rows, 2 * keys), BF16),
            jax.ShapeDtypeStruct((rows, LANES), F32),
        ),
        grid=(PAIRS,),
        in_specs=[
            SMEM,
            SMEM,
            pl.BlockSpec((rows, LANES), lambda p: (0, p)),
            pl.BlockSpec((keys, LANES), lambda p: (0, p)),
        ],
        out_specs=(
            pl.BlockSpec((1, rows, 2 * keys), lambda p: (p, 0, 0)),
            pl.BlockSpec((rows, LANES), lambda p: (0, 0)),
        ),
        scratch_shapes=[pltpu.VMEM((rows, LANES), BF16)],
        compiler_params=params(28 * 2**20),
        cost_estimate=cost(512 * work, 2 * work, work),
        name="expo",
    )(own, other, queries, keys_values)


def weigh_kernel(
    root, ks, seg, place_ref, gain_ref, rate_ref, own_ref, other_ref, expo_ref, v_ref, peak_ref,
    *refs,
):
    out_refs, (p_ref, ranks_ref, right_ref) = refs[-3 - len(ks) : -3], refs[-3:]
    cols = own_ref.shape[1]
    keys = 2 * cols
    chip = lax.div(place_ref[1], CORES)
    first_head = lax.rem(place_ref[1], CORES) * 2 * PAIRS
    starts = [pl.multiple_of(lax.bitwise_xor(chip, k) * seg, seg) for k in ks]

    for i in range(len(ks)):
        at = slice(i * seg, (i + 1) * seg)
        ranks_ref[at, :cols] = own_ref[at, :].astype(F32)
        ranks_ref[at, cols:] = other_ref[at, :].astype(F32)
    lane = lax.broadcasted_iota(jnp.int32, (keys, LANES), 1)
    zero = jnp.zeros((keys, LANES), BF16)
    right_ref[:keys, LANES:] = jnp.where(lane < HDIM, 1.0, 0.0).astype(BF16)
    right_ref[keys:, LANES:] = jnp.where(lane < HDIM, 0.0, 1.0).astype(BF16)
    out_lane = lax.broadcasted_iota(jnp.int32, (seg, LANES), 1)

    def pair(p, totals):
        lanes = pl.ds(pl.multiple_of(p * LANES, LANES), LANES)
        values = v_ref[:, lanes]
        right_ref[:keys, :LANES] = jnp.where(lane < HDIM, values, zero)
        right_ref[keys:, :LANES] = jnp.where(lane < HDIM, zero, values)
        for i in range(len(ks)):
            rows_at = slice(i * seg, (i + 1) * seg)
            for half in range(2):
                ranks = ranks_ref[rows_at, half * cols : (half + 1) * cols]
                for side in range(2):
                    rate = rate_ref[first_head + 2 * p + side] * root
                    gain = gain_ref[first_head + 2 * p + side] * math.log2(math.e)
                    at = slice(side * keys + half * cols, side * keys + (half + 1) * cols)
                    weight = expo_ref[p, pl.ds(starts[i], seg), at].astype(F32) * jnp.exp2(
                        gain * jnp.tanh(rate * ranks)
                    )
                    p_ref[rows_at, at] = weight.astype(BF16)
        sums = jnp.dot(p_ref[...], right_ref[...], preferred_element_type=F32)
        now = []
        for i, out_ref in enumerate(out_refs):
            part = sums[i * seg : (i + 1) * seg, :]
            out_ref[:seg, lanes] = part[:, :LANES].astype(BF16)
            now.append(jnp.where(out_lane % HDIM == p, part[:, LANES:], totals[i]))
        return tuple(now)

    totals = lax.fori_loop(
        0, PAIRS, pair, tuple(jnp.zeros((seg, LANES), F32) for _ in ks)
    )
    half = WIDTH // 2
    for i, out_ref in enumerate(out_refs):
        extra = totals[i]
        rest = peak_ref[pl.ds(starts[i], seg), :]
        for n in range(1, 4):
            piece = rest.astype(BF16).astype(F32)
            rest = rest - piece
            here = (out_lane % HDIM >= n * PAIRS) & (out_lane % HDIM < (n + 1) * PAIRS)
            extra = jnp.where(here, pltpu.roll(piece, n * PAIRS, 1), extra)
        extra = jnp.concatenate([extra, jnp.zeros((half - seg, LANES), F32)], axis=0).T
        for side in range(2):
            out_ref[seg:, side * half : (side + 1) * half] = extra[
                side * HDIM : side * HDIM + EXTRA
            ].astype(BF16)


def weigh(root, chips, ks, first, place, gain, rate, own, other, expo, values, peak, follows):
    (_, rows, _), cols = expo.shape, own.shape[1]
    seg = rows // chips
    n_rows, keys = seg * len(ks), 2 * cols
    part = pl.BlockSpec((n_rows, cols), lambda i: (first // len(ks), 0))
    work = n_rows * keys * 2 * PAIRS
    return pl.pallas_call(
        functools.partial(weigh_kernel, root, ks, seg),
        out_shape=(jax.ShapeDtypeStruct((seg + EXTRA, WIDTH), BF16),) * len(ks),
        grid=(1,),
        in_specs=[
            SMEM,
            SMEM,
            SMEM,
            part,
            part,
            VMEM,
            pl.BlockSpec((keys, WIDTH), lambda i: (0, 1)),
            pl.BlockSpec((rows, LANES), lambda i: (0, 0)),
            *[HBM] * len(follows),
        ],
        out_specs=(pl.BlockSpec((seg + EXTRA, WIDTH), lambda i: (0, 0)),) * len(ks),
        scratch_shapes=[
            pltpu.VMEM((n_rows, 2 * keys), BF16),
            pltpu.VMEM((n_rows, keys), F32),
            pltpu.VMEM((2 * keys, 2 * LANES), BF16),
        ],
        compiler_params=params(28 * 2**20),
        cost_estimate=cost(512 * work, 2 * work, 2 * work),
        name="weigh",
    )(place, gain, rate, own, other, expo, values, peak, *follows)


def divide_kernel(*refs):
    parts, out_ref = refs[:-1], refs[-1]
    seg, half = out_ref.shape[0], WIDTH // 2
    lane = lax.broadcasted_iota(jnp.int32, (seg, LANES), 1)
    fit = LANES // (2 * EXTRA)
    totals, peaks, largest = [], [], None
    for first in range(0, len(parts), fit):
        group = parts[first : first + fit]
        extra = [
            part[seg:, side * half : (side + 1) * half].astype(F32)
            for part in group
            for side in range(2)
        ]
        spare = LANES - EXTRA * len(extra)
        if spare:
            extra.append(jnp.zeros((spare, half), F32))
        extra = jnp.concatenate(extra, axis=0).T[:seg]
        totals.append(extra)
        peak = sum(pltpu.roll(extra, LANES - n * PAIRS, 1) for n in range(1, 4))
        if spare:
            peak = jnp.where(lane < LANES - spare, peak, -jnp.inf)
        peaks.append(peak)
        largest = peak if largest is None else jnp.maximum(largest, peak)

    def over_parts(value, combine):
        step = 2 * EXTRA
        while step < LANES:
            value = combine(value, pltpu.roll(value, step, 1))
            step *= 2
        return value

    largest = over_parts(largest, jnp.maximum)
    weights = [jnp.exp(peak - largest) for peak in peaks]
    inverse = 1.0 / over_parts(
        sum(w * x for w, x in zip(weights, totals, strict=True)), lambda x, y: x + y
    )
    scales = [w * inverse for w in weights]
    for p in range(PAIRS):
        lanes = slice(p * LANES, (p + 1) * LANES)
        total = jnp.zeros((seg, LANES), F32)
        for i, part in enumerate(parts):
            at = i % fit * 2 * EXTRA + p
            scale = scales[i // fit]
            both = jnp.where(
                lane < HDIM, scale[:, at : at + 1], scale[:, at + EXTRA : at + EXTRA + 1]
            )
            total += part[:seg, lanes].astype(F32) * both
        out_ref[:, lanes] = total.astype(BF16)


def divide(parts):
    seg = parts[0].shape[0] - EXTRA
    return pl.pallas_call(
        divide_kernel,
        out_shape=jax.ShapeDtypeStruct((seg, WIDTH), BF16),
        in_specs=[VMEM] * len(parts),
        out_specs=VMEM,
        compiler_params=params(SMALL_LIMIT),
        cost_estimate=cost(8 * seg * D, 8 * seg * D),
        name="divide",
    )(*parts)


def project_out_kernel(place_ref, own_ref, other_ref, *refs):
    n = len(refs) // 2
    core = lax.rem(place_ref[1], CORES)
    mine = pl.ds(pl.multiple_of(core * WIDTH, WIDTH), WIDTH)
    others = pl.ds(pl.multiple_of((1 - core) * WIDTH, WIDTH), WIDTH)
    for w_ref, out_ref in zip(refs[:n], refs[n:], strict=True):
        total = jnp.dot(own_ref[...], w_ref[mine, :], preferred_element_type=F32)
        total += jnp.dot(other_ref[...], w_ref[others, :], preferred_element_type=F32)
        out_ref[...] = total.astype(BF16)


def project_out(place, own, other, w_all):
    seg, (depth, width) = own.shape[0], w_all[0].shape
    chips = len(w_all)
    return pl.pallas_call(
        project_out_kernel,
        out_shape=(jax.ShapeDtypeStruct((seg, width), BF16),) * chips,
        in_specs=[SMEM] + [VMEM] * (2 + chips),
        out_specs=(VMEM,) * chips,
        compiler_params=params(SMALL_LIMIT),
        cost_estimate=cost(2 * seg * depth * width * chips, 2 * depth * width * chips),
        name="project_out",
    )(place, own, other, *w_all)


def shards(node_features, edge_weight, pattern, w_qkv, w_out, bias_gain, bias_rate):
    rows, cols = edge_weight.shape
    row_count, col_count = lax.axis_size("row"), lax.axis_size("col")
    row_pos, col_pos = lax.axis_index("row"), lax.axis_index("col")
    ratio = rows // cols
    chips = col_count // CORES
    chip = col_pos // CORES
    root = math.sqrt(rows * row_count)
    place = jnp.stack([row_pos, col_pos]).astype(jnp.int32)
    core = (col_pos % CORES).astype(jnp.int32).reshape(1)
    pattern = pattern.T
    together = lax.optimization_barrier

    def along_col(value, j):
        return lax.ppermute(value, "col", xor_pairs(col_count, j))

    def along_row(value, j):
        return lax.ppermute(value, "row", xor_pairs(row_count, j))

    def from_rows(value):
        return [value] + [along_row(value, j) for j in range(1, row_count)]

    def spread(blocks, bits):
        new = dict(blocks)
        for k in range(chips - 1, 0, -1):
            if k.bit_count() == bits:
                low = k & -k
                new[k] = along_col(blocks[k ^ low], CORES * low)
        return new

    ring = [0, 1, 3, 2] if row_count == 4 else list(range(row_count))
    def place_of(r):
        return r ^ (r >> 1) if row_count == 4 else r

    steps_away = (
        (place_of(row_pos) - place_of(col_pos // ratio)) * (1 - 2 * (col_pos % CORES))
    ) % row_count

    def feature_step(value, s):
        pairs = []
        for c in range(col_count):
            way = 1 - 2 * (c % CORES)
            i = ring.index(c // ratio) + way * (s - 1)
            here, there = ring[i % row_count], ring[(i + way) % row_count]
            pairs.append((here * col_count + c, there * col_count + c))
        return lax.ppermute(value, ("row", "col"), pairs)

    adjacency, features = start(pattern, edge_weight, node_features)
    blocks = spread({0: adjacency}, 1)
    near = [1, 2] if row_count == 4 else list(range(1, row_count))
    columns = {j: along_row(adjacency, j) for j in near}
    other_pattern = along_col(pattern, 1)
    queries = project_in(core, [node_features], w_qkv, [0], 1.0 / math.sqrt(HDIM))
    moved = [features, feature_step(features, 1)]
    raw_columns = columns
    queries, moved, columns, blocks = together((queries, moved, columns, blocks))

    order = sorted(blocks)
    swapped = along_col(jnp.stack([blocks[k] for k in order]), 1)
    far = []
    if row_count == 4:
        half = rows // 2
        far = [along_row(columns[2][:half], 1), along_row(columns[1][half:], 2)]
    moved.append(feature_step(moved[-1], 2))
    for bits in range(2, chips.bit_length()):
        blocks = spread(blocks, bits)
    raw_far = far
    far, swapped, blocks = together((far, swapped, blocks))
    for s in range(3, row_count):
        moved.append(feature_step(moved[-1], s))
    panel = [(x, CORES * k, None) for k, x in blocks.items()]
    panel += [(swapped, CORES * k + 1, i) for i, k in enumerate(order)]
    panel += [(along_col(x, 1), CORES * k + 1, None) for k, x in blocks.items() if k not in order]
    columns = [(0, 0, adjacency)] + [(j, 0, x) for j, x in raw_columns.items()]
    columns += [(3, i * x.shape[0], x) for i, x in enumerate(raw_far)]
    key_rows = features
    for s in range(1, row_count - 1):
        key_rows = jnp.where(steps_away == s, moved[s], key_rows)
    ranks = sweep(True, range(chips), place, pattern, panel, columns, [key_rows], 50 * 2**20)
    columns = [(j, 0, x) for j, x in enumerate(from_rows(ranks))]

    ranks, last = together((ranks, moved[-1]))
    key_rows = jnp.where(steps_away == row_count - 1, last, key_rows)
    keys_values = project_in(core, [key_rows, along_col(key_rows, 1)], w_qkv, [D, 2 * D], limit=28 * 2**20)
    keys_values, w_out = together((keys_values, w_out))
    w_all = spread({0: w_out}, 1)
    expo, peak = exponentials(pattern, other_pattern, queries, keys_values)
    w_all, peak = together((w_all, peak))
    for bits in range(2, chips.bit_length()):
        w_all = spread(w_all, bits)
    w_all = [w_all[k] for k in range(chips)]

    groups = [list(range(chips // 2, chips)), list(range(chips // 2))]
    ranks = [
        sweep(False, ks, place, pattern, panel, columns, follow, 24 * 2**20)
        for ks, follow in zip(groups, [[peak], [peak, *w_all[1:]]], strict=True)
    ]
    others = [along_col(x, 1) for x in ranks]
    parts, follows = [None] * chips, [ranks[1]]
    cuts = [(0, n, n + 1) for n in reversed(range(len(groups[0])))] + [(1, 0, len(groups[1]))]
    for g, begin, end in cuts:
        ks = groups[g][begin:end]
        sums = weigh(
            root, chips, ks, begin, place, bias_gain, bias_rate, ranks[g], others[g], expo,
            keys_values, peak, follows,
        )
        for k, part in zip(ks, sums, strict=False):
            parts[k] = part if k == 0 else along_col(part, CORES * k)
        follows = [sums[0]]
    attended = divide(parts)
    mixed = project_out(place, attended, along_col(attended, 1), w_all)
    mixed = [x if k == 0 else along_col(x, CORES * k) for k, x in enumerate(mixed)]
    for bit in range(chips.bit_length() - 1):
        turned = chip >> bit & 1 == 1
        mixed = [jnp.where(turned, mixed[k ^ 1 << bit], mixed[k]) for k in range(chips)]
    return jnp.concatenate(mixed, axis=0)


def solution(mesh):
    in_specs = (P("row", None), P("row", "col"), P("row", "col"), P(), P(None, "col"), P(), P())
    out_specs = P("row", "col")
    return jax.shard_map(shards, mesh=mesh, in_specs=in_specs, out_specs=out_specs, check_vma=False)
```

```python
import functools
import math

import jax
import jax.numpy as jnp
from jax import lax
from jax.experimental import pallas as pl
from jax.experimental.pallas import tpu as pltpu
from jax.sharding import PartitionSpec as P

D = 1024
HEADS = 16
BLK = 128
HDIM = 64
CORES = 2
PAIRS = HEADS // 2 // CORES
WIDTH = D // CORES
EXTRA = 4 * PAIRS
LANES = 128
VMEM_LIMIT = 58 * 2**20
SMALL_LIMIT = 16 * 2**20

VMEM = pl.BlockSpec(memory_space=pltpu.VMEM)
SMEM = pl.BlockSpec(memory_space=pltpu.SMEM)
HBM = pl.BlockSpec(memory_space=pltpu.HBM)
BF16 = jnp.bfloat16
F32 = jnp.float32


def params(limit=VMEM_LIMIT):
    return pltpu.CompilerParams(vmem_limit_bytes=limit)


def cost(flops, nbytes, trans=0):
    return pl.CostEstimate(flops=int(flops), bytes_accessed=int(nbytes), transcendentals=int(trans))


def xor_pairs(n, j):
    return [(i, i ^ j) for i in range(n)]


def keep_tile(pattern_ref, first_row, block_rows):
    block_cols = pattern_ref.shape[0]
    tiles = []
    for i in range(block_rows):
        parts = [
            jnp.full((1, BLK), jnp.where(pattern_ref[b, first_row + i] > 0, 1.0, 0.0), F32)
            for b in range(block_cols)
        ]
        tiles.append(
            jnp.broadcast_to(jnp.concatenate(parts, axis=1), (BLK, block_cols * BLK))
        )
    return jnp.concatenate(tiles, axis=0)


def start_kernel(pattern_ref, weight_ref, features_ref, out_ref, cut_ref, kept_ref, held_ref, sem):
    cols = cut_ref.shape[0]
    rows = out_ref.shape[0] // 2
    ratio = features_ref.shape[0] // cols
    at = pl.multiple_of(lax.rem(lax.axis_index("col"), ratio) * cols, cols)
    halves = [slice(h * rows, (h + 1) * rows) for h in range(2)]
    come = [
        pltpu.make_async_copy(weight_ref.at[x, :], kept_ref.at[x, :], sem.at[h])
        for h, x in enumerate(halves)
    ]
    go = [
        pltpu.make_async_copy(kept_ref.at[x, :], out_ref.at[x, :], sem.at[2 + h])
        for h, x in enumerate(halves)
    ]
    cut_in = pltpu.make_async_copy(features_ref.at[pl.ds(at, cols), :], held_ref, sem.at[4])
    cut_out = pltpu.make_async_copy(held_ref, cut_ref, sem.at[5])
    for copy in (*come, cut_in):
        copy.start()
    for h in range(2):
        come[h].wait()
        for i in range(h * rows // BLK, (h + 1) * rows // BLK):
            x = slice(i * BLK, (i + 1) * BLK)
            keep = keep_tile(pattern_ref, i, 1)
            kept_ref[x, :] = jnp.where(keep > 0, kept_ref[x, :].astype(F32), 0.0).astype(BF16)
        go[h].start()
        if h == 0:
            cut_in.wait()
            cut_out.start()
    for copy in (*go, cut_out):
        copy.wait()


def start(pattern, weight, features):
    rows, cols = weight.shape
    depth = features.shape[1]
    return pl.pallas_call(
        start_kernel,
        out_shape=(
            jax.ShapeDtypeStruct((rows, cols), BF16),
            jax.ShapeDtypeStruct((cols, depth), BF16),
        ),
        in_specs=[SMEM, HBM, HBM],
        out_specs=(HBM, HBM),
        scratch_shapes=[
            pltpu.VMEM((rows, cols), BF16),
            pltpu.VMEM((cols, depth), BF16),
            pltpu.SemaphoreType.DMA((6,)),
        ],
        compiler_params=params(),
        cost_estimate=cost(rows * cols, 4 * rows * cols),
        name="start",
    )(pattern, weight, features)


def choose_kernel(which_ref, *refs):
    values, (out_ref, held_ref, sem) = refs[:-3], refs[-3:]
    which = jnp.where(which_ref[0] < len(values), which_ref[0], 0)
    for i, value in enumerate(values):

        @pl.when(which == i)
        def _():
            copy = pltpu.make_async_copy(value, held_ref, sem)
            copy.start()
            copy.wait()

    copy = pltpu.make_async_copy(held_ref, out_ref, sem)
    copy.start()
    copy.wait()


def choose(which, values):
    one = jax.ShapeDtypeStruct(values[0].shape, values[0].dtype)
    return pl.pallas_call(
        choose_kernel,
        out_shape=one,
        in_specs=[SMEM] + [HBM] * len(values),
        out_specs=HBM,
        scratch_shapes=[pltpu.VMEM(one.shape, one.dtype), pltpu.SemaphoreType.DMA],
        compiler_params=params(),
        cost_estimate=cost(0, 4 * values[0].size),
        name="choose",
    )(which.astype(jnp.int32).reshape(1), *values)


def project_in_kernel(scale, place_ref, *refs):
    xs, (w_ref, out_ref) = refs[:-2], refs[-2:]
    rows = xs[0].shape[0]
    for i, x_ref in enumerate(xs):
        out = jnp.dot(x_ref[...], w_ref[...], preferred_element_type=F32).astype(BF16)
        if scale is not None:
            out = out * jnp.asarray(scale, BF16)
        out_ref[i * rows : (i + 1) * rows, :] = out


def project_in(core, xs, w, firsts, scale=None, tile=256, limit=VMEM_LIMIT):
    rows, depth = xs[0].shape
    steps = WIDTH // tile

    def column(i, core_ref):
        first = firsts[0] // tile
        for n, start in enumerate(firsts[1:], 1):
            first = jnp.where(i >= n * steps, start // tile, first)
        return 0, first + core_ref[0] * steps + lax.rem(i, steps)

    return pl.pallas_call(
        functools.partial(project_in_kernel, scale),
        out_shape=jax.ShapeDtypeStruct((rows * len(xs), WIDTH * len(firsts)), BF16),
        grid_spec=pltpu.PrefetchScalarGridSpec(
            num_scalar_prefetch=1,
            grid=(steps * len(firsts),),
            in_specs=[pl.BlockSpec((rows, depth), lambda i, c: (0, 0))] * len(xs)
            + [pl.BlockSpec((depth, tile), column)],
            out_specs=pl.BlockSpec((rows * len(xs), tile), lambda i, c: (0, i)),
        ),
        compiler_params=params(limit),
        cost_estimate=cost(
            2 * rows * len(xs) * depth * WIDTH * len(firsts),
            2 * depth * (rows * len(xs) + WIDTH * len(firsts)),
        ),
        name="project_in",
    )(core, *xs, w)


def sweep_kernel(first, ks, chips, left_at, right_at, place_ref, pattern_ref, *refs):
    n_right = len(right_at)
    panel, rights = refs[: len(left_at)], refs[len(left_at) : len(left_at) + n_right]
    out_ref, left_ref, right_ref, acc_ref, left_sem, right_sem = refs[-6:]
    rows, cols = panel[0].shape[-2:]
    seg = rows // chips
    row_pos, col_pos = place_ref[0], place_ref[1]
    chip, core = lax.div(col_pos, CORES), lax.rem(col_pos, CORES)
    starts = [pl.multiple_of(lax.bitwise_xor(chip, k) * seg, seg) for k in ks]
    if len(ks) == chips:
        starts, seg = [0], rows

    part = min(ref.shape[0] for ref in rights)

    def right_copies(i, slot):
        xor, offset = right_at[i]
        for at in range(0, rights[i].shape[0], part):
            target = right_ref.at[slot, pl.ds(offset + at, part), :]
            source = rights[i].at[pl.ds(at, part), :]
            yield pltpu.make_async_copy(source, target, right_sem.at[slot, (offset + at) // part])

    def left_copies(k):
        for ref, (j, index) in zip(panel, left_at, strict=True):
            if j // CORES != k:
                continue
            block = ref if index is None else ref.at[index]
            at = pl.multiple_of(lax.bitwise_xor(core, j % CORES) * cols, cols)
            for n, start in enumerate(starts):
                yield pltpu.make_async_copy(
                    block.at[pl.ds(start, seg), :],
                    left_ref.at[k, pl.ds(n * seg, seg), pl.ds(at, cols)],
                    left_sem.at[k, j % CORES * len(starts) + n],
                )

    for k in range(chips):
        for copy in left_copies(k):
            copy.start()
        for xor in sorted({at[0] for at in right_at}):

            @pl.when(lax.bitwise_xor(row_pos, chip) == xor ^ k)
            def _():
                for i in range(n_right):
                    if right_at[i][0] == xor:
                        for copy in right_copies(i, k):
                            copy.start()

    for k in range(chips):
        for at in range(0, rows, part):
            half = right_ref.at[k, pl.ds(at, part), :]
            pltpu.make_async_copy(half, half, right_sem.at[k, at // part]).wait()
        for copy in left_copies(k):
            copy.wait()
        product = jnp.dot(left_ref[k], right_ref[k], preferred_element_type=F32)
        if k == 0:
            acc_ref[...] = product
        elif k < chips - 1:
            acc_ref[...] += product
    product = product + acc_ref[...]
    own = left_ref[0, :, pl.ds(pl.multiple_of(core * cols, cols), cols)].astype(F32)
    total = 0.1275 * own + (0.85 * 0.1275 if first else 0.85) * product
    diagonal = lax.broadcasted_iota(jnp.int32, (seg, cols), 1) - lax.broadcasted_iota(
        jnp.int32, (seg, cols), 0
    )
    lane_block = lax.broadcasted_iota(jnp.int32, (1, cols), 1) // BLK
    for n, start in enumerate(starts):
        at = slice(n * seg, (n + 1) * seg)
        part = total[at, :]
        if not first:
            here = diagonal == row_pos * rows + start - col_pos * cols
            part = jnp.where(here, part + 0.15, part)
        size = math.gcd(seg, BLK)
        for i in range(seg // size):
            keep = jnp.zeros((1, cols), F32)
            for b in range(cols // BLK):
                kept = pattern_ref[b, lax.div(start + i * size, BLK)] > 0
                keep = jnp.where(lane_block == b, jnp.where(kept, 1.0, 0.0), keep)
            piece = part[i * size : (i + 1) * size, :]
            out_ref[n * seg + i * size : n * seg + (i + 1) * size, :] = jnp.where(
                keep > 0, piece, 0.0
            ).astype(BF16)


def sweep(first, ks, place, pattern, panel, blocks, follows, limit=VMEM_LIMIT):
    rows, cols = panel[0][0].shape[-2:]
    chips = len(panel) // CORES
    n_rows = rows // chips * len(ks)
    depth = len(panel) * cols
    return pl.pallas_call(
        functools.partial(
            sweep_kernel,
            first,
            ks,
            chips,
            [at for _, *at in panel],
            [(j, at) for j, at, _ in blocks],
        ),
        out_shape=jax.ShapeDtypeStruct((n_rows, cols), BF16),
        in_specs=[SMEM, SMEM] + [HBM] * (len(panel) + len(blocks) + len(follows)),
        out_specs=VMEM,
        scratch_shapes=[
            pltpu.VMEM((chips, n_rows, CORES * cols), BF16),
            pltpu.VMEM((depth // rows, rows, cols), BF16),
            pltpu.VMEM((n_rows, cols), F32),
            pltpu.SemaphoreType.DMA((chips, CORES * len(ks))),
            pltpu.SemaphoreType.DMA((chips, rows // min(x.shape[0] for *_, x in blocks))),
        ],
        compiler_params=params(limit),
        cost_estimate=cost(2 * n_rows * depth * cols, 2 * (n_rows + rows) * depth),
        name="rank_sweep",
    )(place, pattern, *[x for x, *_ in panel], *[x for *_, x in blocks], *follows)


def split_heads(keys):
    lane = lax.broadcasted_iota(jnp.int32, keys.shape, 1)
    zero = jnp.zeros_like(keys)
    return jnp.concatenate(
        [jnp.where(lane < HDIM, keys, zero), jnp.where(lane >= HDIM, keys, zero)], axis=0
    )


def expo_kernel(own_ref, other_ref, q_ref, k_ref, out_ref, peak_ref, mask_ref):
    p = pl.program_id(0)
    rows, keys = q_ref.shape[0], k_ref.shape[0]
    block_rows, block_cols = rows // BLK, keys // BLK
    tile = BLK

    @pl.when(p == 0)
    def _():
        lane = lax.broadcasted_iota(jnp.int32, (BLK, LANES), 1)
        for i in range(block_rows):
            excluded = jnp.zeros((BLK, LANES), F32)
            for b in range(block_cols):
                ref, at = (own_ref, b) if b < block_cols // 2 else (other_ref, b - block_cols // 2)
                excluded = jnp.where(lane == b, jnp.where(ref[at, i] > 0, 0.0, -1e30), excluded)
            mask_ref[i * BLK : (i + 1) * BLK, :] = excluded.astype(BF16)
        peak_ref[...] = jnp.zeros_like(peak_ref)

    lane = lax.broadcasted_iota(jnp.int32, (2 * keys, LANES), 1)
    key = lax.broadcasted_iota(jnp.int32, (2 * keys, LANES), 0)
    block_of = jnp.where(key >= keys, key - keys, key) // BLK
    in_block = jnp.where(lane == block_of, 1.0, 0.0).astype(BF16)
    right = jnp.concatenate([split_heads(k_ref[...]), in_block], axis=1)
    peak_lane = lax.broadcasted_iota(jnp.int32, (tile, LANES), 1)
    for t in range(rows // tile):
        at = slice(t * tile, (t + 1) * tile)
        left = jnp.concatenate([q_ref[at, :], mask_ref[at, :]], axis=1)
        s = lax.dot_general(left, right, (((1,), (1,)), ((), ())), preferred_element_type=F32)
        peaks = peak_ref[at, :]
        for side in range(2):
            part = s[:, side * keys : (side + 1) * keys]
            peak = jnp.max(part, axis=1, keepdims=True)
            peaks = jnp.where(peak_lane == HDIM * side + p, peak, peaks)
            out_ref[0, at, side * keys : (side + 1) * keys] = jnp.exp(part - peak).astype(BF16)
        peak_ref[at, :] = peaks


def exponentials(own, other, queries, keys_values):
    rows, keys = queries.shape[0], keys_values.shape[0]
    work = rows * keys * 2 * PAIRS
    return pl.pallas_call(
        expo_kernel,
        out_shape=(
            jax.ShapeDtypeStruct((PAIRS, rows, 2 * keys), BF16),
            jax.ShapeDtypeStruct((rows, LANES), F32),
        ),
        grid=(PAIRS,),
        in_specs=[
            SMEM,
            SMEM,
            pl.BlockSpec((rows, LANES), lambda p: (0, p)),
            pl.BlockSpec((keys, LANES), lambda p: (0, p)),
        ],
        out_specs=(
            pl.BlockSpec((1, rows, 2 * keys), lambda p: (p, 0, 0)),
            pl.BlockSpec((rows, LANES), lambda p: (0, 0)),
        ),
        scratch_shapes=[pltpu.VMEM((rows, LANES), BF16)],
        compiler_params=params(28 * 2**20),
        cost_estimate=cost(512 * work, 2 * work, work),
        name="expo",
    )(own, other, queries, keys_values)


def weigh_kernel(
    root, ks, seg, place_ref, gain_ref, rate_ref, own_ref, other_ref, expo_ref, v_ref, peak_ref,
    *refs,
):
    out_refs, (p_ref, ranks_ref, right_ref) = refs[-3 - len(ks) : -3], refs[-3:]
    cols = own_ref.shape[1]
    keys = 2 * cols
    chip = lax.div(place_ref[1], CORES)
    first_head = lax.rem(place_ref[1], CORES) * 2 * PAIRS
    starts = [pl.multiple_of(lax.bitwise_xor(chip, k) * seg, seg) for k in ks]

    for i in range(len(ks)):
        at = slice(i * seg, (i + 1) * seg)
        ranks_ref[at, :cols] = own_ref[at, :].astype(F32)
        ranks_ref[at, cols:] = other_ref[at, :].astype(F32)
    lane = lax.broadcasted_iota(jnp.int32, (keys, LANES), 1)
    zero = jnp.zeros((keys, LANES), BF16)
    right_ref[:keys, LANES:] = jnp.where(lane < HDIM, 1.0, 0.0).astype(BF16)
    right_ref[keys:, LANES:] = jnp.where(lane < HDIM, 0.0, 1.0).astype(BF16)
    out_lane = lax.broadcasted_iota(jnp.int32, (seg, LANES), 1)

    def pair(p, totals):
        lanes = pl.ds(pl.multiple_of(p * LANES, LANES), LANES)
        values = v_ref[:, lanes]
        right_ref[:keys, :LANES] = jnp.where(lane < HDIM, values, zero)
        right_ref[keys:, :LANES] = jnp.where(lane < HDIM, zero, values)
        for i in range(len(ks)):
            rows_at = slice(i * seg, (i + 1) * seg)
            for half in range(2):
                ranks = ranks_ref[rows_at, half * cols : (half + 1) * cols]
                for side in range(2):
                    rate = rate_ref[first_head + 2 * p + side] * root
                    gain = gain_ref[first_head + 2 * p + side] * math.log2(math.e)
                    at = slice(side * keys + half * cols, side * keys + (half + 1) * cols)
                    weight = expo_ref[p, pl.ds(starts[i], seg), at].astype(F32) * jnp.exp2(
                        gain * jnp.tanh(rate * ranks)
                    )
                    p_ref[rows_at, at] = weight.astype(BF16)
        sums = jnp.dot(p_ref[...], right_ref[...], preferred_element_type=F32)
        now = []
        for i, out_ref in enumerate(out_refs):
            part = sums[i * seg : (i + 1) * seg, :]
            out_ref[:seg, lanes] = part[:, :LANES].astype(BF16)
            now.append(jnp.where(out_lane % HDIM == p, part[:, LANES:], totals[i]))
        return tuple(now)

    totals = lax.fori_loop(
        0, PAIRS, pair, tuple(jnp.zeros((seg, LANES), F32) for _ in ks)
    )
    half = WIDTH // 2
    for i, out_ref in enumerate(out_refs):
        extra = totals[i]
        rest = peak_ref[pl.ds(starts[i], seg), :]
        for n in range(1, 4):
            piece = rest.astype(BF16).astype(F32)
            rest = rest - piece
            here = (out_lane % HDIM >= n * PAIRS) & (out_lane % HDIM < (n + 1) * PAIRS)
            extra = jnp.where(here, pltpu.roll(piece, n * PAIRS, 1), extra)
        extra = jnp.concatenate([extra, jnp.zeros((half - seg, LANES), F32)], axis=0).T
        for side in range(2):
            out_ref[seg:, side * half : (side + 1) * half] = extra[
                side * HDIM : side * HDIM + EXTRA
            ].astype(BF16)


def weigh(root, chips, ks, first, place, gain, rate, own, other, expo, values, peak, follows):
    (_, rows, _), cols = expo.shape, own.shape[1]
    seg = rows // chips
    n_rows, keys = seg * len(ks), 2 * cols
    part = pl.BlockSpec((n_rows, cols), lambda i: (first // len(ks), 0))
    work = n_rows * keys * 2 * PAIRS
    return pl.pallas_call(
        functools.partial(weigh_kernel, root, ks, seg),
        out_shape=(jax.ShapeDtypeStruct((seg + EXTRA, WIDTH), BF16),) * len(ks),
        grid=(1,),
        in_specs=[
            SMEM,
            SMEM,
            SMEM,
            part,
            part,
            VMEM,
            pl.BlockSpec((keys, WIDTH), lambda i: (0, 1)),
            pl.BlockSpec((rows, LANES), lambda i: (0, 0)),
            *[HBM] * len(follows),
        ],
        out_specs=(pl.BlockSpec((seg + EXTRA, WIDTH), lambda i: (0, 0)),) * len(ks),
        scratch_shapes=[
            pltpu.VMEM((n_rows, 2 * keys), BF16),
            pltpu.VMEM((n_rows, keys), F32),
            pltpu.VMEM((2 * keys, 2 * LANES), BF16),
        ],
        compiler_params=params(28 * 2**20),
        cost_estimate=cost(512 * work, 2 * work, 2 * work),
        name="weigh",
    )(place, gain, rate, own, other, expo, values, peak, *follows)


def divide_kernel(*refs):
    parts, out_ref = refs[:-1], refs[-1]
    seg, half = out_ref.shape[0], WIDTH // 2
    lane = lax.broadcasted_iota(jnp.int32, (seg, LANES), 1)
    fit = LANES // (2 * EXTRA)
    totals, peaks, largest = [], [], None
    for first in range(0, len(parts), fit):
        group = parts[first : first + fit]
        extra = [
            part[seg:, side * half : (side + 1) * half].astype(F32)
            for part in group
            for side in range(2)
        ]
        spare = LANES - EXTRA * len(extra)
        if spare:
            extra.append(jnp.zeros((spare, half), F32))
        extra = jnp.concatenate(extra, axis=0).T[:seg]
        totals.append(extra)
        peak = sum(pltpu.roll(extra, LANES - n * PAIRS, 1) for n in range(1, 4))
        if spare:
            peak = jnp.where(lane < LANES - spare, peak, -jnp.inf)
        peaks.append(peak)
        largest = peak if largest is None else jnp.maximum(largest, peak)

    def over_parts(value, combine):
        step = 2 * EXTRA
        while step < LANES:
            value = combine(value, pltpu.roll(value, step, 1))
            step *= 2
        return value

    largest = over_parts(largest, jnp.maximum)
    weights = [jnp.exp(peak - largest) for peak in peaks]
    inverse = 1.0 / over_parts(
        sum(w * x for w, x in zip(weights, totals, strict=True)), lambda x, y: x + y
    )
    scales = [w * inverse for w in weights]
    for p in range(PAIRS):
        lanes = slice(p * LANES, (p + 1) * LANES)
        total = jnp.zeros((seg, LANES), F32)
        for i, part in enumerate(parts):
            at = i % fit * 2 * EXTRA + p
            scale = scales[i // fit]
            both = jnp.where(
                lane < HDIM, scale[:, at : at + 1], scale[:, at + EXTRA : at + EXTRA + 1]
            )
            total += part[:seg, lanes].astype(F32) * both
        out_ref[:, lanes] = total.astype(BF16)


def divide(parts):
    seg = parts[0].shape[0] - EXTRA
    return pl.pallas_call(
        divide_kernel,
        out_shape=jax.ShapeDtypeStruct((seg, WIDTH), BF16),
        in_specs=[VMEM] * len(parts),
        out_specs=VMEM,
        compiler_params=params(SMALL_LIMIT),
        cost_estimate=cost(8 * seg * D, 8 * seg * D),
        name="divide",
    )(*parts)


def project_out_kernel(place_ref, own_ref, other_ref, *refs):
    n = len(refs) // 2
    core = lax.rem(place_ref[1], CORES)
    mine = pl.ds(pl.multiple_of(core * WIDTH, WIDTH), WIDTH)
    others = pl.ds(pl.multiple_of((1 - core) * WIDTH, WIDTH), WIDTH)
    for w_ref, out_ref in zip(refs[:n], refs[n:], strict=True):
        total = jnp.dot(own_ref[...], w_ref[mine, :], preferred_element_type=F32)
        total += jnp.dot(other_ref[...], w_ref[others, :], preferred_element_type=F32)
        out_ref[...] = total.astype(BF16)


def project_out(place, own, other, w_all):
    seg, (depth, width) = own.shape[0], w_all[0].shape
    chips = len(w_all)
    return pl.pallas_call(
        project_out_kernel,
        out_shape=(jax.ShapeDtypeStruct((seg, width), BF16),) * chips,
        in_specs=[SMEM] + [VMEM] * (2 + chips),
        out_specs=(VMEM,) * chips,
        compiler_params=params(SMALL_LIMIT),
        cost_estimate=cost(2 * seg * depth * width * chips, 2 * depth * width * chips),
        name="project_out",
    )(place, own, other, *w_all)


def shards(node_features, edge_weight, pattern, w_qkv, w_out, bias_gain, bias_rate):
    rows, cols = edge_weight.shape
    row_count, col_count = lax.axis_size("row"), lax.axis_size("col")
    row_pos, col_pos = lax.axis_index("row"), lax.axis_index("col")
    ratio = rows // cols
    chips = col_count // CORES
    chip = col_pos // CORES
    root = math.sqrt(rows * row_count)
    place = jnp.stack([row_pos, col_pos]).astype(jnp.int32)
    core = (col_pos % CORES).astype(jnp.int32).reshape(1)
    pattern = pattern.T
    together = lax.optimization_barrier

    def along_col(value, j):
        return lax.ppermute(value, "col", xor_pairs(col_count, j))

    def along_row(value, j):
        return lax.ppermute(value, "row", xor_pairs(row_count, j))

    def from_rows(value):
        return [value] + [along_row(value, j) for j in range(1, row_count)]

    def spread(blocks, bits):
        new = dict(blocks)
        for k in range(chips - 1, 0, -1):
            if k.bit_count() == bits:
                low = k & -k
                new[k] = along_col(blocks[k ^ low], CORES * low)
        return new

    ring = [0, 1, 3, 2] if row_count == 4 else list(range(row_count))
    def place_of(r):
        return r ^ (r >> 1) if row_count == 4 else r

    steps_away = (
        (place_of(row_pos) - place_of(col_pos // ratio)) * (1 - 2 * (col_pos % CORES))
    ) % row_count

    def feature_step(value, s):
        pairs = []
        for c in range(col_count):
            way = 1 - 2 * (c % CORES)
            i = ring.index(c // ratio) + way * (s - 1)
            here, there = ring[i % row_count], ring[(i + way) % row_count]
            pairs.append((here * col_count + c, there * col_count + c))
        return lax.ppermute(value, ("row", "col"), pairs)

    adjacency, features = start(pattern, edge_weight, node_features)
    blocks = spread({0: adjacency}, 1)
    near = [1, 2] if row_count == 4 else list(range(1, row_count))
    columns = {j: along_row(adjacency, j) for j in near}
    other_pattern = along_col(pattern, 1)
    queries = project_in(core, [node_features], w_qkv, [0], 1.0 / math.sqrt(HDIM))
    moved = [features, feature_step(features, 1)]
    raw_columns = columns
    queries, moved, columns, blocks = together((queries, moved, columns, blocks))

    order = sorted(blocks)
    swapped = along_col(jnp.stack([blocks[k] for k in order]), 1)
    far = []
    if row_count == 4:
        half = rows // 2
        far = [along_row(columns[2][:half], 1), along_row(columns[1][half:], 2)]
    moved.append(feature_step(moved[-1], 2))
    for bits in range(2, chips.bit_length()):
        blocks = spread(blocks, bits)
    raw_far = far
    far, swapped, blocks = together((far, swapped, blocks))
    for s in range(3, row_count):
        moved.append(feature_step(moved[-1], s))
    panel = [(x, CORES * k, None) for k, x in blocks.items()]
    panel += [(swapped, CORES * k + 1, i) for i, k in enumerate(order)]
    panel += [(along_col(x, 1), CORES * k + 1, None) for k, x in blocks.items() if k not in order]
    columns = [(0, 0, adjacency)] + [(j, 0, x) for j, x in raw_columns.items()]
    columns += [(3, i * x.shape[0], x) for i, x in enumerate(raw_far)]
    key_rows = choose(steps_away, moved[: row_count - 1])
    ranks = sweep(True, range(chips), place, pattern, panel, columns, [key_rows], 50 * 2**20)
    columns = [(j, 0, x) for j, x in enumerate(from_rows(ranks))]

    ranks, last = together((ranks, moved[-1]))
    key_rows = jnp.where(steps_away == row_count - 1, last, key_rows)
    keys_values = project_in(core, [key_rows, along_col(key_rows, 1)], w_qkv, [D, 2 * D], limit=28 * 2**20)
    keys_values, w_out = together((keys_values, w_out))
    w_all = spread({0: w_out}, 1)
    expo, peak = exponentials(pattern, other_pattern, queries, keys_values)
    w_all, peak = together((w_all, peak))
    for bits in range(2, chips.bit_length()):
        w_all = spread(w_all, bits)
    w_all = [w_all[k] for k in range(chips)]

    groups = [list(range(chips // 2, chips)), list(range(chips // 2))]
    ranks = [
        sweep(False, ks, place, pattern, panel, columns, follow, 24 * 2**20)
        for ks, follow in zip(groups, [[peak], [peak, *w_all[1:]]], strict=True)
    ]
    others = [along_col(x, 1) for x in ranks]
    parts, follows = [None] * chips, [ranks[1]]
    cuts = [(0, n, n + 1) for n in reversed(range(len(groups[0])))] + [(1, 0, len(groups[1]))]
    for g, begin, end in cuts:
        ks = groups[g][begin:end]
        sums = weigh(
            root, chips, ks, begin, place, bias_gain, bias_rate, ranks[g], others[g], expo,
            keys_values, peak, follows,
        )
        for k, part in zip(ks, sums, strict=False):
            parts[k] = part if k == 0 else along_col(part, CORES * k)
        follows = [sums[0]]
    attended = divide(parts)
    mixed = project_out(place, attended, along_col(attended, 1), w_all)
    mixed = [x if k == 0 else along_col(x, CORES * k) for k, x in enumerate(mixed)]
    for bit in range(chips.bit_length() - 1):
        turned = chip >> bit & 1 == 1
        mixed = [jnp.where(turned, mixed[k ^ 1 << bit], mixed[k]) for k in range(chips)]
    return jnp.concatenate(mixed, axis=0)


def solution(mesh):
    in_specs = (P("row", None), P("row", "col"), P("row", "col"), P(), P(None, "col"), P(), P())
    out_specs = P("row", "col")
    return jax.shard_map(shards, mesh=mesh, in_specs=in_specs, out_specs=out_specs, check_vma=False)
```
